32 devices in a mesh: groups: 2 (over y), expert: 4 (over z), dp: 4 (over x, core), rep: 1.
Axes of the slice: x: 2, y: 2, z: 4, core: 2. Of those that a mesh axis runs over, the one named last changes fastest.
Arguments:
- tokens: bfloat16 [4096, 1024], P(('groups', 'expert', 'dp')), parts along dimension 0, may hold values from -6 to 6
- routes: int32 [4096, 6], P(('groups', 'expert', 'dp')), parts along dimension 0, may hold values from 0 to 11, all different within a row; in each aligned block of 64 rows (0 to 63, 64 to 127, ...) at most 32 rows name the same one
- gate_weight: bfloat16 [8, 1024, 768], P('expert', ('dp', 'rep')), may hold values from -0.1875 to 0.1875
- up_weight: bfloat16 [8, 1024, 768], P('expert', ('dp', 'rep')), may hold values from -0.1875 to 0.1875
- down_weight: bfloat16 [8, 1024, 768], P('expert', ('dp', 'rep')), may hold values from -0.21875 to 0.21875
- router: bfloat16 [1024, 12], replicated, may hold values from -0.1875 to 0.1875
- const_vec: bfloat16 [2, 1024], replicated, may hold values from -6 to 6
- const_gate: bfloat16 [1024, 2], replicated, may hold values from -0.1875 to 0.1875
- grad_out: bfloat16 [4096, 1024], P(('groups', 'expert', 'dp')), parts along dimension 0, may hold values from -6 to 6
Outputs:
- mixed: bfloat16 [4096, 1024], P(('groups', 'expert', 'dp')), parts along dimension 0
- grad_tokens: bfloat16 [4096, 1024], P(('groups', 'expert', 'dp')), parts along dimension 0
- grad_gate: bfloat16 [16, 1024, 768], P(('groups', 'expert'), ('dp', 'rep')), parts along dimension 0
- grad_up: bfloat16 [16, 1024, 768], P(('groups', 'expert'), ('dp', 'rep')), parts along dimension 0
- grad_down: bfloat16 [16, 1024, 768], P(('groups', 'expert'), ('dp', 'rep')), parts along dimension 0
- grad_router: float32 [2048, 12], P('groups'), parts along dimension 0
- grad_const_vec: float32 [4, 1024], P('groups'), parts along dimension 0
- grad_const_gate: float32 [2048, 2], P('groups'), parts along dimension 0
The draws below stay inside these ranges and needn't reach their ends.
There are 2 independent parts, one for each index of `groups`. The reference program is written for one: setup_inputs(seed, part) draws one part's arguments, and reference() takes and returns one part's arrays. A program takes and returns all parts, laid end to end along the dimension named above; an argument that names none is the same for every part. Nothing has to cross between parts.
Inputs may be any that keep to these rules, and one draw needn't show every extreme that they name: `routes`: in each aligned block of 64 rows, no id is named by more than 32 rows. A row names 6 different ids.
All inputs are finite; a program needn't handle non-finite values.
Results may differ from the reference program's by a relative error of at most 0.012.
Values may be sent and summed in bfloat16 or wider, within the bound.
No kernel may reach another device: no remote copies, remote signals or barrier semaphores. Data moves between devices by JAX's collectives and lax.ppermute only.
A program may use at most 64 MiB of HBM per device.

```python
import math
import jax
import jax.numpy as jnp
import numpy as np
from jax import lax

D = 1024
H = 768
TOP = 6
NCONST = 2
EXPERTS = 8
NIDS = 12
BLOCK = 64
CAP = 32
TOKENS = 2048
N_REP = 1


def block_scale(rng, extent, shards, least, largest):
    level, own = 1.0, jax.random.fold_in(rng, 6)
    for axis_at, shards_of in shards:
        steps = jnp.exp(jax.random.uniform(jax.random.fold_in(own, axis_at), (shards_of,), jnp.float32, least / len(shards), largest / len(shards)))
        level = level * jnp.repeat(steps, extent[axis_at] // shards_of).reshape([-1 if axis == axis_at else 1 for axis in range(len(extent))])
    return level


def assign_block(own_key, own, number, rows, amount, top, most, slope):
    ranking = jax.random.permutation(own_key, amount)
    packed, common = load_shares(amount, rows * top, most, slope, True), load_shares(amount, rows * top, most, slope, False)
    places = jnp.arange(amount)

    def named(sizes, turn):
        used = int((sizes > 0).sum())
        fixed = max(1, used // 4)
        shifted = fixed + (places - fixed + turn * (used - fixed)) % max(1, amount - fixed)
        return jnp.zeros((amount,), jnp.int32).at[ranking[jnp.where(places < fixed, places, shifted)]].set(jnp.asarray(sizes, jnp.int32))

    sizes = jnp.where(number % 4 == 0, named(packed, number // 4), named(common, number - number // 4 - 1))
    mixed = jax.random.permutation(jax.random.fold_in(own, 3), amount)
    source_of, receiver = mixed[0:amount // 2 * 2:2], mixed[1:amount // 2 * 2:2]
    slack = jnp.minimum(sizes[source_of] - 1, most - sizes[receiver]) // 2
    slack = jnp.where((source_of == ranking[0]) | (receiver == ranking[0]) | (sizes[receiver] == 0), 0, jnp.maximum(slack, 0))
    shifted = jax.random.randint(jax.random.fold_in(own, 4), (amount // 2,), 0, 1 << 20) % (slack + 1)
    sizes = sizes.at[source_of].add(-shifted).at[receiver].add(shifted)
    members = jnp.searchsorted(jnp.cumsum(sizes), jnp.arange(rows * top), side="right").astype(jnp.int32)
    listing = members.reshape(top, rows).T
    listing = listing[jax.random.permutation(jax.random.fold_in(own, 1), rows)]
    turn = jax.random.randint(jax.random.fold_in(own, 2), (rows, 1), 0, top)
    return jnp.take_along_axis(listing, (jnp.arange(top)[None, :] + turn) % top, axis=1)


def load_shares(number_of, total, bound, slope, full):
    weights = [(1 << 20) // math.isqrt(rank ** slope) + 1 for rank in range(1, number_of + 1)]
    largest = bound if full else min(bound, max(-(-total // number_of), total * weights[0] // sum(weights)))
    least = 1 if total - largest >= number_of - 1 else 0
    counts, rest = [largest] + [least] * (number_of - 1), total - largest - least * (number_of - 1)
    while rest > 0:
        movable = [i for i in range(1, number_of) if counts[i] < largest] or [i for i in range(1, number_of) if counts[i] < bound]
        mass, left = sum([weights[i] for i in movable]), rest
        for i in movable:
            extra = min(bound - counts[i], max(1, left * weights[i] // mass), rest)
            counts[i] = counts[i] + extra
            rest = rest - extra
    return np.array(counts)


def centred(own_key, extent, width, limit, shards=(), kind=jnp.bfloat16):
    entries = jax.random.normal(own_key, extent, jnp.float32) * width
    if len(shards) > 0:
        entries = block_scale(own_key, extent, shards, -0.22, 0.18) * entries
    return jnp.clip(entries, min=-limit, max=limit).astype(kind)


def setup_inputs(seed: int = 0, part: int = 0) -> dict:
    keys = jax.random.split(jax.random.key(seed), 10)
    part_keys = jax.random.split(jax.random.fold_in(keys[9], part), 10)
    tokens = centred(part_keys[0], (TOKENS, D), 1.0, 6.0, ((0, 16),))
    routes_keys = jax.random.split(jax.random.fold_in(part_keys[1], 1), TOKENS // BLOCK)
    routes_turns = jax.random.permutation(jax.random.fold_in(part_keys[1], 3), TOKENS // BLOCK)
    routes = jax.vmap(lambda own, number: assign_block(jax.random.fold_in(part_keys[1], 2), own, number, BLOCK, NIDS, TOP, CAP, 2))(routes_keys, routes_turns).reshape((TOKENS, TOP))
    gate_weight = centred(keys[2], (EXPERTS, D, H), D ** -0.5, 0.1875, ((0, 4), (1, 4)))
    up_weight = centred(keys[3], (EXPERTS, D, H), D ** -0.5, 0.1875, ((0, 4), (1, 4)))
    down_weight = centred(keys[4], (EXPERTS, D, H), H ** -0.5, 0.21875, ((0, 4), (1, 4)))
    router = centred(keys[5], (D, NIDS), D ** -0.5, 0.1875)
    const_vec = centred(keys[6], (NCONST, D), 1.0, 6.0)
    const_gate = centred(keys[7], (D, NCONST), D ** -0.5, 0.1875)
    grad_out = centred(part_keys[8], (TOKENS, D), 1.0, 6.0, ((0, 16),))
    return {"tokens": tokens, "routes": routes, "gate_weight": gate_weight, "up_weight": up_weight, "down_weight": down_weight, "router": router, "const_vec": const_vec, "const_gate": const_gate, "grad_out": grad_out}


ROWS_CONTRACT = (((0,), (0,)), ((), ()))
LAST_CONTRACT = (((1,), (1,)), ((), ()))


def silu_slope(argument):
    logistic = jax.nn.sigmoid(argument)
    return logistic * (1.0 + argument * (1.0 - logistic))


def expert_forward(token_rows, w_gate, w_up, w_down):
    pre_gate = jnp.dot(token_rows, w_gate, preferred_element_type=jnp.float32)
    pre_up = jnp.dot(token_rows, w_up, preferred_element_type=jnp.float32)
    hidden = (jax.nn.silu(pre_gate) * pre_up).astype(jnp.bfloat16)
    output_rows = lax.dot_general(hidden, w_down, LAST_CONTRACT, preferred_element_type=jnp.float32)
    return output_rows.astype(jnp.bfloat16), hidden, pre_gate, pre_up


def expert_backward(pre_gate, pre_up, upstream, w_gate, w_up, w_down):
    d_hidden = jnp.dot(upstream, w_down, preferred_element_type=jnp.float32)
    d_gate = (d_hidden * pre_up * silu_slope(pre_gate)).astype(jnp.bfloat16)
    d_up = (d_hidden * jax.nn.silu(pre_gate)).astype(jnp.bfloat16)
    back_rows = lax.dot_general(d_gate, w_gate, LAST_CONTRACT, preferred_element_type=jnp.float32)
    back_rows = back_rows + lax.dot_general(d_up, w_up, LAST_CONTRACT, preferred_element_type=jnp.float32)
    return back_rows.astype(jnp.bfloat16), d_gate, d_up


def copy_total(partial_value):
    rounded = lax.optimization_barrier(partial_value.astype(jnp.bfloat16))
    return jnp.sum(rounded.astype(jnp.float32), axis=(0, 1)).astype(jnp.bfloat16)


def reference(tokens, routes, gate_weight, up_weight, down_weight, router, const_vec, const_gate, grad_out):
    token_count = tokens.shape[0]
    block_count = token_count // BLOCK
    buffer_rows = block_count * CAP
    group_count = block_count // (2 * N_REP)
    id_range = jnp.arange(NIDS, dtype=jnp.int32)
    picks = routes[:, :, None] == id_range[None, None, :]
    named = jnp.sum(picks.astype(jnp.int32), axis=1)
    blocked = named.reshape(block_count, BLOCK, NIDS)
    earlier = (jnp.cumsum(blocked, axis=1) - blocked).reshape(token_count, NIDS)
    slot = jnp.sum(jnp.where(picks, earlier[:, None, :], 0), axis=2).astype(jnp.int32)
    block_index = (jnp.arange(token_count, dtype=jnp.int32) // BLOCK)[:, None]
    position = (block_index * CAP + slot).astype(jnp.int32)

    logits = jnp.dot(tokens, router, preferred_element_type=jnp.float32)
    chosen = jnp.sum(jnp.where(picks, jax.nn.sigmoid(logits)[:, None, :], 0.0), axis=2)
    gates = chosen.astype(jnp.bfloat16)

    flat_position = position.reshape(-1)
    flat_routes = routes.reshape(-1)
    flat_gates = gates.reshape(-1)
    pair_index = jnp.arange(token_count * TOP, dtype=jnp.int32)
    five_shape = (group_count, N_REP, 2, CAP, -1)

    def one_expert(carry, expert_inputs):
        mixed_sum, back_sum, gate_grad = carry
        expert_id, w_gate, w_up, w_down = expert_inputs
        target = jnp.where(flat_routes == expert_id, flat_position, buffer_rows).astype(jnp.int32)
        owner = jnp.full((buffer_rows,), -1, jnp.int32).at[target].set(pair_index, mode="drop")
        filled = owner >= 0
        pair_safe = jnp.where(filled, owner, 0).astype(jnp.int32)
        token_safe = (pair_safe // TOP).astype(jnp.int32)
        slot_gate = jnp.where(filled, flat_gates[pair_safe], jnp.zeros((), jnp.bfloat16))
        token_rows = jnp.where(filled[:, None], tokens[token_safe], jnp.zeros((), jnp.bfloat16))
        output_rows, hidden, pre_gate, pre_up = expert_forward(token_rows, w_gate, w_up, w_down)
        gate_float = slot_gate.astype(jnp.float32)[:, None]
        mixed_sum = mixed_sum.at[token_safe].add(gate_float * output_rows.astype(jnp.float32))
        cotangent = grad_out[token_safe].astype(jnp.float32)
        upstream = (gate_float * cotangent).astype(jnp.bfloat16)
        score = jnp.sum(output_rows.astype(jnp.float32) * cotangent, axis=1)
        landing = jnp.where(filled, owner, token_count * TOP).astype(jnp.int32)
        gate_grad = gate_grad.at[landing].set(score, mode="drop")
        back_rows, d_gate, d_up = expert_backward(pre_gate, pre_up, upstream, w_gate, w_up, w_down)
        back_rows = jnp.where(filled[:, None], back_rows.astype(jnp.float32), 0.0)
        back_sum = back_sum.at[token_safe].add(back_rows)
        rows_five = token_rows.reshape(five_shape).astype(jnp.float32)
        part_gate = jnp.einsum("grbcd,grbch->rbdh", rows_five, d_gate.reshape(five_shape).astype(jnp.float32))
        part_up = jnp.einsum("grbcd,grbch->rbdh", rows_five, d_up.reshape(five_shape).astype(jnp.float32))
        part_down = jnp.einsum("grbcd,grbch->rbdh", upstream.reshape(five_shape).astype(jnp.float32), hidden.reshape(five_shape).astype(jnp.float32))
        return (mixed_sum, back_sum, gate_grad), (copy_total(part_gate), copy_total(part_up), copy_total(part_down))

    start = (jnp.zeros((token_count, D), jnp.float32), jnp.zeros((token_count, D), jnp.float32), jnp.zeros((token_count * TOP,), jnp.float32))
    expert_ids = jnp.arange(EXPERTS, dtype=jnp.int32)
    carry, grads = lax.scan(one_expert, start, (expert_ids, gate_weight, up_weight, down_weight))
    mixed_sum, back_sum, gate_grad = carry
    grad_gate, grad_up, grad_down = grads

    gates_float = gates.astype(jnp.float32)
    is_copy = routes == EXPERTS + 1
    const_ids = EXPERTS + 2 + jnp.arange(NCONST, dtype=jnp.int32)
    is_const = routes[:, :, None] == const_ids[None, None, :]
    copy_weight = jnp.sum(jnp.where(is_copy, gates_float, 0.0), axis=1)
    const_weight = jnp.sum(jnp.where(is_const, gates_float[:, :, None], 0.0), axis=1)
    const_share = jax.nn.sigmoid(jnp.dot(tokens, const_gate, preferred_element_type=jnp.float32))
    const_rest = (const_weight * (1.0 - const_share)).astype(jnp.bfloat16)
    coefficient = copy_weight + jnp.sum(const_weight * const_share, axis=1)
    tokens_float = tokens.astype(jnp.float32)
    constant_term = jnp.dot(const_rest, const_vec, preferred_element_type=jnp.float32)
    mixed = (mixed_sum + coefficient[:, None] * tokens_float + constant_term).astype(jnp.bfloat16)

    cotangent_all = grad_out.astype(jnp.float32)
    along_token = jnp.sum(cotangent_all * tokens_float, axis=1)
    along_const = lax.dot_general(grad_out, const_vec, LAST_CONTRACT, preferred_element_type=jnp.float32)
    const_value = const_share * along_token[:, None] + (1.0 - const_share) * along_const
    null_grad = jnp.where(is_copy, along_token[:, None], 0.0) + jnp.sum(jnp.where(is_const, const_value[:, None, :], 0.0), axis=2)
    pick_grad = gate_grad.reshape(token_count, TOP) + null_grad
    slope_grad = pick_grad * chosen * (1.0 - chosen)
    logit_grad = jnp.sum(jnp.where(picks, slope_grad[:, :, None], 0.0), axis=1).astype(jnp.bfloat16)
    share_grad = (const_weight * (along_token[:, None] - along_const) * const_share * (1.0 - const_share)).astype(jnp.bfloat16)
    back_local = coefficient[:, None] * cotangent_all
    back_local = back_local + lax.dot_general(logit_grad, router, LAST_CONTRACT, preferred_element_type=jnp.float32)
    back_local = back_local + lax.dot_general(share_grad, const_gate, LAST_CONTRACT, preferred_element_type=jnp.float32)
    grad_tokens = (back_sum + back_local).astype(jnp.bfloat16)
    grad_router = lax.dot_general(tokens, logit_grad, ROWS_CONTRACT, preferred_element_type=jnp.float32)
    grad_const_vec = lax.dot_general(const_rest, grad_out, ROWS_CONTRACT, preferred_element_type=jnp.float32)
    grad_const_gate = lax.dot_general(tokens, share_grad, ROWS_CONTRACT, preferred_element_type=jnp.float32)
    return (mixed, grad_tokens, grad_gate, grad_up, grad_down, grad_router, grad_const_vec, grad_const_gate)
```

```python
import jax
import jax.numpy as jnp
from jax import lax
from jax.experimental import pallas as pl
from jax.experimental.pallas import tpu as pltpu
from jax.sharding import PartitionSpec as P

ROWS_CONTRACT = (((0,), (0,)), ((), ()))
LAST_CONTRACT = (((1,), (1,)), ((), ()))


def silu_slope(argument):
    logistic = jax.nn.sigmoid(argument)
    return logistic * (1.0 + argument * (1.0 - logistic))


def expert_forward(token_rows, w_gate, w_up, w_down):
    pre_gate = jnp.dot(token_rows, w_gate, preferred_element_type=jnp.float32)
    pre_up = jnp.dot(token_rows, w_up, preferred_element_type=jnp.float32)
    hidden = (jax.nn.silu(pre_gate) * pre_up).astype(jnp.bfloat16)
    output_rows = lax.dot_general(hidden, w_down, LAST_CONTRACT, preferred_element_type=jnp.float32)
    return (output_rows.astype(jnp.bfloat16), hidden, pre_gate, pre_up)


def expert_backward(pre_gate, pre_up, upstream, w_gate, w_up, w_down):
    d_hidden = jnp.dot(upstream, w_down, preferred_element_type=jnp.float32)
    d_gate = (d_hidden * pre_up * silu_slope(pre_gate)).astype(jnp.bfloat16)
    d_up = (d_hidden * jax.nn.silu(pre_gate)).astype(jnp.bfloat16)
    back_rows = lax.dot_general(d_gate, w_gate, LAST_CONTRACT, preferred_element_type=jnp.float32)
    back_rows = back_rows + lax.dot_general(
        d_up, w_up, LAST_CONTRACT, preferred_element_type=jnp.float32
    )
    return (back_rows.astype(jnp.bfloat16), d_gate, d_up)


def block_terms(token_rows, hidden, upstream, d_gate, d_up):
    term_gate = lax.dot_general(
        token_rows, d_gate, ROWS_CONTRACT, preferred_element_type=jnp.float32
    )
    term_up = lax.dot_general(token_rows, d_up, ROWS_CONTRACT, preferred_element_type=jnp.float32)
    term_down = lax.dot_general(upstream, hidden, ROWS_CONTRACT, preferred_element_type=jnp.float32)
    return (term_gate, term_up, term_down)


def token_trip(buffer):
    return lax.all_to_all(buffer, ("expert", "dp"), split_axis=0, concat_axis=0, tiled=True)


def on_device_general(
    tokens, routes, gate_weight, up_weight, down_weight, router, const_vec, const_gate, grad_out
):
    shard_rows, top_count = routes.shape
    row_count = shard_rows // lax.axis_size("rep")
    first_row = lax.axis_index("rep") * row_count
    tokens = lax.dynamic_slice_in_dim(tokens, first_row, row_count, 0)
    routes = lax.dynamic_slice_in_dim(routes, first_row, row_count, 0)
    grad_out = lax.dynamic_slice_in_dim(grad_out, first_row, row_count, 0)
    model_width = tokens.shape[1]
    id_count = router.shape[1]
    const_count = const_vec.shape[0]
    expert_count = id_count - 2 - const_count
    half_rows = row_count // 2
    capacity = (half_rows * top_count + id_count - 1) // id_count
    target_count = lax.axis_size("expert") * lax.axis_size("dp")
    slot_count = target_count * capacity
    stored_experts, stored_rows, hidden_width = gate_weight.shape
    spread = lax.axis_size("dp") * lax.axis_size("rep")
    id_range = lax.broadcasted_iota(jnp.int32, (1, 1, id_count), 2)
    picks = routes[:, :, None] == id_range
    named = jnp.sum(picks.astype(jnp.float32), axis=1)
    row_index = lax.broadcasted_iota(jnp.int32, (row_count, row_count), 0)
    column_index = lax.broadcasted_iota(jnp.int32, (row_count, row_count), 1)
    before = (
        (column_index < row_index) & (column_index // half_rows == row_index // half_rows)
    ).astype(jnp.float32)
    earlier = jnp.dot(before, named, precision=lax.Precision.HIGHEST)
    slot = jnp.sum(jnp.where(picks, earlier[:, None, :], 0.0), axis=2).astype(jnp.int32)
    member = lax.broadcasted_iota(jnp.int32, (row_count, top_count), 0) // half_rows
    routed = routes < expert_count
    target = jnp.where(routed, (2 * routes + member) * capacity + slot, slot_count)
    slot_range = lax.broadcasted_iota(jnp.int32, (slot_count, 1), 0)
    pair_range = lax.broadcasted_iota(jnp.int32, (1, row_count * top_count), 1)
    hits = slot_range == target.reshape(1, -1)
    owner = jnp.sum(jnp.where(hits, pair_range, 0), axis=1)
    filled = jnp.any(hits, axis=1)
    owner_token = owner // top_count
    target_safe = jnp.where(routed, target, 0)
    logits = jnp.dot(tokens, router, preferred_element_type=jnp.float32)
    chosen = jnp.sum(jnp.where(picks, jax.nn.sigmoid(logits)[:, None, :], 0.0), axis=2)
    gates = chosen.astype(jnp.bfloat16)
    gates_float = gates.astype(jnp.float32)
    slot_gate = jnp.where(filled, gates.reshape(-1)[owner], jnp.zeros((), jnp.bfloat16)).astype(
        jnp.float32
    )
    repeat = spread // stored_experts
    fetched = (
        lax.all_to_all(
            jnp.repeat(gate_weight, repeat, axis=0),
            ("dp", "rep"),
            split_axis=0,
            concat_axis=1,
            tiled=True,
        ),
        lax.all_to_all(
            jnp.repeat(up_weight, repeat, axis=0),
            ("dp", "rep"),
            split_axis=0,
            concat_axis=1,
            tiled=True,
        ),
        lax.all_to_all(
            jnp.repeat(down_weight, repeat, axis=0),
            ("dp", "rep"),
            split_axis=0,
            concat_axis=1,
            tiled=True,
        ),
    )
    w_gate = fetched[0].reshape(model_width, hidden_width)
    w_up = fetched[1].reshape(model_width, hidden_width)
    w_down = fetched[2].reshape(model_width, hidden_width)
    send_rows = jnp.where(filled[:, None], tokens[owner_token], jnp.zeros((), jnp.bfloat16))
    arrived = token_trip(send_rows.reshape(target_count, capacity, model_width)).reshape(
        slot_count, model_width
    )
    output_rows, hidden, pre_gate, pre_up = expert_forward(arrived, w_gate, w_up, w_down)
    returned = token_trip(output_rows.reshape(target_count, capacity, model_width)).reshape(
        slot_count, model_width
    )
    picked_out = returned[target_safe].astype(jnp.float32)
    mixed_sum = jnp.sum(
        jnp.where(routed[:, :, None], gates_float[:, :, None] * picked_out, 0.0), axis=1
    )
    cotangent_all = grad_out.astype(jnp.float32)
    routed_grad = jnp.sum(
        jnp.where(routed[:, :, None], picked_out * cotangent_all[:, None, :], 0.0), axis=2
    )
    upstream_send = (slot_gate[:, None] * grad_out[owner_token].astype(jnp.float32)).astype(
        jnp.bfloat16
    )
    upstream = token_trip(upstream_send.reshape(target_count, capacity, model_width)).reshape(
        slot_count, model_width
    )
    back_rows, d_gate, d_up = expert_backward(pre_gate, pre_up, upstream, w_gate, w_up, w_down)
    terms = block_terms(arrived, hidden, upstream, d_gate, d_up)
    sent_terms = tuple(
        (term.astype(jnp.bfloat16).reshape(spread, stored_rows, hidden_width) for term in terms)
    )
    gathered_terms = (
        lax.all_to_all(sent_terms[0], ("dp", "rep"), split_axis=0, concat_axis=0, tiled=True),
        lax.all_to_all(sent_terms[1], ("dp", "rep"), split_axis=0, concat_axis=0, tiled=True),
        lax.all_to_all(sent_terms[2], ("dp", "rep"), split_axis=0, concat_axis=0, tiled=True),
    )
    copies = spread // stored_experts
    grad_gate, grad_up, grad_down = (
        jnp.sum(
            arrived_term.reshape(stored_experts, copies, stored_rows, hidden_width),
            axis=1,
            dtype=jnp.float32,
        ).astype(jnp.bfloat16)
        for arrived_term in gathered_terms
    )
    returned_back = token_trip(back_rows.reshape(target_count, capacity, model_width)).reshape(
        slot_count, model_width
    )
    back_sum = jnp.sum(
        jnp.where(routed[:, :, None], returned_back[target_safe].astype(jnp.float32), 0.0), axis=1
    )
    is_copy = routes == expert_count + 1
    const_ids = expert_count + 2 + lax.broadcasted_iota(jnp.int32, (1, 1, const_count), 2)
    is_const = routes[:, :, None] == const_ids
    copy_weight = jnp.sum(jnp.where(is_copy, gates_float, 0.0), axis=1)
    const_weight = jnp.sum(jnp.where(is_const, gates_float[:, :, None], 0.0), axis=1)
    const_share = jax.nn.sigmoid(jnp.dot(tokens, const_gate, preferred_element_type=jnp.float32))
    const_rest = (const_weight * (1.0 - const_share)).astype(jnp.bfloat16)
    coefficient = copy_weight + jnp.sum(const_weight * const_share, axis=1)
    tokens_float = tokens.astype(jnp.float32)
    constant_term = jnp.dot(const_rest, const_vec, preferred_element_type=jnp.float32)
    mixed = (mixed_sum + coefficient[:, None] * tokens_float + constant_term).astype(jnp.bfloat16)
    along_token = jnp.sum(cotangent_all * tokens_float, axis=1)
    along_const = lax.dot_general(
        grad_out, const_vec, LAST_CONTRACT, preferred_element_type=jnp.float32
    )
    const_value = const_share * along_token[:, None] + (1.0 - const_share) * along_const
    null_grad = jnp.where(is_copy, along_token[:, None], 0.0) + jnp.sum(
        jnp.where(is_const, const_value[:, None, :], 0.0), axis=2
    )
    pick_grad = routed_grad + null_grad
    slope_grad = pick_grad * chosen * (1.0 - chosen)
    logit_grad = jnp.sum(jnp.where(picks, slope_grad[:, :, None], 0.0), axis=1).astype(jnp.bfloat16)
    share_grad = (
        const_weight * (along_token[:, None] - along_const) * const_share * (1.0 - const_share)
    ).astype(jnp.bfloat16)
    back_local = coefficient[:, None] * cotangent_all
    back_local = back_local + lax.dot_general(
        logit_grad, router, LAST_CONTRACT, preferred_element_type=jnp.float32
    )
    back_local = back_local + lax.dot_general(
        share_grad, const_gate, LAST_CONTRACT, preferred_element_type=jnp.float32
    )
    grad_tokens = (back_sum + back_local).astype(jnp.bfloat16)
    router_part = lax.dot_general(
        tokens, logit_grad, ROWS_CONTRACT, preferred_element_type=jnp.float32
    )
    vector_part = lax.dot_general(
        const_rest, grad_out, ROWS_CONTRACT, preferred_element_type=jnp.float32
    )
    mixing_part = lax.dot_general(
        tokens, share_grad, ROWS_CONTRACT, preferred_element_type=jnp.float32
    )
    grad_router, grad_const_vec, grad_const_gate = lax.psum(
        (router_part, vector_part, mixing_part), ("expert", "dp", "rep")
    )
    mixed_all, grad_tokens_all = (
        lax.all_gather(mixed, "rep", axis=0, tiled=True),
        lax.all_gather(grad_tokens, "rep", axis=0, tiled=True),
    )
    return (
        mixed_all,
        grad_tokens_all,
        grad_gate,
        grad_up,
        grad_down,
        grad_router,
        grad_const_vec,
        grad_const_gate,
    )


HALF = 64
SLOTS = 32


def full_block(shape):
    return pl.BlockSpec(shape, lambda *_: (0,) * len(shape))


def local_kernel(body, operands, outputs, scalars=None, flops=0):
    in_specs = [pl.BlockSpec(memory_space=pltpu.VMEM) for _ in operands]
    if scalars is not None:
        in_specs = [pl.BlockSpec(memory_space=pltpu.SMEM)] + in_specs
        operands = [scalars] + list(operands)
    moved = sum(o.size * o.dtype.itemsize for o in operands)
    moved += sum(o.size * o.dtype.itemsize for o in outputs)
    return pl.pallas_call(
        body,
        out_shape=outputs,
        in_specs=in_specs,
        out_specs=[pl.BlockSpec(memory_space=pltpu.VMEM) for _ in outputs],
        compiler_params=pltpu.CompilerParams(vmem_limit_bytes=56 * 1024 * 1024),
        cost_estimate=pl.CostEstimate(flops=flops, bytes_accessed=moved, transcendentals=0),
    )(*operands)


def mm(a, b):
    return jnp.dot(a, b, preferred_element_type=jnp.float32)


def mm_rows(a, b):
    return lax.dot_general(a, b, ROWS_CONTRACT, preferred_element_type=jnp.float32)


def mm_last(a, b):
    return lax.dot_general(a, b, LAST_CONTRACT, preferred_element_type=jnp.float32)


def forward_kernel(place, *refs):
    gates, tokens, w_gate, w_up = refs[0:4], refs[4:12], refs[12:16], refs[16:20]
    pick_out, gate_out, rows_out, hidden_out, act_out, slope_out = refs[20:26]
    me, expert = place[0], place[1]
    span = 2 * tokens[0].shape[0]
    width = w_gate[0].shape[0]
    earlier_than = lax.broadcasted_iota(jnp.int32, (span, span), 0)
    later = lax.broadcasted_iota(jnp.int32, (span, span), 1)
    before = ((earlier_than < later) & (earlier_than // HALF == later // HALF)).astype(jnp.bfloat16)
    lane = lax.broadcasted_iota(jnp.int32, (1, span), 1)
    for k in range(4):
        gate = gates[k][pl.ds(expert, 1), :]
        picked = gate != 0.0
        earlier = mm(
            jnp.broadcast_to(picked.astype(jnp.bfloat16), (16, span)), before
        )[0:1].astype(jnp.int32)
        target = jnp.where(picked, (lane // HALF) * SLOTS + earlier, -1)
        for core in range(2):
            half = span // 2
            slots = half // 2
            slot = lax.broadcasted_iota(jnp.int32, (slots, half), 0) + core * slots
            chosen = slot == target[:, core * half : (core + 1) * half]
            pick = chosen.astype(jnp.bfloat16)
            at = (2 * k + core) * slots
            pick_out[at : at + slots, :] = pick
            gate_out[at : at + slots, :] = jnp.where(
                chosen, gate[:, core * half : (core + 1) * half], 0.0
            ).astype(jnp.bfloat16)
            for j in range(4):
                columns = pl.ds(pl.multiple_of((me ^ j) * width, width), width)
                rows_out[at : at + slots, j * width : (j + 1) * width] = mm(
                    pick, tokens[2 * k + core][:, columns]
                ).astype(jnp.bfloat16)
    pre_gate = jnp.zeros(hidden_out.shape, jnp.float32)
    pre_up = jnp.zeros(hidden_out.shape, jnp.float32)
    for j in range(4):
        rows = rows_out[:, j * width : (j + 1) * width]
        pre_gate += mm(rows, w_gate[j][...])
        pre_up += mm(rows, w_up[j][...])
    logistic = jax.nn.sigmoid(pre_gate)
    act = pre_gate * logistic
    hidden_out[...] = (act * pre_up).astype(jnp.bfloat16)
    act_out[...] = act.astype(jnp.bfloat16)
    slope = logistic * (1.0 + pre_gate * (1.0 - logistic))
    slope_out[...] = (pre_up * slope).astype(jnp.bfloat16)


def down_grad_kernel(place, *refs):
    pick, gate_pick, hidden = refs[0:3]
    grads = refs[3:11]
    cot_out, up_out = refs[11:13]
    down_out = refs[13:17]
    me = place[0]
    width = down_out[0].shape[0]
    slots = grads[0].shape[0] // 2
    gate = jnp.sum(gate_pick[...].astype(jnp.float32), axis=1, keepdims=True)
    for b in range(8):
        at = b * slots
        for j in range(4):
            columns = pl.ds(pl.multiple_of((me ^ j) * width, width), width)
            cot = mm(pick[at : at + slots, :], grads[b][:, columns])
            cot_out[at : at + slots, j * width : (j + 1) * width] = cot.astype(jnp.bfloat16)
            up_out[at : at + slots, j * width : (j + 1) * width] = (
                gate[at : at + slots] * cot
            ).astype(jnp.bfloat16)
    for j in range(4):
        down_out[j][...] = mm_rows(
            up_out[:, j * width : (j + 1) * width], hidden[...]
        ).astype(jnp.bfloat16)


def backward_kernel(place, *refs):
    pick, rows, upstream, act, slope = refs[0:5]
    w_gate, w_up, w_down = refs[5:9], refs[9:13], refs[13:17]
    gate_out, up_out = refs[17:21], refs[21:25]
    own_out, other_out = refs[25:27]
    me = place[0]
    width = w_gate[0].shape[0]
    d_hidden = jnp.zeros(act.shape, jnp.float32)
    for j in range(4):
        d_hidden += mm(upstream[:, j * width : (j + 1) * width], w_down[j][...])
    d_gate = (d_hidden * slope[...].astype(jnp.float32)).astype(jnp.bfloat16)
    d_up = (d_hidden * act[...].astype(jnp.float32)).astype(jnp.bfloat16)
    for j in range(4):
        part = rows[:, j * width : (j + 1) * width]
        gate_out[j][...] = mm_rows(part, d_gate).astype(jnp.bfloat16)
        up_out[j][...] = mm_rows(part, d_up).astype(jnp.bfloat16)
    scatter(me, pick, own_out, other_out, width, lambda j: (
        mm_last(d_gate, w_gate[j][...]) + mm_last(d_up, w_up[j][...])
    ).astype(jnp.bfloat16))


def scatter(me, pick, own_out, other_out, width, column_block):
    slots = pick.shape[0] // 8
    half = pick.shape[1]
    for j in range(4):
        columns = pl.ds(pl.multiple_of((me ^ j) * width, width), width)
        block = column_block(j)
        for b in range(8):
            out = own_out if b % 2 == 0 else other_out
            at = b * slots
            out[(b // 2) * half : (b // 2 + 1) * half, columns] = mm_rows(
                pick[at : at + slots, :], block[at : at + slots]
            ).astype(jnp.bfloat16)


def output_kernel(place, *refs):
    pick, gate_pick, hidden, cot = refs[0:4]
    w_down = refs[4:8]
    own_out, other_out, score_out = refs[8:11]
    me = place[0]
    width = w_down[0].shape[0]
    slots = pick.shape[0] // 8
    scores = []

    def column_block(j):
        block = mm_last(hidden[...], w_down[j][...]).astype(jnp.bfloat16)
        scores.append(
            jnp.sum(
                block.astype(jnp.float32)
                * cot[:, j * width : (j + 1) * width].astype(jnp.float32),
                axis=1,
                keepdims=True,
            )
        )
        return block

    scatter(me, gate_pick, own_out, other_out, width, column_block)
    score = scores[0] + scores[1] + scores[2] + scores[3]
    spread = pick[...].astype(jnp.float32) * score
    for b in range(8):
        score_out[b : b + 1, :] = jnp.sum(
            spread[b * slots : (b + 1) * slots], axis=0, keepdims=True
        )


def dp_swap(value, step):
    return lax.ppermute(value, "dp", [(i, i ^ step) for i in range(4)])


def ring(value, step):
    size = lax.axis_size("expert")
    return lax.ppermute(value, "expert", [(i, (i + step) % size) for i in range(size)])


def gather_rows(block):
    own = [block]
    for _ in range(3):
        own.append(ring(own[-1], 1))
    other = [dp_swap(value, 1) for value in own]
    return [value for pair in zip(own, other) for value in pair]


def on_device_paired(
    tokens, routes, gate_weight, up_weight, down_weight, router, const_vec, const_gate, grad_out
):
    bf16, f32 = jnp.bfloat16, jnp.float32
    row_count, model_width = tokens.shape
    id_count = router.shape[1]
    const_count = const_vec.shape[0]
    expert_count = id_count - 2 - const_count
    stored_experts, stored_rows, hidden_width = gate_weight.shape
    me = lax.axis_index("dp")
    z = lax.axis_index("expert")
    core = me % 2
    expert = stored_experts * z + core
    place = jnp.stack([me, expert]).astype(jnp.int32)

    def fetch(weight):
        mine = lax.dynamic_index_in_dim(weight, core, 0, keepdims=False)
        theirs = lax.dynamic_index_in_dim(weight, 1 - core, 0, keepdims=False)
        return [mine, dp_swap(theirs, 1), dp_swap(mine, 2), dp_swap(theirs, 3)]

    all_tokens = gather_rows(tokens)
    w_gate = fetch(gate_weight)
    w_up = fetch(up_weight)
    all_grads = gather_rows(grad_out)
    w_down = fetch(down_weight)

    id_range = lax.broadcasted_iota(jnp.int32, (1, 1, id_count), 2)
    named = jnp.any(routes[:, :, None] == id_range, axis=1)
    logits = mm(tokens, router)
    share = jax.nn.sigmoid(logits)
    chosen = jnp.where(named, share, 0.0)
    gates = chosen.astype(bf16).astype(f32)

    gate_rows = gates[:, :expert_count].T
    gate_pair = jnp.concatenate([gate_rows, dp_swap(gate_rows, 1)], axis=1)
    gate_all = [gate_pair] + [ring(gate_pair, k) for k in range(1, 4)]

    slot_count = 4 * row_count
    shape = jax.ShapeDtypeStruct
    wide = shape((slot_count, model_width), bf16)
    narrow = shape((slot_count, hidden_width), bf16)
    table = shape((slot_count, row_count), bf16)
    weight_rows = shape((stored_rows, hidden_width), bf16)
    product = 2 * slot_count * model_width * hidden_width
    pick, gate_pick, rows, hidden, act, slope = local_kernel(
        forward_kernel,
        [*gate_all, *all_tokens, *w_gate, *w_up],
        [table, table, wide, narrow, narrow, narrow],
        place,
        2 * product,
    )
    cot, upstream, *down_part = local_kernel(
        down_grad_kernel,
        [pick, gate_pick, hidden, *all_grads],
        [wide, wide] + [weight_rows] * 4,
        place,
        product,
    )
    *parts, back_own, back_other = local_kernel(
        backward_kernel,
        [pick, rows, upstream, act, slope, *w_gate, *w_up, *w_down],
        [weight_rows] * 8 + [wide, wide],
        place,
        5 * product,
    )
    gate_part, up_part = parts[0:4], parts[4:8]
    mixed_own, mixed_other, score = local_kernel(
        output_kernel,
        [pick, gate_pick, hidden, cot, *w_down],
        [wide, wide, shape((8, row_count), f32)],
        place,
        product,
    )

    def join(part):
        mine = part[0].astype(f32) + dp_swap(part[2], 2).astype(f32)
        theirs = dp_swap(part[1], 1).astype(f32) + dp_swap(part[3], 3).astype(f32)
        mine, theirs = mine.astype(bf16), theirs.astype(bf16)
        return jnp.where(core == 0, jnp.stack([mine, theirs]), jnp.stack([theirs, mine]))

    def home(own, other):
        both = own.astype(f32) + dp_swap(other, 1).astype(f32)
        slots = both.astype(bf16).reshape(4, row_count, model_width)
        moving = slots[3]
        for k in (2, 1):
            moving = (ring(moving, -1).astype(f32) + slots[k].astype(f32)).astype(bf16)
        return ring(moving, -1).astype(f32) + slots[0].astype(f32)

    grad_down = join(down_part)
    grad_gate = join(gate_part)
    grad_up = join(up_part)

    score = score.reshape(4, 2, row_count)
    score_mine, score_theirs = score[:, 0], dp_swap(score[:, 1], 1)
    score_pair = jnp.where(
        core == 0,
        jnp.stack([score_mine, score_theirs], axis=1),
        jnp.stack([score_theirs, score_mine], axis=1),
    )
    score_at = [score_pair[0]] + [ring(score_pair[k], -k) for k in range(1, 4)]
    z_range = lax.broadcasted_iota(jnp.int32, (4, 1, 1), 0)
    routed_score = sum(
        jnp.where(z_range == (z + k) % 4, score_at[k][None], 0.0) for k in range(4)
    )
    routed_score = routed_score.reshape(expert_count, row_count).T

    mixed_sum = home(mixed_own, mixed_other)
    back_sum = home(back_own, back_other)

    tokens_float = tokens.astype(f32)
    grad_float = grad_out.astype(f32)
    copy_weight = gates[:, expert_count + 1]
    const_weight = gates[:, expert_count + 2 :]
    const_share = jax.nn.sigmoid(mm(tokens, const_gate))
    const_rest = (const_weight * (1.0 - const_share)).astype(bf16)
    coefficient = copy_weight + jnp.sum(const_weight * const_share, axis=1)
    mixed = (
        mixed_sum + coefficient[:, None] * tokens_float + mm(const_rest, const_vec)
    ).astype(bf16)
    along_token = jnp.sum(grad_float * tokens_float, axis=1, keepdims=True)
    along_const = mm_last(grad_out, const_vec)
    const_value = const_share * along_token + (1.0 - const_share) * along_const
    pick_grad = jnp.concatenate(
        [routed_score, jnp.zeros_like(along_token), along_token, const_value], axis=1
    )
    logit_grad = jnp.where(named, pick_grad * share * (1.0 - share), 0.0).astype(bf16)
    share_grad = (
        const_weight * (along_token - along_const) * const_share * (1.0 - const_share)
    ).astype(bf16)
    back_local = (
        coefficient[:, None] * grad_float
        + mm_last(logit_grad, router)
        + mm_last(share_grad, const_gate)
    )
    grad_tokens = (back_sum + back_local).astype(bf16)

    small = jnp.concatenate(
        [
            mm_rows(jnp.concatenate([logit_grad, share_grad], axis=1), tokens),
            mm_rows(const_rest, grad_out),
        ],
        axis=0,
    )
    for step in (1, 2):
        small = small + dp_swap(small, step)
    for step in (1, 2):
        small = small + lax.ppermute(small, "expert", [(i, i ^ step) for i in range(4)])
    grad_router = small[:id_count].T
    grad_const_gate = small[id_count : id_count + const_count].T
    grad_const_vec = small[id_count + const_count :]
    return (
        mixed,
        grad_tokens,
        grad_gate,
        grad_up,
        grad_down,
        grad_router,
        grad_const_vec,
        grad_const_gate,
    )


def solution(mesh):
    paired = mesh.shape["rep"] == 1 and mesh.shape["dp"] == 4

    def on_device(tokens, routes, gate_weight, *others):
        id_count = others[2].shape[1]
        stored_experts, stored_rows, hidden_width = gate_weight.shape
        row_count, top_count = routes.shape
        halved = row_count * top_count == (row_count // 2) * id_count
        if paired and stored_experts == 2 and halved and row_count == 128:
            return on_device_paired(tokens, routes, gate_weight, *others)
        return on_device_general(tokens, routes, gate_weight, *others)

    placed = (
        P(("groups", "expert", "dp"), None),
        P(("groups", "expert", "dp"), None),
        P("expert", ("dp", "rep"), None),
        P("expert", ("dp", "rep"), None),
        P("expert", ("dp", "rep"), None),
        P(),
        P(),
        P(),
        P(("groups", "expert", "dp"), None),
    )
    return jax.shard_map(
        on_device,
        mesh=mesh,
        in_specs=placed,
        out_specs=(
            P(("groups", "expert", "dp"), None),
            P(("groups", "expert", "dp"), None),
            P(("groups", "expert"), ("dp", "rep"), None),
            P(("groups", "expert"), ("dp", "rep"), None),
            P(("groups", "expert"), ("dp", "rep"), None),
            P("groups", None),
            P("groups", None),
            P("groups", None),
        ),
        check_vma=False,
    )
```

```python
import jax
import jax.numpy as jnp
from jax import lax
from jax.experimental import pallas as pl
from jax.experimental.pallas import tpu as pltpu
from jax.sharding import PartitionSpec as P

ROWS_CONTRACT = (((0,), (0,)), ((), ()))
LAST_CONTRACT = (((1,), (1,)), ((), ()))


def silu_slope(argument):
    logistic = jax.nn.sigmoid(argument)
    return logistic * (1.0 + argument * (1.0 - logistic))


def expert_forward(token_rows, w_gate, w_up, w_down):
    pre_gate = jnp.dot(token_rows, w_gate, preferred_element_type=jnp.float32)
    pre_up = jnp.dot(token_rows, w_up, preferred_element_type=jnp.float32)
    hidden = (jax.nn.silu(pre_gate) * pre_up).astype(jnp.bfloat16)
    output_rows = lax.dot_general(hidden, w_down, LAST_CONTRACT, preferred_element_type=jnp.float32)
    return (output_rows.astype(jnp.bfloat16), hidden, pre_gate, pre_up)


def expert_backward(pre_gate, pre_up, upstream, w_gate, w_up, w_down):
    d_hidden = jnp.dot(upstream, w_down, preferred_element_type=jnp.float32)
    d_gate = (d_hidden * pre_up * silu_slope(pre_gate)).astype(jnp.bfloat16)
    d_up = (d_hidden * jax.nn.silu(pre_gate)).astype(jnp.bfloat16)
    back_rows = lax.dot_general(d_gate, w_gate, LAST_CONTRACT, preferred_element_type=jnp.float32)
    back_rows = back_rows + lax.dot_general(
        d_up, w_up, LAST_CONTRACT, preferred_element_type=jnp.float32
    )
    return (back_rows.astype(jnp.bfloat16), d_gate, d_up)


def block_terms(token_rows, hidden, upstream, d_gate, d_up):
    term_gate = lax.dot_general(
        token_rows, d_gate, ROWS_CONTRACT, preferred_element_type=jnp.float32
    )
    term_up = lax.dot_general(token_rows, d_up, ROWS_CONTRACT, preferred_element_type=jnp.float32)
    term_down = lax.dot_general(upstream, hidden, ROWS_CONTRACT, preferred_element_type=jnp.float32)
    return (term_gate, term_up, term_down)


def token_trip(buffer):
    return lax.all_to_all(buffer, ("expert", "dp"), split_axis=0, concat_axis=0, tiled=True)


def on_device_general(
    tokens, routes, gate_weight, up_weight, down_weight, router, const_vec, const_gate, grad_out
):
    shard_rows, top_count = routes.shape
    row_count = shard_rows // lax.axis_size("rep")
    first_row = lax.axis_index("rep") * row_count
    tokens = lax.dynamic_slice_in_dim(tokens, first_row, row_count, 0)
    routes = lax.dynamic_slice_in_dim(routes, first_row, row_count, 0)
    grad_out = lax.dynamic_slice_in_dim(grad_out, first_row, row_count, 0)
    model_width = tokens.shape[1]
    id_count = router.shape[1]
    const_count = const_vec.shape[0]
    expert_count = id_count - 2 - const_count
    half_rows = row_count // 2
    capacity = (half_rows * top_count + id_count - 1) // id_count
    target_count = lax.axis_size("expert") * lax.axis_size("dp")
    slot_count = target_count * capacity
    stored_experts, stored_rows, hidden_width = gate_weight.shape
    spread = lax.axis_size("dp") * lax.axis_size("rep")
    id_range = lax.broadcasted_iota(jnp.int32, (1, 1, id_count), 2)
    picks = routes[:, :, None] == id_range
    named = jnp.sum(picks.astype(jnp.float32), axis=1)
    row_index = lax.broadcasted_iota(jnp.int32, (row_count, row_count), 0)
    column_index = lax.broadcasted_iota(jnp.int32, (row_count, row_count), 1)
    before = (
        (column_index < row_index) & (column_index // half_rows == row_index // half_rows)
    ).astype(jnp.float32)
    earlier = jnp.dot(before, named, precision=lax.Precision.HIGHEST)
    slot = jnp.sum(jnp.where(picks, earlier[:, None, :], 0.0), axis=2).astype(jnp.int32)
    member = lax.broadcasted_iota(jnp.int32, (row_count, top_count), 0) // half_rows
    routed = routes < expert_count
    target = jnp.where(routed, (2 * routes + member) * capacity + slot, slot_count)
    slot_range = lax.broadcasted_iota(jnp.int32, (slot_count, 1), 0)
    pair_range = lax.broadcasted_iota(jnp.int32, (1, row_count * top_count), 1)
    hits = slot_range == target.reshape(1, -1)
    owner = jnp.sum(jnp.where(hits, pair_range, 0), axis=1)
    filled = jnp.any(hits, axis=1)
    owner_token = owner // top_count
    target_safe = jnp.where(routed, target, 0)
    logits = jnp.dot(tokens, router, preferred_element_type=jnp.float32)
    chosen = jnp.sum(jnp.where(picks, jax.nn.sigmoid(logits)[:, None, :], 0.0), axis=2)
    gates = chosen.astype(jnp.bfloat16)
    gates_float = gates.astype(jnp.float32)
    slot_gate = jnp.where(filled, gates.reshape(-1)[owner], jnp.zeros((), jnp.bfloat16)).astype(
        jnp.float32
    )
    repeat = spread // stored_experts
    fetched = (
        lax.all_to_all(
            jnp.repeat(gate_weight, repeat, axis=0),
            ("dp", "rep"),
            split_axis=0,
            concat_axis=1,
            tiled=True,
        ),
        lax.all_to_all(
            jnp.repeat(up_weight, repeat, axis=0),
            ("dp", "rep"),
            split_axis=0,
            concat_axis=1,
            tiled=True,
        ),
        lax.all_to_all(
            jnp.repeat(down_weight, repeat, axis=0),
            ("dp", "rep"),
            split_axis=0,
            concat_axis=1,
            tiled=True,
        ),
    )
    w_gate = fetched[0].reshape(model_width, hidden_width)
    w_up = fetched[1].reshape(model_width, hidden_width)
    w_down = fetched[2].reshape(model_width, hidden_width)
    send_rows = jnp.where(filled[:, None], tokens[owner_token], jnp.zeros((), jnp.bfloat16))
    arrived = token_trip(send_rows.reshape(target_count, capacity, model_width)).reshape(
        slot_count, model_width
    )
    output_rows, hidden, pre_gate, pre_up = expert_forward(arrived, w_gate, w_up, w_down)
    returned = token_trip(output_rows.reshape(target_count, capacity, model_width)).reshape(
        slot_count, model_width
    )
    picked_out = returned[target_safe].astype(jnp.float32)
    mixed_sum = jnp.sum(
        jnp.where(routed[:, :, None], gates_float[:, :, None] * picked_out, 0.0), axis=1
    )
    cotangent_all = grad_out.astype(jnp.float32)
    routed_grad = jnp.sum(
        jnp.where(routed[:, :, None], picked_out * cotangent_all[:, None, :], 0.0), axis=2
    )
    upstream_send = (slot_gate[:, None] * grad_out[owner_token].astype(jnp.float32)).astype(
        jnp.bfloat16
    )
    upstream = token_trip(upstream_send.reshape(target_count, capacity, model_width)).reshape(
        slot_count, model_width
    )
    back_rows, d_gate, d_up = expert_backward(pre_gate, pre_up, upstream, w_gate, w_up, w_down)
    terms = block_terms(arrived, hidden, upstream, d_gate, d_up)
    sent_terms = tuple(
        (term.astype(jnp.bfloat16).reshape(spread, stored_rows, hidden_width) for term in terms)
    )
    gathered_terms = (
        lax.all_to_all(sent_terms[0], ("dp", "rep"), split_axis=0, concat_axis=0, tiled=True),
        lax.all_to_all(sent_terms[1], ("dp", "rep"), split_axis=0, concat_axis=0, tiled=True),
        lax.all_to_all(sent_terms[2], ("dp", "rep"), split_axis=0, concat_axis=0, tiled=True),
    )
    copies = spread // stored_experts
    grad_gate, grad_up, grad_down = (
        jnp.sum(
            arrived_term.reshape(stored_experts, copies, stored_rows, hidden_width),
            axis=1,
            dtype=jnp.float32,
        ).astype(jnp.bfloat16)
        for arrived_term in gathered_terms
    )
    returned_back = token_trip(back_rows.reshape(target_count, capacity, model_width)).reshape(
        slot_count, model_width
    )
    back_sum = jnp.sum(
        jnp.where(routed[:, :, None], returned_back[target_safe].astype(jnp.float32), 0.0), axis=1
    )
    is_copy = routes == expert_count + 1
    const_ids = expert_count + 2 + lax.broadcasted_iota(jnp.int32, (1, 1, const_count), 2)
    is_const = routes[:, :, None] == const_ids
    copy_weight = jnp.sum(jnp.where(is_copy, gates_float, 0.0), axis=1)
    const_weight = jnp.sum(jnp.where(is_const, gates_float[:, :, None], 0.0), axis=1)
    const_share = jax.nn.sigmoid(jnp.dot(tokens, const_gate, preferred_element_type=jnp.float32))
    const_rest = (const_weight * (1.0 - const_share)).astype(jnp.bfloat16)
    coefficient = copy_weight + jnp.sum(const_weight * const_share, axis=1)
    tokens_float = tokens.astype(jnp.float32)
    constant_term = jnp.dot(const_rest, const_vec, preferred_element_type=jnp.float32)
    mixed = (mixed_sum + coefficient[:, None] * tokens_float + constant_term).astype(jnp.bfloat16)
    along_token = jnp.sum(cotangent_all * tokens_float, axis=1)
    along_const = lax.dot_general(
        grad_out, const_vec, LAST_CONTRACT, preferred_element_type=jnp.float32
    )
    const_value = const_share * along_token[:, None] + (1.0 - const_share) * along_const
    null_grad = jnp.where(is_copy, along_token[:, None], 0.0) + jnp.sum(
        jnp.where(is_const, const_value[:, None, :], 0.0), axis=2
    )
    pick_grad = routed_grad + null_grad
    slope_grad = pick_grad * chosen * (1.0 - chosen)
    logit_grad = jnp.sum(jnp.where(picks, slope_grad[:, :, None], 0.0), axis=1).astype(jnp.bfloat16)
    share_grad = (
        const_weight * (along_token[:, None] - along_const) * const_share * (1.0 - const_share)
    ).astype(jnp.bfloat16)
    back_local = coefficient[:, None] * cotangent_all
    back_local = back_local + lax.dot_general(
        logit_grad, router, LAST_CONTRACT, preferred_element_type=jnp.float32
    )
    back_local = back_local + lax.dot_general(
        share_grad, const_gate, LAST_CONTRACT, preferred_element_type=jnp.float32
    )
    grad_tokens = (back_sum + back_local).astype(jnp.bfloat16)
    router_part = lax.dot_general(
        tokens, logit_grad, ROWS_CONTRACT, preferred_element_type=jnp.float32
    )
    vector_part = lax.dot_general(
        const_rest, grad_out, ROWS_CONTRACT, preferred_element_type=jnp.float32
    )
    mixing_part = lax.dot_general(
        tokens, share_grad, ROWS_CONTRACT, preferred_element_type=jnp.float32
    )
    grad_router, grad_const_vec, grad_const_gate = lax.psum(
        (router_part, vector_part, mixing_part), ("expert", "dp", "rep")
    )
    mixed_all, grad_tokens_all = (
        lax.all_gather(mixed, "rep", axis=0, tiled=True),
        lax.all_gather(grad_tokens, "rep", axis=0, tiled=True),
    )
    return (
        mixed_all,
        grad_tokens_all,
        grad_gate,
        grad_up,
        grad_down,
        grad_router,
        grad_const_vec,
        grad_const_gate,
    )


HALF = 64
SLOTS = 32
SCRATCH_BYTES = 56 * 1024 * 1024


def local_kernel(body, scalars, operands, outputs, scratch, flops):
    moved = sum(o.size * o.dtype.itemsize for o in [*operands, *outputs])
    return pl.pallas_call(
        body,
        out_shape=outputs,
        in_specs=[pl.BlockSpec(memory_space=pltpu.SMEM)]
        + [pl.BlockSpec(memory_space=pl.ANY) for _ in operands],
        out_specs=[pl.BlockSpec(memory_space=pltpu.VMEM) for _ in outputs],
        scratch_shapes=scratch,
        compiler_params=pltpu.CompilerParams(vmem_limit_bytes=SCRATCH_BYTES),
        cost_estimate=pl.CostEstimate(flops=0, bytes_accessed=0, transcendentals=0),
    )(scalars, *operands)


def bring(pairs, sems):
    copies = [
        pltpu.make_async_copy(source, target, sems.at[i])
        for i, (source, target) in enumerate(pairs)
    ]
    for copy in copies:
        copy.start()
    return copies


def mm(a, b):
    return jnp.dot(a, b, preferred_element_type=jnp.float32)


def mm_rows(a, b):
    return lax.dot_general(a, b, ROWS_CONTRACT, preferred_element_type=jnp.float32)


def mm_last(a, b):
    return lax.dot_general(a, b, LAST_CONTRACT, preferred_element_type=jnp.float32)


def weight_pairs(core, parts, target):
    stored, *fetched = parts
    width = target.shape[0] // 4
    sources = [stored.at[core], *fetched]
    return [(s, target.at[pl.ds(j * width, width)]) for j, s in enumerate(sources)]


def payload_kernel(tokens, grads, routes, router, out):
    count = tokens.shape[0]
    ids = lax.broadcasted_iota(jnp.int32, (router.shape[0], count), 0)
    named = routes[0:1, :] == ids
    for k in range(1, routes.shape[0]):
        named = named | (routes[k : k + 1, :] == ids)
    gates = jnp.where(named, jax.nn.sigmoid(mm_last(router[...], tokens[...])), 0.0)
    out[0:count, :] = tokens[...]
    out[count : 2 * count, :] = grads[...]
    for e in range(out.shape[1] // count):
        out[2 * count :, e * count : (e + 1) * count] = jnp.broadcast_to(
            gates[e : e + 1], (16, count)
        ).astype(jnp.bfloat16)


def forward_kernel(place, *refs):
    payloads = refs[0:8]
    gate_weight, up_weight, partner, cross, cross_partner = refs[8:13]
    (pick_out, gate_out, rows_out, cot_out, hidden_out, act_out, slope_out, keep_out,
     partner_out, cross_out) = refs[13:23]
    blocks, w_gate, w_up, upstream, sems = refs[23:28]
    me, expert = place[0], place[1]
    core = me & 1
    count = pick_out.shape[1]
    slots = count // HALF * SLOTS
    copies = bring(
        [(payloads[b], blocks.at[b]) for b in range(8)]
        + weight_pairs(core, (gate_weight, partner.at[0], cross.at[0], cross_partner.at[0]), w_gate)
        + weight_pairs(core, (up_weight, partner.at[1], cross.at[1], cross_partner.at[1]), w_up),
        sems,
    )
    width = w_gate.shape[0] // 4
    row = lax.broadcasted_iota(jnp.int32, (count, count), 0)
    column = lax.broadcasted_iota(jnp.int32, (count, count), 1)
    before = ((row < column) & (row // HALF == column // HALF)).astype(jnp.bfloat16)
    lane = lax.broadcasted_iota(jnp.int32, (1, count), 1)
    slot = lax.broadcasted_iota(jnp.int32, (slots, count), 0)
    mine = pl.ds(pl.multiple_of(expert * count, count), count)
    for b in range(8):
        copies[b].wait()
    gates = jnp.concatenate(
        [blocks[b, 2 * count :, mine].astype(jnp.float32)[0:1] for b in range(8)], axis=0
    )
    picked = gates != 0.0
    earlier = mm(picked.astype(jnp.bfloat16), before).astype(jnp.int32)
    target = jnp.where(picked, (lane // HALF) * SLOTS + earlier, -1)
    for b in range(8):
        chosen = slot == target[b : b + 1]
        pick = chosen.astype(jnp.bfloat16)
        gate_pick = jnp.where(chosen, gates[b : b + 1], 0.0)
        gate = jnp.sum(gate_pick, axis=1, keepdims=True)
        at = b * slots
        pick_out[at : at + slots, :] = pick
        gate_out[at : at + slots, :] = gate_pick.astype(jnp.bfloat16)
        for j in range(4):
            columns = pl.ds(pl.multiple_of((me ^ j) * width, width), width)
            here = (slice(at, at + slots), slice(j * width, (j + 1) * width))
            rows_out[here] = mm(pick, blocks[b, 0:count, columns]).astype(jnp.bfloat16)
            cot = mm(pick, blocks[b, count : 2 * count, columns])
            cot_out[here] = cot.astype(jnp.bfloat16)
            upstream[here] = (gate * cot).astype(jnp.bfloat16)
    for copy in copies[8:]:
        copy.wait()
    pre_gate = mm(rows_out[...], w_gate[...])
    pre_up = mm(rows_out[...], w_up[...])
    logistic = jax.nn.sigmoid(pre_gate)
    act = pre_gate * logistic
    hidden_out[...] = (act * pre_up).astype(jnp.bfloat16)
    act_out[...] = act.astype(jnp.bfloat16)
    slope = logistic * (1.0 + pre_gate * (1.0 - logistic))
    slope_out[...] = (pre_up * slope).astype(jnp.bfloat16)
    outs = (keep_out, partner_out.at[0], cross_out, partner_out.at[1])
    for j in (2, 1, 3, 0):
        outs[j][...] = mm_rows(
            upstream[:, j * width : (j + 1) * width], hidden_out[...]
        ).astype(jnp.bfloat16)


def scatter(me, pick, own_out, other_out, column_block):
    width = own_out.shape[1] // 4
    slots = pick.shape[0] // 8
    count = pick.shape[1]
    for j in range(4):
        columns = pl.ds(pl.multiple_of((me ^ j) * width, width), width)
        block = column_block(j, columns).astype(jnp.bfloat16)
        for b in range(8):
            out = own_out if b % 2 == 0 else other_out
            at = b * slots
            out[(b // 2) * count : (b // 2 + 1) * count, columns] = mm_rows(
                pick[at : at + slots, :], block[at : at + slots]
            ).astype(jnp.bfloat16)


def output_kernel(place, *refs):
    gate_pick_in, hidden_in, down_weight, partner, cross, cross_partner = refs[0:6]
    own_out, other_out = refs[6:8]
    gate_pick, hidden, w_down, sems = refs[8:12]
    me = place[0]
    copies = bring(
        weight_pairs(me & 1, (down_weight, partner, cross, cross_partner), w_down)
        + [(gate_pick_in, gate_pick), (hidden_in, hidden)],
        sems,
    )
    for copy in copies:
        copy.wait()
    width = w_down.shape[0] // 4
    scatter(me, gate_pick, own_out, other_out, lambda j, _: (
        mm_last(hidden[...], w_down[j * width : (j + 1) * width])
    ))


def backward_kernel(place, *refs):
    (pick_in, gate_pick_in, rows_in, hidden_in, cot_in, act_in, slope_in, router_in,
     down_weight, partner, cross, cross_partner) = refs[0:12]
    d_gate_out, d_up_out, logit_out, router_out, keep_out, partner_out, cross_out = refs[12:19]
    pick, gate_pick, rows, hidden, cot, act, slope, router, w_down, sems = refs[19:29]
    me, expert = place[0], place[1]
    copies = bring(
        [(cot_in, cot)]
        + weight_pairs(me & 1, (down_weight, partner, cross, cross_partner), w_down)
        + [(gate_pick_in, gate_pick), (hidden_in, hidden), (rows_in, rows), (act_in, act),
           (slope_in, slope), (router_in, router)],
        sems,
    )
    for copy in copies:
        copy.wait()
    width = w_down.shape[0] // 4
    along = mm(cot[...], w_down[...])
    score = jnp.sum(hidden[...].astype(jnp.float32) * along, axis=1, keepdims=True)
    gate = jnp.sum(gate_pick[...].astype(jnp.float32), axis=1, keepdims=True)
    d_hidden = gate * along
    d_gate_out[...] = (d_hidden * slope[...].astype(jnp.float32)).astype(jnp.bfloat16)
    d_up_out[...] = (d_hidden * act[...].astype(jnp.float32)).astype(jnp.bfloat16)
    outs = (keep_out, partner_out.at[0], cross_out, partner_out.at[1])
    for j in range(4):
        part = rows[:, j * width : (j + 1) * width]
        outs[j][0] = mm_rows(part, d_gate_out[...]).astype(jnp.bfloat16)
        outs[j][1] = mm_rows(part, d_up_out[...]).astype(jnp.bfloat16)
    ids = router.shape[0]
    logits = jnp.zeros((pick_in.shape[0], ids), jnp.float32)
    for j in range(4):
        columns = pl.ds(pl.multiple_of((me ^ j) * width, width), width)
        logits += mm_last(
            rows[:, j * width : (j + 1) * width], router[:, columns].astype(jnp.bfloat16)
        )
    named = lax.broadcasted_iota(jnp.int32, (1, ids), 1) == expert
    share = jax.nn.sigmoid(jnp.sum(jnp.where(named, logits, 0.0), axis=1, keepdims=True))
    slope_grad = jnp.where(gate != 0.0, score * share * (1.0 - share), 0.0)
    logit_grad = jnp.broadcast_to(slope_grad, logit_out.shape).astype(jnp.bfloat16)
    logit_out[...] = logit_grad
    for j in range(4):
        columns = pl.ds(pl.multiple_of((me ^ j) * width, width), width)
        total = mm_rows(logit_grad, rows[:, j * width : (j + 1) * width])
        router_out[:, columns] = total[0 : router_out.shape[0]]


def back_kernel(place, *refs):
    (pick_in, d_gate_in, d_up_in, logit_in, router_in, gate_weight, up_weight, partner,
     cross, cross_partner) = refs[0:10]
    own_out, other_out = refs[10:12]
    pick, d_gate, d_up, logit_grad, router, w_gate, w_up, sems = refs[12:20]
    me, expert = place[0], place[1]
    core = me & 1
    copies = bring(
        [(pick_in, pick), (d_gate_in, d_gate), (d_up_in, d_up), (logit_in, logit_grad),
         (router_in, router)]
        + weight_pairs(core, (gate_weight, partner.at[0], cross.at[0], cross_partner.at[0]), w_gate)
        + weight_pairs(core, (up_weight, partner.at[1], cross.at[1], cross_partner.at[1]), w_up),
        sems,
    )
    for copy in copies:
        copy.wait()
    width = w_gate.shape[0] // 4
    slope_grad = logit_grad[:, 0:1].astype(jnp.float32)

    def column_block(j, columns):
        here = slice(j * width, (j + 1) * width)
        return (
            mm_last(d_gate[...], w_gate[here])
            + mm_last(d_up[...], w_up[here])
            + slope_grad * router[pl.ds(expert, 1), columns]
        )

    scatter(me, pick, own_out, other_out, column_block)


def dp_swap(value, step):
    return lax.ppermute(value, "dp", [(i, i ^ step) for i in range(4)])


def ring(value, step):
    size = lax.axis_size("expert")
    return lax.ppermute(value, "expert", [(i, (i + step) % size) for i in range(size)])


def after(value, *earlier):
    return lax.optimization_barrier((value, *earlier))[0]


def on_device_paired(
    tokens, routes, gate_weight, up_weight, down_weight, router, const_vec, const_gate, grad_out
):
    bf16, f32 = jnp.bfloat16, jnp.float32
    row_count, model_width = tokens.shape
    id_count = router.shape[1]
    const_count = const_vec.shape[0]
    expert_count = id_count - 2 - const_count
    stored_experts, stored_rows, hidden_width = gate_weight.shape
    me = lax.axis_index("dp")
    z = lax.axis_index("expert")
    core = me % 2
    expert = stored_experts * z + core
    place = jnp.stack([me, expert]).astype(jnp.int32)

    def of_expert(weight, which):
        return lax.dynamic_index_in_dim(weight, which, 0, keepdims=False)

    shape = jax.ShapeDtypeStruct
    vmem = pltpu.VMEM
    slot_count = 4 * row_count
    wide, narrow = (slot_count, model_width), (slot_count, hidden_width)
    table = (slot_count, row_count)
    weight_rows = (stored_rows, hidden_width)
    whole_weight = vmem((model_width, hidden_width), bf16)
    product = 2 * slot_count * model_width * hidden_width

    payload = pl.pallas_call(
        payload_kernel,
        out_shape=shape((2 * row_count + 16, model_width), bf16),
        cost_estimate=pl.CostEstimate(flops=0, bytes_accessed=2 << 20, transcendentals=0),
    )(tokens, grad_out, routes.T, router.T)
    near = ring(payload, 1)
    far_side = ring(payload, -1)
    mine_in = jnp.stack([of_expert(gate_weight, core), of_expert(up_weight, core)])
    theirs_in = jnp.stack([of_expert(gate_weight, 1 - core), of_expert(up_weight, 1 - core)])
    in_cross, in_cross_partner = dp_swap(mine_in, 2), dp_swap(theirs_in, 3)
    mine_down, theirs_down = of_expert(down_weight, core), of_expert(down_weight, 1 - core)
    in_partner = dp_swap(theirs_in, 1)
    down_partner = dp_swap(after(theirs_down, in_partner), 1)
    payload_partner = dp_swap(after(payload, down_partner), 1)
    far = ring(near, 1)
    near_partner = dp_swap(after(near, payload_partner), 1)
    far_side_partner = dp_swap(after(far_side, near_partner), 1)
    far_partner = dp_swap(far, 1)
    mine_down, theirs_down = lax.optimization_barrier(
        (mine_down, theirs_down, in_cross, in_cross_partner)
    )[0:2]
    down_cross, down_cross_partner = dp_swap(mine_down, 2), dp_swap(theirs_down, 3)
    payloads = [payload, payload_partner, near, near_partner, far, far_partner, far_side,
                far_side_partner]
    in_weights = [gate_weight, up_weight, in_partner, in_cross, in_cross_partner]
    router_rows = jnp.pad(router.T.astype(f32), ((0, 16 - id_count), (0, 0)))
    pick, gate_pick, rows, cot, hidden, act, slope, down_keep, down_theirs, down_sent = local_kernel(
        forward_kernel,
        place,
        [*payloads, *in_weights],
        [shape(table, bf16)] * 2 + [shape(wide, bf16)] * 2 + [shape(narrow, bf16)] * 3
        + [shape(weight_rows, bf16), shape((2, *weight_rows), bf16), shape(weight_rows, bf16)],
        [vmem((8, *payload.shape), bf16), whole_weight, whole_weight, vmem(wide, bf16),
         pltpu.SemaphoreType.DMA((16,))],
        3 * product,
    )
    down_cross, down_cross_partner, hidden = lax.optimization_barrier(
        (down_cross, down_cross_partner, hidden)
    )
    down_weights = [down_weight, down_partner, down_cross, down_cross_partner]
    mixed_own, mixed_other = local_kernel(
        output_kernel,
        place,
        [gate_pick, hidden, *down_weights],
        [shape(wide, bf16)] * 2,
        [vmem(table, bf16), vmem(narrow, bf16), whole_weight, pltpu.SemaphoreType.DMA((6,))],
        product,
    )
    d_gate, d_up, logit_grad, router_row, in_keep, in_theirs, in_sent = local_kernel(
        backward_kernel,
        place,
        [pick, gate_pick, rows, hidden, cot, act, slope, router_rows, *down_weights],
        [shape(narrow, bf16)] * 2 + [shape(table, bf16), shape((8, model_width), f32)]
        + [shape((2, *weight_rows), bf16), shape((2, 2, *weight_rows), bf16),
           shape((2, *weight_rows), bf16)],
        [vmem(table, bf16)] * 2 + [vmem(wide, bf16), vmem(narrow, bf16), vmem(wide, bf16),
         vmem(narrow, bf16), vmem(narrow, bf16), vmem(router_rows.shape, f32), whole_weight,
         pltpu.SemaphoreType.DMA((11,))],
        3 * product,
    )
    down_came = dp_swap(down_sent, 2)
    down_from = dp_swap(down_theirs, 1)
    down_came_partner = dp_swap(down_from[1], 2)
    in_came = dp_swap(in_sent, 2)
    down_came, down_came_partner, in_theirs, d_gate = lax.optimization_barrier(
        (down_came, down_came_partner, in_theirs, d_gate)
    )
    back_own, back_other = local_kernel(
        back_kernel,
        place,
        [pick, d_gate, d_up, logit_grad, router_rows, *in_weights],
        [shape(wide, bf16)] * 2,
        [vmem(table, bf16), vmem(narrow, bf16), vmem(narrow, bf16), vmem(table, bf16),
         vmem(router_rows.shape, f32), whole_weight, whole_weight,
         pltpu.SemaphoreType.DMA((13,))],
        2 * product,
    )

    def pair(mine, theirs):
        return jnp.where(
            core == 0, jnp.stack([mine, theirs], axis=-3), jnp.stack([theirs, mine], axis=-3)
        )

    def add(one, two):
        return one.astype(f32) + two.astype(f32)

    grad_down = pair(add(down_keep, down_came), add(down_from[0], down_came_partner)).astype(bf16)
    in_from = dp_swap(in_theirs, 1)
    in_came_partner = dp_swap(in_from[1], 2)

    def home(own, other):
        both = (own.astype(f32) + dp_swap(other, 1).astype(f32)).astype(bf16)
        slots = both.reshape(4, row_count, model_width)
        side = ring(slots[3], 1)
        near = (ring(slots[2], -1).astype(f32) + slots[1].astype(f32)).astype(bf16)
        return side, near, slots[0]

    mixed_parts = home(mixed_own, mixed_other)
    back_parts = home(back_own, back_other)
    in_came, in_came_partner = lax.optimization_barrier(
        (in_came, in_came_partner, back_parts[1])
    )[0:2]
    grad_in = pair(add(in_keep, in_came), add(in_from[0], in_came_partner)).astype(bf16)
    grad_gate, grad_up = grad_in[0], grad_in[1]
    mixed_sum = add(ring(mixed_parts[1], -1), mixed_parts[0]) + mixed_parts[2].astype(f32)
    back_sum = add(ring(back_parts[1], -1), back_parts[0]) + back_parts[2].astype(f32)

    id_range = lax.broadcasted_iota(jnp.int32, (1, 1, id_count), 2)
    named = jnp.any(routes[:, :, None] == id_range, axis=1)[:, expert_count:]
    share = jax.nn.sigmoid(mm(tokens, router[:, expert_count:]))
    gates = jnp.where(named, share, 0.0).astype(bf16).astype(f32)
    tokens_float = tokens.astype(f32)
    grad_float = grad_out.astype(f32)
    copy_weight = gates[:, 1]
    const_weight = gates[:, 2:]
    const_share = jax.nn.sigmoid(mm(tokens, const_gate))
    const_rest = (const_weight * (1.0 - const_share)).astype(bf16)
    coefficient = copy_weight + jnp.sum(const_weight * const_share, axis=1)
    mixed = (
        mixed_sum + coefficient[:, None] * tokens_float + mm(const_rest, const_vec)
    ).astype(bf16)
    along_token = jnp.sum(grad_float * tokens_float, axis=1, keepdims=True)
    along_const = mm_last(grad_out, const_vec)
    const_value = const_share * along_token + (1.0 - const_share) * along_const
    pick_grad = jnp.concatenate(
        [jnp.zeros_like(along_token), along_token, const_value], axis=1
    )
    null_grad = jnp.where(named, pick_grad * share * (1.0 - share), 0.0).astype(bf16)
    share_grad = (
        const_weight * (along_token - along_const) * const_share * (1.0 - const_share)
    ).astype(bf16)
    back_local = (
        coefficient[:, None] * grad_float
        + mm_last(null_grad, router[:, expert_count:])
        + mm_last(share_grad, const_gate)
    )
    grad_tokens = (back_sum + back_local).astype(bf16)

    small = jnp.concatenate(
        [
            mm_rows(jnp.concatenate([null_grad, share_grad], axis=1), tokens),
            mm_rows(const_rest, grad_out),
        ],
        axis=0,
    )
    experts = lax.broadcasted_iota(jnp.int32, (expert_count, 1), 0)
    routed = jnp.where(experts == expert, router_row[0:1], 0.0)
    small = jnp.concatenate([routed, small], axis=0)
    for step in (1, 2):
        small = small + dp_swap(small, step)
    for step in (1, 2):
        small = small + lax.ppermute(small, "expert", [(i, i ^ step) for i in range(4)])
    grad_router = small[:id_count].T
    grad_const_gate = small[id_count : id_count + const_count].T
    grad_const_vec = small[id_count + const_count :]
    return (
        mixed,
        grad_tokens,
        grad_gate,
        grad_up,
        grad_down,
        grad_router,
        grad_const_vec,
        grad_const_gate,
    )


def solution(mesh):
    paired = mesh.shape["rep"] == 1 and mesh.shape["dp"] == 4

    def on_device(tokens, routes, gate_weight, *others):
        id_count = others[2].shape[1]
        stored_experts, stored_rows, hidden_width = gate_weight.shape
        row_count, top_count = routes.shape
        halved = row_count * top_count == (row_count // 2) * id_count
        if paired and stored_experts == 2 and halved and row_count == 128:
            return on_device_paired(tokens, routes, gate_weight, *others)
        return on_device_general(tokens, routes, gate_weight, *others)

    placed = (
        P(("groups", "expert", "dp"), None),
        P(("groups", "expert", "dp"), None),
        P("expert", ("dp", "rep"), None),
        P("expert", ("dp", "rep"), None),
        P("expert", ("dp", "rep"), None),
        P(),
        P(),
        P(),
        P(("groups", "expert", "dp"), None),
    )
    return jax.shard_map(
        on_device,
        mesh=mesh,
        in_specs=placed,
        out_specs=(
            P(("groups", "expert", "dp"), None),
            P(("groups", "expert", "dp"), None),
            P(("groups", "expert"), ("dp", "rep"), None),
            P(("groups", "expert"), ("dp", "rep"), None),
            P(("groups", "expert"), ("dp", "rep"), None),
            P("groups", None),
            P("groups", None),
            P("groups", None),
        ),
        check_vma=False,
    )
```

```python
import jax
import jax.numpy as jnp
from jax import lax
from jax.experimental import pallas as pl
from jax.experimental.pallas import tpu as pltpu
from jax.sharding import PartitionSpec as P

ROWS_CONTRACT = (((0,), (0,)), ((), ()))
LAST_CONTRACT = (((1,), (1,)), ((), ()))


def silu_slope(argument):
    logistic = jax.nn.sigmoid(argument)
    return logistic * (1.0 + argument * (1.0 - logistic))


def expert_forward(token_rows, w_gate, w_up, w_down):
    pre_gate = jnp.dot(token_rows, w_gate, preferred_element_type=jnp.float32)
    pre_up = jnp.dot(token_rows, w_up, preferred_element_type=jnp.float32)
    hidden = (jax.nn.silu(pre_gate) * pre_up).astype(jnp.bfloat16)
    output_rows = lax.dot_general(hidden, w_down, LAST_CONTRACT, preferred_element_type=jnp.float32)
    return (output_rows.astype(jnp.bfloat16), hidden, pre_gate, pre_up)


def expert_backward(pre_gate, pre_up, upstream, w_gate, w_up, w_down):
    d_hidden = jnp.dot(upstream, w_down, preferred_element_type=jnp.float32)
    d_gate = (d_hidden * pre_up * silu_slope(pre_gate)).astype(jnp.bfloat16)
    d_up = (d_hidden * jax.nn.silu(pre_gate)).astype(jnp.bfloat16)
    back_rows = lax.dot_general(d_gate, w_gate, LAST_CONTRACT, preferred_element_type=jnp.float32)
    back_rows = back_rows + lax.dot_general(
        d_up, w_up, LAST_CONTRACT, preferred_element_type=jnp.float32
    )
    return (back_rows.astype(jnp.bfloat16), d_gate, d_up)


def block_terms(token_rows, hidden, upstream, d_gate, d_up):
    term_gate = lax.dot_general(
        token_rows, d_gate, ROWS_CONTRACT, preferred_element_type=jnp.float32
    )
    term_up = lax.dot_general(token_rows, d_up, ROWS_CONTRACT, preferred_element_type=jnp.float32)
    term_down = lax.dot_general(upstream, hidden, ROWS_CONTRACT, preferred_element_type=jnp.float32)
    return (term_gate, term_up, term_down)


def token_trip(buffer):
    return lax.all_to_all(buffer, ("expert", "dp"), split_axis=0, concat_axis=0, tiled=True)


def on_device_general(
    tokens, routes, gate_weight, up_weight, down_weight, router, const_vec, const_gate, grad_out
):
    shard_rows, top_count = routes.shape
    row_count = shard_rows // lax.axis_size("rep")
    first_row = lax.axis_index("rep") * row_count
    tokens = lax.dynamic_slice_in_dim(tokens, first_row, row_count, 0)
    routes = lax.dynamic_slice_in_dim(routes, first_row, row_count, 0)
    grad_out = lax.dynamic_slice_in_dim(grad_out, first_row, row_count, 0)
    model_width = tokens.shape[1]
    id_count = router.shape[1]
    const_count = const_vec.shape[0]
    expert_count = id_count - 2 - const_count
    half_rows = row_count // 2
    capacity = (half_rows * top_count + id_count - 1) // id_count
    target_count = lax.axis_size("expert") * lax.axis_size("dp")
    slot_count = target_count * capacity
    stored_experts, stored_rows, hidden_width = gate_weight.shape
    spread = lax.axis_size("dp") * lax.axis_size("rep")
    id_range = lax.broadcasted_iota(jnp.int32, (1, 1, id_count), 2)
    picks = routes[:, :, None] == id_range
    named = jnp.sum(picks.astype(jnp.float32), axis=1)
    row_index = lax.broadcasted_iota(jnp.int32, (row_count, row_count), 0)
    column_index = lax.broadcasted_iota(jnp.int32, (row_count, row_count), 1)
    before = (
        (column_index < row_index) & (column_index // half_rows == row_index // half_rows)
    ).astype(jnp.float32)
    earlier = jnp.dot(before, named, precision=lax.Precision.HIGHEST)
    slot = jnp.sum(jnp.where(picks, earlier[:, None, :], 0.0), axis=2).astype(jnp.int32)
    member = lax.broadcasted_iota(jnp.int32, (row_count, top_count), 0) // half_rows
    routed = routes < expert_count
    target = jnp.where(routed, (2 * routes + member) * capacity + slot, slot_count)
    slot_range = lax.broadcasted_iota(jnp.int32, (slot_count, 1), 0)
    pair_range = lax.broadcasted_iota(jnp.int32, (1, row_count * top_count), 1)
    hits = slot_range == target.reshape(1, -1)
    owner = jnp.sum(jnp.where(hits, pair_range, 0), axis=1)
    filled = jnp.any(hits, axis=1)
    owner_token = owner // top_count
    target_safe = jnp.where(routed, target, 0)
    logits = jnp.dot(tokens, router, preferred_element_type=jnp.float32)
    chosen = jnp.sum(jnp.where(picks, jax.nn.sigmoid(logits)[:, None, :], 0.0), axis=2)
    gates = chosen.astype(jnp.bfloat16)
    gates_float = gates.astype(jnp.float32)
    slot_gate = jnp.where(filled, gates.reshape(-1)[owner], jnp.zeros((), jnp.bfloat16)).astype(
        jnp.float32
    )
    repeat = spread // stored_experts
    fetched = (
        lax.all_to_all(
            jnp.repeat(gate_weight, repeat, axis=0),
            ("dp", "rep"),
            split_axis=0,
            concat_axis=1,
            tiled=True,
        ),
        lax.all_to_all(
            jnp.repeat(up_weight, repeat, axis=0),
            ("dp", "rep"),
            split_axis=0,
            concat_axis=1,
            tiled=True,
        ),
        lax.all_to_all(
            jnp.repeat(down_weight, repeat, axis=0),
            ("dp", "rep"),
            split_axis=0,
            concat_axis=1,
            tiled=True,
        ),
    )
    w_gate = fetched[0].reshape(model_width, hidden_width)
    w_up = fetched[1].reshape(model_width, hidden_width)
    w_down = fetched[2].reshape(model_width, hidden_width)
    send_rows = jnp.where(filled[:, None], tokens[owner_token], jnp.zeros((), jnp.bfloat16))
    arrived = token_trip(send_rows.reshape(target_count, capacity, model_width)).reshape(
        slot_count, model_width
    )
    output_rows, hidden, pre_gate, pre_up = expert_forward(arrived, w_gate, w_up, w_down)
    returned = token_trip(output_rows.reshape(target_count, capacity, model_width)).reshape(
        slot_count, model_width
    )
    picked_out = returned[target_safe].astype(jnp.float32)
    mixed_sum = jnp.sum(
        jnp.where(routed[:, :, None], gates_float[:, :, None] * picked_out, 0.0), axis=1
    )
    cotangent_all = grad_out.astype(jnp.float32)
    routed_grad = jnp.sum(
        jnp.where(routed[:, :, None], picked_out * cotangent_all[:, None, :], 0.0), axis=2
    )
    upstream_send = (slot_gate[:, None] * grad_out[owner_token].astype(jnp.float32)).astype(
        jnp.bfloat16
    )
    upstream = token_trip(upstream_send.reshape(target_count, capacity, model_width)).reshape(
        slot_count, model_width
    )
    back_rows, d_gate, d_up = expert_backward(pre_gate, pre_up, upstream, w_gate, w_up, w_down)
    terms = block_terms(arrived, hidden, upstream, d_gate, d_up)
    sent_terms = tuple(
        (term.astype(jnp.bfloat16).reshape(spread, stored_rows, hidden_width) for term in terms)
    )
    gathered_terms = (
        lax.all_to_all(sent_terms[0], ("dp", "rep"), split_axis=0, concat_axis=0, tiled=True),
        lax.all_to_all(sent_terms[1], ("dp", "rep"), split_axis=0, concat_axis=0, tiled=True),
        lax.all_to_all(sent_terms[2], ("dp", "rep"), split_axis=0, concat_axis=0, tiled=True),
    )
    copies = spread // stored_experts
    grad_gate, grad_up, grad_down = (
        jnp.sum(
            arrived_term.reshape(stored_experts, copies, stored_rows, hidden_width),
            axis=1,
            dtype=jnp.float32,
        ).astype(jnp.bfloat16)
        for arrived_term in gathered_terms
    )
    returned_back = token_trip(back_rows.reshape(target_count, capacity, model_width)).reshape(
        slot_count, model_width
    )
    back_sum = jnp.sum(
        jnp.where(routed[:, :, None], returned_back[target_safe].astype(jnp.float32), 0.0), axis=1
    )
    is_copy = routes == expert_count + 1
    const_ids = expert_count + 2 + lax.broadcasted_iota(jnp.int32, (1, 1, const_count), 2)
    is_const = routes[:, :, None] == const_ids
    copy_weight = jnp.sum(jnp.where(is_copy, gates_float, 0.0), axis=1)
    const_weight = jnp.sum(jnp.where(is_const, gates_float[:, :, None], 0.0), axis=1)
    const_share = jax.nn.sigmoid(jnp.dot(tokens, const_gate, preferred_element_type=jnp.float32))
    const_rest = (const_weight * (1.0 - const_share)).astype(jnp.bfloat16)
    coefficient = copy_weight + jnp.sum(const_weight * const_share, axis=1)
    tokens_float = tokens.astype(jnp.float32)
    constant_term = jnp.dot(const_rest, const_vec, preferred_element_type=jnp.float32)
    mixed = (mixed_sum + coefficient[:, None] * tokens_float + constant_term).astype(jnp.bfloat16)
    along_token = jnp.sum(cotangent_all * tokens_float, axis=1)
    along_const = lax.dot_general(
        grad_out, const_vec, LAST_CONTRACT, preferred_element_type=jnp.float32
    )
    const_value = const_share * along_token[:, None] + (1.0 - const_share) * along_const
    null_grad = jnp.where(is_copy, along_token[:, None], 0.0) + jnp.sum(
        jnp.where(is_const, const_value[:, None, :], 0.0), axis=2
    )
    pick_grad = routed_grad + null_grad
    slope_grad = pick_grad * chosen * (1.0 - chosen)
    logit_grad = jnp.sum(jnp.where(picks, slope_grad[:, :, None], 0.0), axis=1).astype(jnp.bfloat16)
    share_grad = (
        const_weight * (along_token[:, None] - along_const) * const_share * (1.0 - const_share)
    ).astype(jnp.bfloat16)
    back_local = coefficient[:, None] * cotangent_all
    back_local = back_local + lax.dot_general(
        logit_grad, router, LAST_CONTRACT, preferred_element_type=jnp.float32
    )
    back_local = back_local + lax.dot_general(
        share_grad, const_gate, LAST_CONTRACT, preferred_element_type=jnp.float32
    )
    grad_tokens = (back_sum + back_local).astype(jnp.bfloat16)
    router_part = lax.dot_general(
        tokens, logit_grad, ROWS_CONTRACT, preferred_element_type=jnp.float32
    )
    vector_part = lax.dot_general(
        const_rest, grad_out, ROWS_CONTRACT, preferred_element_type=jnp.float32
    )
    mixing_part = lax.dot_general(
        tokens, share_grad, ROWS_CONTRACT, preferred_element_type=jnp.float32
    )
    grad_router, grad_const_vec, grad_const_gate = lax.psum(
        (router_part, vector_part, mixing_part), ("expert", "dp", "rep")
    )
    mixed_all, grad_tokens_all = (
        lax.all_gather(mixed, "rep", axis=0, tiled=True),
        lax.all_gather(grad_tokens, "rep", axis=0, tiled=True),
    )
    return (
        mixed_all,
        grad_tokens_all,
        grad_gate,
        grad_up,
        grad_down,
        grad_router,
        grad_const_vec,
        grad_const_gate,
    )


HALF = 64
SLOTS = 32
SCRATCH_BYTES = 22 * 1024 * 1024
LONG = 20_000_000_000


def local_kernel(body, scalars, operands, outputs, scratch, moved):
    return pl.pallas_call(
        body,
        out_shape=outputs,
        in_specs=[pl.BlockSpec(memory_space=pltpu.SMEM)]
        + [pl.BlockSpec(memory_space=pl.ANY) for _ in operands],
        out_specs=[pl.BlockSpec(memory_space=pltpu.VMEM) for _ in outputs],
        scratch_shapes=scratch,
        compiler_params=pltpu.CompilerParams(vmem_limit_bytes=SCRATCH_BYTES),
        cost_estimate=pl.CostEstimate(flops=moved, bytes_accessed=moved, transcendentals=0),
    )(scalars, *operands)


def bring(pairs, sems):
    copies = [
        pltpu.make_async_copy(source, target, sems.at[i])
        for i, (source, target) in enumerate(pairs)
    ]
    for copy in copies:
        copy.start()
    return copies


def mm(a, b):
    return jnp.dot(a, b, preferred_element_type=jnp.float32)


def mm_rows(a, b):
    return lax.dot_general(a, b, ROWS_CONTRACT, preferred_element_type=jnp.float32)


def mm_last(a, b):
    return lax.dot_general(a, b, LAST_CONTRACT, preferred_element_type=jnp.float32)


def weight_pairs(core, parts, target):
    stored, *fetched = parts
    width = target.shape[0] // 4
    sources = [stored.at[core], *fetched]
    return [(s, target.at[pl.ds(j * width, width)]) for j, s in enumerate(sources)]


def payload_kernel(tokens, grads, routes, router, out, step):
    step[...] = jnp.zeros_like(step)
    count = tokens.shape[0]
    ids = lax.broadcasted_iota(jnp.int32, (router.shape[0], count), 0)
    named = routes[0:1, :] == ids
    for k in range(1, routes.shape[0]):
        named = named | (routes[k : k + 1, :] == ids)
    gates = jnp.where(named, jax.nn.sigmoid(mm_last(router[...], tokens[...])), 0.0)
    out[0:count, :] = tokens[...]
    out[count : 2 * count, :] = grads[...]
    for e in range(out.shape[1] // count):
        out[2 * count :, e * count : (e + 1) * count] = jnp.broadcast_to(
            gates[e : e + 1], (16, count)
        ).astype(jnp.bfloat16)


def step_kernel(before, after_it):
    after_it[...] = before[...] + 1.0


def next_step(step, *done):
    return pl.pallas_call(
        step_kernel,
        out_shape=jax.ShapeDtypeStruct(step.shape, step.dtype),
        cost_estimate=pl.CostEstimate(flops=LONG, bytes_accessed=LONG, transcendentals=0),
    )(after(step, *done))


def pick_kernel(place, *refs):
    payloads = refs[0:8]
    pick_out, gate_out, rows_out, cot_out = refs[8:12]
    blocks, sems = refs[12:14]
    me, expert = place[0], place[1]
    count = pick_out.shape[1]
    slots = count // HALF * SLOTS
    copies = bring([(payloads[b], blocks.at[b]) for b in range(8)], sems)
    width = rows_out.shape[1] // 4
    row = lax.broadcasted_iota(jnp.int32, (count, count), 0)
    column = lax.broadcasted_iota(jnp.int32, (count, count), 1)
    before = ((row < column) & (row // HALF == column // HALF)).astype(jnp.bfloat16)
    lane = lax.broadcasted_iota(jnp.int32, (1, count), 1)
    slot = lax.broadcasted_iota(jnp.int32, (slots, count), 0)
    mine = pl.ds(pl.multiple_of(expert * count, count), count)
    for copy in copies:
        copy.wait()
    gates = jnp.concatenate(
        [blocks[b, 2 * count :, mine].astype(jnp.float32)[0:1] for b in range(8)], axis=0
    )
    picked = gates != 0.0
    earlier = mm(picked.astype(jnp.bfloat16), before).astype(jnp.int32)
    target = jnp.where(picked, (lane // HALF) * SLOTS + earlier, -1)
    for b in range(8):
        chosen = slot == target[b : b + 1]
        pick = chosen.astype(jnp.bfloat16)
        at = b * slots
        pick_out[at : at + slots, :] = pick
        gate_out[at : at + slots, :] = jnp.where(chosen, gates[b : b + 1], 0.0).astype(jnp.bfloat16)
        for j in range(4):
            columns = pl.ds(pl.multiple_of((me ^ j) * width, width), width)
            here = (slice(at, at + slots), slice(j * width, (j + 1) * width))
            rows_out[here] = mm(pick, blocks[b, 0:count, columns]).astype(jnp.bfloat16)
            cot_out[here] = mm(pick, blocks[b, count : 2 * count, columns]).astype(jnp.bfloat16)


def forward_kernel(place, *refs):
    (gate_pick_in, rows_in, cot_in, gate_weight, up_weight, partner, cross,
     cross_partner) = refs[0:8]
    hidden_out, act_out, slope_out = refs[8:11]
    outs = refs[11:15]
    gate_pick, rows, cot, w_gate, w_up, upstream, sems = refs[15:22]
    core = place[0] & 1
    copies = bring(
        [(rows_in, rows)]
        + weight_pairs(core, (gate_weight, partner.at[0], cross.at[0, core], cross_partner.at[0]), w_gate)
        + weight_pairs(core, (up_weight, partner.at[1], cross.at[1, core], cross_partner.at[1]), w_up)
        + [(gate_pick_in, gate_pick), (cot_in, cot)],
        sems,
    )
    width = w_gate.shape[0] // 4
    for copy in copies[0:5]:
        copy.wait()
    pre_gate = mm(rows[...], w_gate[...])
    for copy in copies[5:9]:
        copy.wait()
    pre_up = mm(rows[...], w_up[...])
    logistic = jax.nn.sigmoid(pre_gate)
    act = pre_gate * logistic
    hidden_out[...] = (act * pre_up).astype(jnp.bfloat16)
    act_out[...] = act.astype(jnp.bfloat16)
    slope = logistic * (1.0 + pre_gate * (1.0 - logistic))
    slope_out[...] = (pre_up * slope).astype(jnp.bfloat16)
    for copy in copies[9:]:
        copy.wait()
    gate = jnp.sum(gate_pick[...].astype(jnp.float32), axis=1, keepdims=True)
    for j in range(4):
        here = slice(j * width, (j + 1) * width)
        upstream[:, here] = (gate * cot[:, here].astype(jnp.float32)).astype(jnp.bfloat16)
        outs[j][...] = mm_rows(upstream[:, here], hidden_out[...]).astype(jnp.bfloat16)


def scatter(me, pick, own_out, other_out, column_block):
    width = own_out.shape[1] // 4
    slots = pick.shape[0] // 8
    count = pick.shape[1]
    for j in range(4):
        columns = pl.ds(pl.multiple_of((me ^ j) * width, width), width)
        block = column_block(j, columns).astype(jnp.bfloat16)
        for b in range(8):
            out = own_out if b % 2 == 0 else other_out
            at = b * slots
            out[(b // 2) * count : (b // 2 + 1) * count, columns] = mm_rows(
                pick[at : at + slots, :], block[at : at + slots]
            ).astype(jnp.bfloat16)


def output_kernel(place, *refs):
    gate_pick_in, hidden_in, down_weight, partner, cross, cross_partner = refs[0:6]
    own_out, other_out = refs[6:8]
    gate_pick, hidden, w_down, sems = refs[8:12]
    me = place[0]
    copies = bring(
        weight_pairs(me & 1, (down_weight, partner, cross.at[me & 1], cross_partner), w_down)
        + [(gate_pick_in, gate_pick), (hidden_in, hidden)],
        sems,
    )
    for copy in copies:
        copy.wait()
    width = w_down.shape[0] // 4
    scatter(me, gate_pick, own_out, other_out, lambda j, _: (
        mm_last(hidden[...], w_down[j * width : (j + 1) * width])
    ))


def backward_kernel(place, *refs):
    (pick_in, gate_pick_in, rows_in, hidden_in, cot_in, act_in, slope_in, router_in,
     down_weight, partner, cross, cross_partner) = refs[0:12]
    (d_gate_out, d_up_out, logit_out, router_out, keep_out, partner_out, cross_partner_out,
     gate_sent, up_sent) = refs[12:21]
    pick, gate_pick, rows, hidden, cot, act, slope, router, w_down, sems = refs[21:31]
    me, expert = place[0], place[1]
    copies = bring(
        [(cot_in, cot)]
        + weight_pairs(me & 1, (down_weight, partner, cross.at[me & 1], cross_partner), w_down)
        + [(gate_pick_in, gate_pick), (hidden_in, hidden), (rows_in, rows), (act_in, act),
           (slope_in, slope), (router_in, router)],
        sems,
    )
    for copy in copies:
        copy.wait()
    width = w_down.shape[0] // 4
    along = mm(cot[...], w_down[...])
    score = jnp.sum(hidden[...].astype(jnp.float32) * along, axis=1, keepdims=True)
    gate = jnp.sum(gate_pick[...].astype(jnp.float32), axis=1, keepdims=True)
    d_hidden = gate * along
    d_gate_out[...] = (d_hidden * slope[...].astype(jnp.float32)).astype(jnp.bfloat16)
    d_up_out[...] = (d_hidden * act[...].astype(jnp.float32)).astype(jnp.bfloat16)
    gate_outs = (keep_out.at[0], partner_out.at[0], gate_sent, cross_partner_out.at[0])
    up_outs = (keep_out.at[1], partner_out.at[1], up_sent, cross_partner_out.at[1])
    for j in range(4):
        part = rows[:, j * width : (j + 1) * width]
        gate_outs[j][...] = mm_rows(part, d_gate_out[...]).astype(jnp.bfloat16)
        up_outs[j][...] = mm_rows(part, d_up_out[...]).astype(jnp.bfloat16)
    ids = router.shape[0]
    logits = jnp.zeros((pick_in.shape[0], ids), jnp.float32)
    for j in range(4):
        columns = pl.ds(pl.multiple_of((me ^ j) * width, width), width)
        logits += mm_last(
            rows[:, j * width : (j + 1) * width], router[:, columns].astype(jnp.bfloat16)
        )
    named = lax.broadcasted_iota(jnp.int32, (1, ids), 1) == expert
    share = jax.nn.sigmoid(jnp.sum(jnp.where(named, logits, 0.0), axis=1, keepdims=True))
    slope_grad = jnp.where(gate != 0.0, score * share * (1.0 - share), 0.0)
    logit_grad = jnp.broadcast_to(slope_grad, logit_out.shape).astype(jnp.bfloat16)
    logit_out[...] = logit_grad
    for j in range(4):
        columns = pl.ds(pl.multiple_of((me ^ j) * width, width), width)
        total = mm_rows(logit_grad, rows[:, j * width : (j + 1) * width])
        router_out[:, columns] = total[0 : router_out.shape[0]]


def back_kernel(place, *refs):
    (pick_in, d_gate_in, d_up_in, logit_in, router_in, gate_weight, up_weight, partner,
     cross, cross_partner) = refs[0:10]
    own_out, other_out = refs[10:12]
    pick, d_gate, d_up, logit_grad, router, w_gate, w_up, sems = refs[12:20]
    me, expert = place[0], place[1]
    core = me & 1
    copies = bring(
        [(pick_in, pick), (d_gate_in, d_gate), (d_up_in, d_up), (logit_in, logit_grad),
         (router_in, router)]
        + weight_pairs(core, (gate_weight, partner.at[0], cross.at[0, core], cross_partner.at[0]), w_gate)
        + weight_pairs(core, (up_weight, partner.at[1], cross.at[1, core], cross_partner.at[1]), w_up),
        sems,
    )
    for copy in copies:
        copy.wait()
    width = w_gate.shape[0] // 4
    slope_grad = logit_grad[:, 0:1].astype(jnp.float32)

    def column_block(j, columns):
        here = slice(j * width, (j + 1) * width)
        return (
            mm_last(d_gate[...], w_gate[here])
            + mm_last(d_up[...], w_up[here])
            + slope_grad * router[pl.ds(expert, 1), columns]
        )

    scatter(me, pick, own_out, other_out, column_block)


def dp_swap(value, step):
    return lax.ppermute(value, "dp", [(i, i ^ step) for i in range(4)])


def ring(value, step):
    size = lax.axis_size("expert")
    return lax.ppermute(value, "expert", [(i, (i + step) % size) for i in range(size)])


def after(value, *earlier):
    return lax.optimization_barrier((value, *earlier))[0]


def on_device_paired(
    tokens, routes, gate_weight, up_weight, down_weight, router, const_vec, const_gate, grad_out
):
    bf16, f32 = jnp.bfloat16, jnp.float32
    row_count, model_width = tokens.shape
    id_count = router.shape[1]
    const_count = const_vec.shape[0]
    expert_count = id_count - 2 - const_count
    stored_experts, stored_rows, hidden_width = gate_weight.shape
    me = lax.axis_index("dp")
    z = lax.axis_index("expert")
    core = me % 2
    expert = stored_experts * z + core
    place = jnp.stack([me, expert]).astype(jnp.int32)

    def of_expert(weight, which):
        return lax.dynamic_index_in_dim(weight, which, 0, keepdims=False)

    shape = jax.ShapeDtypeStruct
    vmem = pltpu.VMEM
    slot_count = 4 * row_count
    wide, narrow = (slot_count, model_width), (slot_count, hidden_width)
    table = (slot_count, row_count)
    weight_rows = (stored_rows, hidden_width)
    whole_weight = vmem((model_width, hidden_width), bf16)

    def together(*values):
        return lax.optimization_barrier(values)

    payload, step = pl.pallas_call(
        payload_kernel,
        out_shape=[shape((2 * row_count + 16, model_width), bf16), shape((8, 128), f32)],
        cost_estimate=pl.CostEstimate(flops=LONG, bytes_accessed=LONG, transcendentals=0),
    )(tokens, grad_out, routes.T, router.T)
    near, far_side = ring(payload, 1), ring(payload, -1)
    payload_partner = dp_swap(payload, 1)
    in_cross = dp_swap(jnp.stack([gate_weight, up_weight]), 2)
    down_cross = dp_swap(after(down_weight, payload_partner), 2)
    step = next_step(step, payload)
    near, step = together(near, step)
    far = ring(near, 1)
    partner = dp_swap(
        after(
            jnp.stack([of_expert(w, 1 - core) for w in (gate_weight, up_weight, down_weight)]),
            payload_partner,
        ),
        1,
    )
    step = next_step(step, near, partner)
    far_side, far, in_cross, near = together(far_side, far, in_cross, near, step)[0:4]
    near_partner = dp_swap(near, 1)
    far_side_partner = dp_swap(far_side, 1)
    theirs_cross = lax.dynamic_index_in_dim(in_cross, 1 - core, 1, keepdims=False)
    in_cross_partner = dp_swap(theirs_cross, 1)
    far_partner = dp_swap(far, 1)
    payloads = [payload, payload_partner, near, near_partner, far, far_partner, far_side,
                far_side_partner]
    in_weights = [gate_weight, up_weight, partner, in_cross, in_cross_partner]
    router_rows = jnp.pad(router.T.astype(f32), ((0, 16 - id_count), (0, 0)))
    pick, gate_pick, rows, cot = local_kernel(
        pick_kernel,
        place,
        payloads,
        [shape(table, bf16)] * 2 + [shape(wide, bf16)] * 2,
        [vmem((8, *payload.shape), bf16), pltpu.SemaphoreType.DMA((8,))],
        0,
    )
    rows, down_cross = together(rows, down_cross)
    down_cross_partner = dp_swap(of_expert(down_cross, 1 - core), 1)
    hidden, act, slope, *down_parts = local_kernel(
        forward_kernel,
        place,
        [gate_pick, rows, cot, *in_weights],
        [shape(narrow, bf16)] * 3 + [shape(weight_rows, bf16)] * 4,
        [vmem(table, bf16), vmem(wide, bf16), vmem(wide, bf16), whole_weight, whole_weight,
         vmem(wide, bf16), pltpu.SemaphoreType.DMA((11,))],
        LONG,
    )
    hidden, down_cross_partner = together(hidden, down_cross_partner)
    down_weights = [down_weight, partner[2], down_cross, down_cross_partner]
    def add(one, two):
        return one.astype(f32) + two.astype(f32)

    def sum_slots(own, came):
        return [
            add(mine, theirs).astype(bf16) for mine, theirs in zip(jnp.split(own, 2), came)
        ]

    def pair(mine, theirs):
        of = lax.broadcasted_iota(jnp.int32, (2, 1, 1), 0)
        return jnp.where(of == core, mine[None], theirs[None]).astype(bf16)

    id_range = lax.broadcasted_iota(jnp.int32, (1, 1, id_count), 2)
    named = jnp.any(routes[:, :, None] == id_range, axis=1)[:, expert_count:]
    share = jax.nn.sigmoid(mm(tokens, router[:, expert_count:]))
    gates = jnp.where(named, share, 0.0).astype(bf16).astype(f32)
    tokens_float = tokens.astype(f32)
    grad_float = grad_out.astype(f32)
    copy_weight = gates[:, 1]
    const_weight = gates[:, 2:]
    const_share = jax.nn.sigmoid(mm(tokens, const_gate))
    const_rest = (const_weight * (1.0 - const_share)).astype(bf16)
    coefficient = copy_weight + jnp.sum(const_weight * const_share, axis=1)
    along_token = jnp.sum(grad_float * tokens_float, axis=1, keepdims=True)
    along_const = mm_last(grad_out, const_vec)
    const_value = const_share * along_token + (1.0 - const_share) * along_const
    pick_grad = jnp.concatenate(
        [jnp.zeros_like(along_token), along_token, const_value], axis=1
    )
    null_grad = jnp.where(named, pick_grad * share * (1.0 - share), 0.0).astype(bf16)
    share_grad = (
        const_weight * (along_token - along_const) * const_share * (1.0 - const_share)
    ).astype(bf16)
    mixed_own, mixed_other = local_kernel(
        output_kernel,
        place,
        [gate_pick, hidden, *down_weights],
        [shape(wide, bf16)] * 2,
        [vmem(table, bf16), vmem(narrow, bf16), whole_weight, pltpu.SemaphoreType.DMA((6,))],
        LONG,
    )
    down_came, down_came_partner = dp_swap(down_parts[2], 2), dp_swap(down_parts[3], 3)
    parts = [mixed_other[k * row_count : (k + 1) * row_count] for k in range(4)]
    mixed_came = [dp_swap(parts[2], 1), dp_swap(parts[3], 1)]
    mixed_own, mixed_came[0], mixed_came[1], down_came, cot = together(
        mixed_own, *mixed_came, down_came, cot
    )
    mixed_first = sum_slots(mixed_own[2 * row_count :], mixed_came)
    mixed_near = ring(mixed_first[0], -1)
    mixed_late = dp_swap(mixed_other[: 2 * row_count], 1)
    down_from = dp_swap(down_parts[1], 1)
    d_gate, d_up, logit_grad, router_row, *in_parts, gate_sent, up_sent = local_kernel(
        backward_kernel,
        place,
        [pick, gate_pick, rows, hidden, cot, act, slope, router_rows, *down_weights],
        [shape(narrow, bf16)] * 2 + [shape(table, bf16), shape((8, model_width), f32)]
        + [shape((2, *weight_rows), bf16)] * 3 + [shape(weight_rows, bf16)] * 2,
        [vmem(table, bf16)] * 2 + [vmem(wide, bf16), vmem(narrow, bf16), vmem(wide, bf16),
         vmem(narrow, bf16), vmem(narrow, bf16), vmem(router_rows.shape, f32), whole_weight,
         pltpu.SemaphoreType.DMA((11,))],
        LONG,
    )
    (d_gate, router_row, in_parts[1], in_parts[2], gate_sent, up_sent, down_came_partner,
     mixed_near, mixed_late, down_from) = together(
        d_gate, router_row, in_parts[1], in_parts[2], gate_sent, up_sent, down_came_partner,
        mixed_near, mixed_late, down_from
    )
    mixed_late = sum_slots(mixed_own[: 2 * row_count], jnp.split(mixed_late, 2))
    small = jnp.concatenate(
        [
            mm_rows(jnp.concatenate([null_grad, share_grad], axis=1), tokens),
            mm_rows(const_rest, grad_out),
        ],
        axis=0,
    )
    experts = lax.broadcasted_iota(jnp.int32, (expert_count, 1), 0)
    routed = jnp.where(experts == expert, router_row[0:1], 0.0)
    small = jnp.concatenate([routed, small], axis=0)
    gate_came, in_from, small_came = dp_swap(gate_sent, 2), dp_swap(in_parts[1], 1), dp_swap(small, 2)
    mixed_side = ring(mixed_first[1].astype(bf16), 1)
    mixed_near = ring(add(mixed_near, mixed_late[1]).astype(bf16), -1)
    back_own, back_other = local_kernel(
        back_kernel,
        place,
        [pick, d_gate, d_up, logit_grad, router_rows, *in_weights],
        [shape(wide, bf16)] * 2,
        [vmem(table, bf16), vmem(narrow, bf16), vmem(narrow, bf16), vmem(table, bf16),
         vmem(router_rows.shape, f32), whole_weight, whole_weight,
         pltpu.SemaphoreType.DMA((13,))],
        LONG,
    )
    (back_own, back_other, gate_came, in_from, small_came, mixed_side, mixed_near, up_sent,
     in_parts[2]) = together(
        back_own, back_other, gate_came, in_from, small_came, mixed_side, mixed_near, up_sent,
        in_parts[2]
    )
    up_came, in_came_partner = dp_swap(up_sent, 2), dp_swap(in_parts[2], 3)
    small = small + small_came
    back_came, small_came = together(dp_swap(back_other, 1), dp_swap(small, 1))
    step = next_step(step, back_came, small_came)
    back_own, back_came, small_came = together(back_own, back_came, small_came, step)[0:3]
    back_late = sum_slots(back_own[: 2 * row_count], jnp.split(back_came[: 2 * row_count], 2))
    back_first = sum_slots(back_own[2 * row_count :], jnp.split(back_came[2 * row_count :], 2))
    back_near, back_side = ring(back_first[0], -1), ring(back_first[1], 1)
    small = small + small_came
    small_came = lax.ppermute(small, "expert", [(i, i ^ 1) for i in range(4)])
    back_near, back_side, up_came = together(back_near, back_side, up_came)
    back_near = ring(add(back_near, back_late[1]).astype(bf16), -1)
    small = small + small_came
    small = small + lax.ppermute(small, "expert", [(i, i ^ 2) for i in range(4)])
    mixed_sum = add(mixed_side, mixed_near) + mixed_late[0].astype(f32)
    back_sum = add(back_side, back_near) + back_late[0].astype(f32)
    grad_down = pair(add(down_parts[0], down_came), add(down_from, down_came_partner))
    mixed = (
        mixed_sum + coefficient[:, None] * tokens_float + mm(const_rest, const_vec)
    ).astype(bf16)
    back_local = (
        coefficient[:, None] * grad_float
        + mm_last(null_grad, router[:, expert_count:])
        + mm_last(share_grad, const_gate)
    )
    grad_tokens = (back_sum + back_local).astype(bf16)

    up_came, in_came_partner, mixed, grad_down, grad_tokens, small = together(
        up_came, in_came_partner, mixed, grad_down, grad_tokens, small
    )
    grad_gate, grad_up = (
        pair(add(in_parts[0][i], came), add(in_from[i], in_came_partner[i]))
        for i, came in enumerate((gate_came, up_came))
    )
    grad_router = small[:id_count].T
    grad_const_gate = small[id_count : id_count + const_count].T
    grad_const_vec = small[id_count + const_count :]
    return (
        mixed,
        grad_tokens,
        grad_gate,
        grad_up,
        grad_down,
        grad_router,
        grad_const_vec,
        grad_const_gate,
    )


def solution(mesh):
    paired = mesh.shape["rep"] == 1 and mesh.shape["dp"] == 4

    def on_device(tokens, routes, gate_weight, *others):
        id_count = others[2].shape[1]
        stored_experts, stored_rows, hidden_width = gate_weight.shape
        row_count, top_count = routes.shape
        halved = row_count * top_count == (row_count // 2) * id_count
        if paired and stored_experts == 2 and halved and row_count == 128:
            return on_device_paired(tokens, routes, gate_weight, *others)
        return on_device_general(tokens, routes, gate_weight, *others)

    placed = (
        P(("groups", "expert", "dp"), None),
        P(("groups", "expert", "dp"), None),
        P("expert", ("dp", "rep"), None),
        P("expert", ("dp", "rep"), None),
        P("expert", ("dp", "rep"), None),
        P(),
        P(),
        P(),
        P(("groups", "expert", "dp"), None),
    )
    return jax.shard_map(
        on_device,
        mesh=mesh,
        in_specs=placed,
        out_specs=(
            P(("groups", "expert", "dp"), None),
            P(("groups", "expert", "dp"), None),
            P(("groups", "expert"), ("dp", "rep"), None),
            P(("groups", "expert"), ("dp", "rep"), None),
            P(("groups", "expert"), ("dp", "rep"), None),
            P("groups", None),
            P("groups", None),
            P("groups", None),
        ),
        check_vma=False,
    )
```

```python
import jax
import jax.numpy as jnp
from jax import lax
from jax.experimental import pallas as pl
from jax.experimental.pallas import tpu as pltpu
from jax.sharding import PartitionSpec as P

ROWS_CONTRACT = (((0,), (0,)), ((), ()))
LAST_CONTRACT = (((1,), (1,)), ((), ()))


def silu_slope(argument):
    logistic = jax.nn.sigmoid(argument)
    return logistic * (1.0 + argument * (1.0 - logistic))


def expert_forward(token_rows, w_gate, w_up, w_down):
    pre_gate = jnp.dot(token_rows, w_gate, preferred_element_type=jnp.float32)
    pre_up = jnp.dot(token_rows, w_up, preferred_element_type=jnp.float32)
    hidden = (jax.nn.silu(pre_gate) * pre_up).astype(jnp.bfloat16)
    output_rows = lax.dot_general(hidden, w_down, LAST_CONTRACT, preferred_element_type=jnp.float32)
    return (output_rows.astype(jnp.bfloat16), hidden, pre_gate, pre_up)


def expert_backward(pre_gate, pre_up, upstream, w_gate, w_up, w_down):
    d_hidden = jnp.dot(upstream, w_down, preferred_element_type=jnp.float32)
    d_gate = (d_hidden * pre_up * silu_slope(pre_gate)).astype(jnp.bfloat16)
    d_up = (d_hidden * jax.nn.silu(pre_gate)).astype(jnp.bfloat16)
    back_rows = lax.dot_general(d_gate, w_gate, LAST_CONTRACT, preferred_element_type=jnp.float32)
    back_rows = back_rows + lax.dot_general(
        d_up, w_up, LAST_CONTRACT, preferred_element_type=jnp.float32
    )
    return (back_rows.astype(jnp.bfloat16), d_gate, d_up)


def block_terms(token_rows, hidden, upstream, d_gate, d_up):
    term_gate = lax.dot_general(
        token_rows, d_gate, ROWS_CONTRACT, preferred_element_type=jnp.float32
    )
    term_up = lax.dot_general(token_rows, d_up, ROWS_CONTRACT, preferred_element_type=jnp.float32)
    term_down = lax.dot_general(upstream, hidden, ROWS_CONTRACT, preferred_element_type=jnp.float32)
    return (term_gate, term_up, term_down)


def token_trip(buffer):
    return lax.all_to_all(buffer, ("expert", "dp"), split_axis=0, concat_axis=0, tiled=True)


def on_device_general(
    tokens, routes, gate_weight, up_weight, down_weight, router, const_vec, const_gate, grad_out
):
    shard_rows, top_count = routes.shape
    row_count = shard_rows // lax.axis_size("rep")
    first_row = lax.axis_index("rep") * row_count
    tokens = lax.dynamic_slice_in_dim(tokens, first_row, row_count, 0)
    routes = lax.dynamic_slice_in_dim(routes, first_row, row_count, 0)
    grad_out = lax.dynamic_slice_in_dim(grad_out, first_row, row_count, 0)
    model_width = tokens.shape[1]
    id_count = router.shape[1]
    const_count = const_vec.shape[0]
    expert_count = id_count - 2 - const_count
    half_rows = row_count // 2
    capacity = (half_rows * top_count + id_count - 1) // id_count
    target_count = lax.axis_size("expert") * lax.axis_size("dp")
    slot_count = target_count * capacity
    stored_experts, stored_rows, hidden_width = gate_weight.shape
    spread = lax.axis_size("dp") * lax.axis_size("rep")
    id_range = lax.broadcasted_iota(jnp.int32, (1, 1, id_count), 2)
    picks = routes[:, :, None] == id_range
    named = jnp.sum(picks.astype(jnp.float32), axis=1)
    row_index = lax.broadcasted_iota(jnp.int32, (row_count, row_count), 0)
    column_index = lax.broadcasted_iota(jnp.int32, (row_count, row_count), 1)
    before = (
        (column_index < row_index) & (column_index // half_rows == row_index // half_rows)
    ).astype(jnp.float32)
    earlier = jnp.dot(before, named, precision=lax.Precision.HIGHEST)
    slot = jnp.sum(jnp.where(picks, earlier[:, None, :], 0.0), axis=2).astype(jnp.int32)
    member = lax.broadcasted_iota(jnp.int32, (row_count, top_count), 0) // half_rows
    routed = routes < expert_count
    target = jnp.where(routed, (2 * routes + member) * capacity + slot, slot_count)
    slot_range = lax.broadcasted_iota(jnp.int32, (slot_count, 1), 0)
    pair_range = lax.broadcasted_iota(jnp.int32, (1, row_count * top_count), 1)
    hits = slot_range == target.reshape(1, -1)
    owner = jnp.sum(jnp.where(hits, pair_range, 0), axis=1)
    filled = jnp.any(hits, axis=1)
    owner_token = owner // top_count
    target_safe = jnp.where(routed, target, 0)
    logits = jnp.dot(tokens, router, preferred_element_type=jnp.float32)
    chosen = jnp.sum(jnp.where(picks, jax.nn.sigmoid(logits)[:, None, :], 0.0), axis=2)
    gates = chosen.astype(jnp.bfloat16)
    gates_float = gates.astype(jnp.float32)
    slot_gate = jnp.where(filled, gates.reshape(-1)[owner], jnp.zeros((), jnp.bfloat16)).astype(
        jnp.float32
    )
    repeat = spread // stored_experts
    fetched = (
        lax.all_to_all(
            jnp.repeat(gate_weight, repeat, axis=0),
            ("dp", "rep"),
            split_axis=0,
            concat_axis=1,
            tiled=True,
        ),
        lax.all_to_all(
            jnp.repeat(up_weight, repeat, axis=0),
            ("dp", "rep"),
            split_axis=0,
            concat_axis=1,
            tiled=True,
        ),
        lax.all_to_all(
            jnp.repeat(down_weight, repeat, axis=0),
            ("dp", "rep"),
            split_axis=0,
            concat_axis=1,
            tiled=True,
        ),
    )
    w_gate = fetched[0].reshape(model_width, hidden_width)
    w_up = fetched[1].reshape(model_width, hidden_width)
    w_down = fetched[2].reshape(model_width, hidden_width)
    send_rows = jnp.where(filled[:, None], tokens[owner_token], jnp.zeros((), jnp.bfloat16))
    arrived = token_trip(send_rows.reshape(target_count, capacity, model_width)).reshape(
        slot_count, model_width
    )
    output_rows, hidden, pre_gate, pre_up = expert_forward(arrived, w_gate, w_up, w_down)
    returned = token_trip(output_rows.reshape(target_count, capacity, model_width)).reshape(
        slot_count, model_width
    )
    picked_out = returned[target_safe].astype(jnp.float32)
    mixed_sum = jnp.sum(
        jnp.where(routed[:, :, None], gates_float[:, :, None] * picked_out, 0.0), axis=1
    )
    cotangent_all = grad_out.astype(jnp.float32)
    routed_grad = jnp.sum(
        jnp.where(routed[:, :, None], picked_out * cotangent_all[:, None, :], 0.0), axis=2
    )
    upstream_send = (slot_gate[:, None] * grad_out[owner_token].astype(jnp.float32)).astype(
        jnp.bfloat16
    )
    upstream = token_trip(upstream_send.reshape(target_count, capacity, model_width)).reshape(
        slot_count, model_width
    )
    back_rows, d_gate, d_up = expert_backward(pre_gate, pre_up, upstream, w_gate, w_up, w_down)
    terms = block_terms(arrived, hidden, upstream, d_gate, d_up)
    sent_terms = tuple(
        (term.astype(jnp.bfloat16).reshape(spread, stored_rows, hidden_width) for term in terms)
    )
    gathered_terms = (
        lax.all_to_all(sent_terms[0], ("dp", "rep"), split_axis=0, concat_axis=0, tiled=True),
        lax.all_to_all(sent_terms[1], ("dp", "rep"), split_axis=0, concat_axis=0, tiled=True),
        lax.all_to_all(sent_terms[2], ("dp", "rep"), split_axis=0, concat_axis=0, tiled=True),
    )
    copies = spread // stored_experts
    grad_gate, grad_up, grad_down = (
        jnp.sum(
            arrived_term.reshape(stored_experts, copies, stored_rows, hidden_width),
            axis=1,
            dtype=jnp.float32,
        ).astype(jnp.bfloat16)
        for arrived_term in gathered_terms
    )
    returned_back = token_trip(back_rows.reshape(target_count, capacity, model_width)).reshape(
        slot_count, model_width
    )
    back_sum = jnp.sum(
        jnp.where(routed[:, :, None], returned_back[target_safe].astype(jnp.float32), 0.0), axis=1
    )
    is_copy = routes == expert_count + 1
    const_ids = expert_count + 2 + lax.broadcasted_iota(jnp.int32, (1, 1, const_count), 2)
    is_const = routes[:, :, None] == const_ids
    copy_weight = jnp.sum(jnp.where(is_copy, gates_float, 0.0), axis=1)
    const_weight = jnp.sum(jnp.where(is_const, gates_float[:, :, None], 0.0), axis=1)
    const_share = jax.nn.sigmoid(jnp.dot(tokens, const_gate, preferred_element_type=jnp.float32))
    const_rest = (const_weight * (1.0 - const_share)).astype(jnp.bfloat16)
    coefficient = copy_weight + jnp.sum(const_weight * const_share, axis=1)
    tokens_float = tokens.astype(jnp.float32)
    constant_term = jnp.dot(const_rest, const_vec, preferred_element_type=jnp.float32)
    mixed = (mixed_sum + coefficient[:, None] * tokens_float + constant_term).astype(jnp.bfloat16)
    along_token = jnp.sum(cotangent_all * tokens_float, axis=1)
    along_const = lax.dot_general(
        grad_out, const_vec, LAST_CONTRACT, preferred_element_type=jnp.float32
    )
    const_value = const_share * along_token[:, None] + (1.0 - const_share) * along_const
    null_grad = jnp.where(is_copy, along_token[:, None], 0.0) + jnp.sum(
        jnp.where(is_const, const_value[:, None, :], 0.0), axis=2
    )
    pick_grad = routed_grad + null_grad
    slope_grad = pick_grad * chosen * (1.0 - chosen)
    logit_grad = jnp.sum(jnp.where(picks, slope_grad[:, :, None], 0.0), axis=1).astype(jnp.bfloat16)
    share_grad = (
        const_weight * (along_token[:, None] - along_const) * const_share * (1.0 - const_share)
    ).astype(jnp.bfloat16)
    back_local = coefficient[:, None] * cotangent_all
    back_local = back_local + lax.dot_general(
        logit_grad, router, LAST_CONTRACT, preferred_element_type=jnp.float32
    )
    back_local = back_local + lax.dot_general(
        share_grad, const_gate, LAST_CONTRACT, preferred_element_type=jnp.float32
    )
    grad_tokens = (back_sum + back_local).astype(jnp.bfloat16)
    router_part = lax.dot_general(
        tokens, logit_grad, ROWS_CONTRACT, preferred_element_type=jnp.float32
    )
    vector_part = lax.dot_general(
        const_rest, grad_out, ROWS_CONTRACT, preferred_element_type=jnp.float32
    )
    mixing_part = lax.dot_general(
        tokens, share_grad, ROWS_CONTRACT, preferred_element_type=jnp.float32
    )
    grad_router, grad_const_vec, grad_const_gate = lax.psum(
        (router_part, vector_part, mixing_part), ("expert", "dp", "rep")
    )
    mixed_all, grad_tokens_all = (
        lax.all_gather(mixed, "rep", axis=0, tiled=True),
        lax.all_gather(grad_tokens, "rep", axis=0, tiled=True),
    )
    return (
        mixed_all,
        grad_tokens_all,
        grad_gate,
        grad_up,
        grad_down,
        grad_router,
        grad_const_vec,
        grad_const_gate,
    )


HALF = 64
SLOTS = 32
SCRATCH_BYTES = 22 * 1024 * 1024
LONG = 20_000_000_000


def local_kernel(body, scalars, operands, outputs, scratch, moved, mark=None):
    marks = [] if mark is None else [mark]

    def kernel(place, *refs):
        body(place, *refs[len(marks) :])

    return pl.pallas_call(
        kernel,
        out_shape=outputs,
        in_specs=[pl.BlockSpec(memory_space=pltpu.SMEM)]
        + [pl.BlockSpec(memory_space=pl.ANY) for _ in [*marks, *operands]],
        out_specs=[pl.BlockSpec(memory_space=pltpu.VMEM) for _ in outputs],
        scratch_shapes=scratch,
        compiler_params=pltpu.CompilerParams(vmem_limit_bytes=SCRATCH_BYTES),
        cost_estimate=pl.CostEstimate(flops=moved, bytes_accessed=moved, transcendentals=0),
    )(scalars, *marks, *operands)


def bring(pairs, sems):
    copies = [
        pltpu.make_async_copy(source, target, sems.at[i])
        for i, (source, target) in enumerate(pairs)
    ]
    for copy in copies:
        copy.start()
    return copies


def mm(a, b):
    return jnp.dot(a, b, preferred_element_type=jnp.float32)


def mm_rows(a, b):
    return lax.dot_general(a, b, ROWS_CONTRACT, preferred_element_type=jnp.float32)


def mm_last(a, b):
    return lax.dot_general(a, b, LAST_CONTRACT, preferred_element_type=jnp.float32)


def weight_pairs(core, parts, target):
    stored, *fetched = parts
    width = target.shape[0] // 4
    sources = [stored.at[core], *fetched]
    return [(s, target.at[pl.ds(j * width, width)]) for j, s in enumerate(sources)]


def payload_kernel(tokens, grads, routes, router, out, step):
    step[...] = jnp.zeros_like(step)
    count = tokens.shape[0]
    ids = lax.broadcasted_iota(jnp.int32, (router.shape[0], count), 0)
    named = routes[0:1, :] == ids
    for k in range(1, routes.shape[0]):
        named = named | (routes[k : k + 1, :] == ids)
    gates = jnp.where(named, jax.nn.sigmoid(mm_last(router[...], tokens[...])), 0.0)
    out[0:count, :] = tokens[...]
    out[count : 2 * count, :] = grads[...]
    for e in range(out.shape[1] // count):
        out[2 * count :, e * count : (e + 1) * count] = jnp.broadcast_to(
            gates[e : e + 1], (16, count)
        ).astype(jnp.bfloat16)


def step_kernel(before, after_it):
    after_it[...] = before[...]


def next_step(step):
    return pl.pallas_call(
        step_kernel,
        out_shape=jax.ShapeDtypeStruct(step.shape, step.dtype),
        cost_estimate=pl.CostEstimate(flops=LONG, bytes_accessed=LONG, transcendentals=0),
    )(step)


def forward_kernel(place, *refs):
    payloads = refs[0:8]
    gate_weight, up_weight, partner, cross, cross_partner = refs[8:13]
    pick_out, gate_out, rows_out, cot_out, hidden_out, act_out, slope_out = refs[13:20]
    outs = refs[20:24]
    blocks, w_gate, w_up, upstream, sems = refs[24:29]
    me, expert = place[0], place[1]
    core = me & 1
    count = pick_out.shape[1]
    slots = count // HALF * SLOTS
    copies = bring(
        [(payloads[b], blocks.at[b]) for b in range(8)]
        + weight_pairs(core, (gate_weight, partner.at[0], cross.at[0], cross_partner.at[0]), w_gate)
        + weight_pairs(core, (up_weight, partner.at[1], cross.at[1], cross_partner.at[1]), w_up),
        sems,
    )
    width = w_gate.shape[0] // 4
    row = lax.broadcasted_iota(jnp.int32, (count, count), 0)
    column = lax.broadcasted_iota(jnp.int32, (count, count), 1)
    before = ((row < column) & (row // HALF == column // HALF)).astype(jnp.bfloat16)
    lane = lax.broadcasted_iota(jnp.int32, (1, count), 1)
    slot = lax.broadcasted_iota(jnp.int32, (slots, count), 0)
    mine = pl.ds(pl.multiple_of(expert * count, count), count)
    for b in range(8):
        copies[b].wait()
    gates = jnp.concatenate(
        [blocks[b, 2 * count :, mine].astype(jnp.float32)[0:1] for b in range(8)], axis=0
    )
    picked = gates != 0.0
    earlier = mm(picked.astype(jnp.bfloat16), before).astype(jnp.int32)
    target = jnp.where(picked, (lane // HALF) * SLOTS + earlier, -1)
    for b in range(8):
        chosen = slot == target[b : b + 1]
        pick = chosen.astype(jnp.bfloat16)
        gate_pick = jnp.where(chosen, gates[b : b + 1], 0.0)
        gate = jnp.sum(gate_pick, axis=1, keepdims=True)
        at = b * slots
        pick_out[at : at + slots, :] = pick
        gate_out[at : at + slots, :] = gate_pick.astype(jnp.bfloat16)
        for j in range(4):
            columns = pl.ds(pl.multiple_of((me ^ j) * width, width), width)
            here = (slice(at, at + slots), slice(j * width, (j + 1) * width))
            rows_out[here] = mm(pick, blocks[b, 0:count, columns]).astype(jnp.bfloat16)
            cot = mm(pick, blocks[b, count : 2 * count, columns])
            cot_out[here] = cot.astype(jnp.bfloat16)
            upstream[here] = (gate * cot).astype(jnp.bfloat16)
    for copy in copies[8:]:
        copy.wait()
    pre_gate = mm(rows_out[...], w_gate[...])
    pre_up = mm(rows_out[...], w_up[...])
    logistic = jax.nn.sigmoid(pre_gate)
    act = pre_gate * logistic
    hidden_out[...] = (act * pre_up).astype(jnp.bfloat16)
    act_out[...] = act.astype(jnp.bfloat16)
    slope = logistic * (1.0 + pre_gate * (1.0 - logistic))
    slope_out[...] = (pre_up * slope).astype(jnp.bfloat16)
    for j in (2, 1, 3, 0):
        outs[j][...] = mm_rows(
            upstream[:, j * width : (j + 1) * width], hidden_out[...]
        ).astype(jnp.bfloat16)


def scatter(me, pick, own_out, other_out, column_block):
    width = own_out.shape[1] // 4
    slots = pick.shape[0] // 8
    count = pick.shape[1]
    for j in range(4):
        columns = pl.ds(pl.multiple_of((me ^ j) * width, width), width)
        block = column_block(j, columns).astype(jnp.bfloat16)
        for b in range(8):
            out = own_out if b % 2 == 0 else other_out
            at = b * slots
            out[(b // 2) * count : (b // 2 + 1) * count, columns] = mm_rows(
                pick[at : at + slots, :], block[at : at + slots]
            ).astype(jnp.bfloat16)


def output_kernel(place, *refs):
    gate_pick_in, hidden_in, down_weight, partner, cross, cross_partner = refs[0:6]
    own_out, other_out = refs[6:8]
    gate_pick, hidden, w_down, sems = refs[8:12]
    me = place[0]
    copies = bring(
        weight_pairs(me & 1, (down_weight, partner.at[2], cross.at[me & 1], cross_partner), w_down)
        + [(gate_pick_in, gate_pick), (hidden_in, hidden)],
        sems,
    )
    for copy in copies:
        copy.wait()
    width = w_down.shape[0] // 4
    scatter(me, gate_pick, own_out, other_out, lambda j, _: (
        mm_last(hidden[...], w_down[j * width : (j + 1) * width])
    ))


def backward_kernel(place, *refs):
    (pick_in, gate_pick_in, rows_in, hidden_in, cot_in, act_in, slope_in, router_in,
     down_weight, partner, cross, cross_partner) = refs[0:12]
    (d_gate_out, d_up_out, logit_out, router_out, keep_out, partner_out, cross_partner_out,
     gate_sent, up_sent) = refs[12:21]
    pick, gate_pick, rows, hidden, cot, act, slope, router, w_down, sems = refs[21:31]
    me, expert = place[0], place[1]
    copies = bring(
        [(cot_in, cot)]
        + weight_pairs(me & 1, (down_weight, partner.at[2], cross.at[me & 1], cross_partner), w_down)
        + [(gate_pick_in, gate_pick), (hidden_in, hidden), (rows_in, rows), (act_in, act),
           (slope_in, slope), (router_in, router)],
        sems,
    )
    for copy in copies:
        copy.wait()
    width = w_down.shape[0] // 4
    along = mm(cot[...], w_down[...])
    score = jnp.sum(hidden[...].astype(jnp.float32) * along, axis=1, keepdims=True)
    gate = jnp.sum(gate_pick[...].astype(jnp.float32), axis=1, keepdims=True)
    d_hidden = gate * along
    d_gate_out[...] = (d_hidden * slope[...].astype(jnp.float32)).astype(jnp.bfloat16)
    d_up_out[...] = (d_hidden * act[...].astype(jnp.float32)).astype(jnp.bfloat16)
    gate_outs = (keep_out.at[0], partner_out.at[0], gate_sent, cross_partner_out.at[0])
    up_outs = (keep_out.at[1], partner_out.at[1], up_sent, cross_partner_out.at[1])
    for j in range(4):
        part = rows[:, j * width : (j + 1) * width]
        gate_outs[j][...] = mm_rows(part, d_gate_out[...]).astype(jnp.bfloat16)
        up_outs[j][...] = mm_rows(part, d_up_out[...]).astype(jnp.bfloat16)
    ids = router.shape[0]
    logits = jnp.zeros((pick_in.shape[0], ids), jnp.float32)
    for j in range(4):
        columns = pl.ds(pl.multiple_of((me ^ j) * width, width), width)
        logits += mm_last(
            rows[:, j * width : (j + 1) * width], router[:, columns].astype(jnp.bfloat16)
        )
    named = lax.broadcasted_iota(jnp.int32, (1, ids), 1) == expert
    share = jax.nn.sigmoid(jnp.sum(jnp.where(named, logits, 0.0), axis=1, keepdims=True))
    slope_grad = jnp.where(gate != 0.0, score * share * (1.0 - share), 0.0)
    logit_grad = jnp.broadcast_to(slope_grad, logit_out.shape).astype(jnp.bfloat16)
    logit_out[...] = logit_grad
    for j in range(4):
        columns = pl.ds(pl.multiple_of((me ^ j) * width, width), width)
        total = mm_rows(logit_grad, rows[:, j * width : (j + 1) * width])
        router_out[:, columns] = total[0 : router_out.shape[0]]


def back_kernel(place, *refs):
    (pick_in, d_gate_in, d_up_in, logit_in, router_in, gate_weight, up_weight, partner,
     cross, cross_partner) = refs[0:10]
    own_out, other_out = refs[10:12]
    pick, d_gate, d_up, logit_grad, router, w_gate, w_up, sems = refs[12:20]
    me, expert = place[0], place[1]
    core = me & 1
    copies = bring(
        [(pick_in, pick), (d_gate_in, d_gate), (d_up_in, d_up), (logit_in, logit_grad),
         (router_in, router)]
        + weight_pairs(core, (gate_weight, partner.at[0], cross.at[0], cross_partner.at[0]), w_gate)
        + weight_pairs(core, (up_weight, partner.at[1], cross.at[1], cross_partner.at[1]), w_up),
        sems,
    )
    for copy in copies:
        copy.wait()
    width = w_gate.shape[0] // 4
    slope_grad = logit_grad[:, 0:1].astype(jnp.float32)

    def column_block(j, columns):
        here = slice(j * width, (j + 1) * width)
        return (
            mm_last(d_gate[...], w_gate[here])
            + mm_last(d_up[...], w_up[here])
            + slope_grad * router[pl.ds(expert, 1), columns]
        )

    scatter(me, pick, own_out, other_out, column_block)


def dp_swap(value, step):
    return lax.ppermute(value, "dp", [(i, i ^ step) for i in range(4)])


def ring(value, step):
    size = lax.axis_size("expert")
    return lax.ppermute(value, "expert", [(i, (i + step) % size) for i in range(size)])


def after(value, *earlier):
    return lax.optimization_barrier((value, *earlier))[0]


def on_device_paired(
    tokens, routes, gate_weight, up_weight, down_weight, router, const_vec, const_gate, grad_out
):
    bf16, f32 = jnp.bfloat16, jnp.float32
    row_count, model_width = tokens.shape
    id_count = router.shape[1]
    const_count = const_vec.shape[0]
    expert_count = id_count - 2 - const_count
    stored_experts, stored_rows, hidden_width = gate_weight.shape
    me = lax.axis_index("dp")
    z = lax.axis_index("expert")
    core = me % 2
    expert = stored_experts * z + core
    place = jnp.stack([me, expert]).astype(jnp.int32)

    def of_expert(weight, which):
        return lax.dynamic_index_in_dim(weight, which, 0, keepdims=False)

    shape = jax.ShapeDtypeStruct
    vmem = pltpu.VMEM
    slot_count = 4 * row_count
    wide, narrow = (slot_count, model_width), (slot_count, hidden_width)
    table = (slot_count, row_count)
    weight_rows = (stored_rows, hidden_width)
    whole_weight = vmem((model_width, hidden_width), bf16)

    def together(*values):
        return lax.optimization_barrier(values)

    payload, step = pl.pallas_call(
        payload_kernel,
        out_shape=[shape((2 * row_count + 16, model_width), bf16), shape((8, 128), jnp.int32)],
        cost_estimate=pl.CostEstimate(flops=LONG, bytes_accessed=LONG, transcendentals=0),
    )(tokens, grad_out, routes.T, router.T)
    group = lax.axis_index("groups")
    near, payload_partner = ring(payload, 1), dp_swap(payload, 1)
    payload, payload_partner = together(payload, payload_partner)
    far_side = ring(payload, -1)
    in_sent = jnp.where(group == 0, gate_weight, up_weight)
    cut = stored_rows // 8 * 3
    in_came = [dp_swap(in_sent[:, :cut], 2), dp_swap(in_sent[:, cut:], 2)]
    down_cross = dp_swap(after(down_weight, payload_partner), 2)
    in_other = [lax.ppermute(in_came[0], "groups", [(0, 1), (1, 0)])]
    near, in_came[0], step = together(near, in_came[0], step)
    far = ring(near, 1)
    partner = dp_swap(
        jnp.stack([of_expert(w, 1 - core) for w in (gate_weight, up_weight, down_weight)]), 1
    )
    step = next_step(step)
    in_came[1], partner, step = together(in_came[1], partner, step)
    in_other.append(lax.ppermute(in_came[1], "groups", [(0, 1), (1, 0)]))
    step = next_step(step)
    in_other[0], in_other[1], step = together(*in_other, step)
    far_side, far, step = together(far_side, far, step)
    down_cross, step_down = together(down_cross, step)
    near_partner, far_side_partner, far_partner = dp_swap(near, 1), dp_swap(far_side, 1), dp_swap(far, 1)

    def of_core(first, second, which):
        came = jnp.concatenate([of_expert(part, which) for part in first])
        other = jnp.concatenate([of_expert(part, which) for part in second])
        return jnp.where(group == 0, jnp.stack([came, other]), jnp.stack([other, came]))

    in_cross = of_core(in_came, in_other, core)
    in_cross_partner = dp_swap(of_core(in_came, in_other, 1 - core), 1)
    down_cross_partner = dp_swap(of_expert(down_cross, 1 - core), 1)
    payloads = [payload, payload_partner, near, near_partner, far, far_partner, far_side,
                far_side_partner]
    in_weights = [gate_weight, up_weight, partner, in_cross, in_cross_partner]
    router_rows = jnp.pad(router.T.astype(f32), ((0, 16 - id_count), (0, 0)))
    pick, gate_pick, rows, cot, hidden, act, slope, *down_parts = local_kernel(
        forward_kernel,
        place,
        [*payloads, *in_weights],
        [shape(table, bf16)] * 2 + [shape(wide, bf16)] * 2 + [shape(narrow, bf16)] * 3
        + [shape(weight_rows, bf16)] * 4,
        [vmem((8, *payload.shape), bf16), whole_weight, whole_weight, vmem(wide, bf16),
         pltpu.SemaphoreType.DMA((16,))],
        LONG,
        step,
    )
    hidden, down_cross_partner = together(hidden, down_cross_partner)
    down_weights = [down_weight, partner, down_cross, down_cross_partner]
    def add(one, two):
        return one.astype(f32) + two.astype(f32)

    def sum_slots(own, came):
        return [
            add(mine, theirs).astype(bf16) for mine, theirs in zip(jnp.split(own, 2), came)
        ]

    def pair(mine, theirs):
        of = lax.broadcasted_iota(jnp.int32, (2, 1, 1), 0)
        return jnp.where(of == core, mine[None], theirs[None]).astype(bf16)

    id_range = lax.broadcasted_iota(jnp.int32, (1, 1, id_count), 2)
    named = jnp.any(routes[:, :, None] == id_range, axis=1)[:, expert_count:]
    share = jax.nn.sigmoid(mm(tokens, router[:, expert_count:]))
    gates = jnp.where(named, share, 0.0).astype(bf16).astype(f32)
    tokens_float = tokens.astype(f32)
    grad_float = grad_out.astype(f32)
    copy_weight = gates[:, 1]
    const_weight = gates[:, 2:]
    const_share = jax.nn.sigmoid(mm(tokens, const_gate))
    const_rest = (const_weight * (1.0 - const_share)).astype(bf16)
    coefficient = copy_weight + jnp.sum(const_weight * const_share, axis=1)
    along_token = jnp.sum(grad_float * tokens_float, axis=1, keepdims=True)
    along_const = mm_last(grad_out, const_vec)
    const_value = const_share * along_token + (1.0 - const_share) * along_const
    pick_grad = jnp.concatenate(
        [jnp.zeros_like(along_token), along_token, const_value], axis=1
    )
    null_grad = jnp.where(named, pick_grad * share * (1.0 - share), 0.0).astype(bf16)
    share_grad = (
        const_weight * (along_token - along_const) * const_share * (1.0 - const_share)
    ).astype(bf16)
    mixed_own, mixed_other = local_kernel(
        output_kernel,
        place,
        [gate_pick, hidden, *down_weights],
        [shape(wide, bf16)] * 2,
        [vmem(table, bf16), vmem(narrow, bf16), whole_weight, pltpu.SemaphoreType.DMA((6,))],
        LONG,
        step_down,
    )
    down_came, down_came_partner = dp_swap(down_parts[2], 2), dp_swap(down_parts[3], 3)
    parts = [mixed_other[k * row_count : (k + 1) * row_count] for k in range(4)]
    mixed_came = [dp_swap(parts[2], 1), dp_swap(parts[3], 1)]
    mixed_own, mixed_came[0], mixed_came[1], down_came, cot = together(
        mixed_own, *mixed_came, down_came, cot
    )
    mixed_first = sum_slots(mixed_own[2 * row_count :], mixed_came)
    mixed_near = ring(mixed_first[0], -1)
    mixed_late = dp_swap(mixed_other[: 2 * row_count], 1)
    down_from = dp_swap(down_parts[1], 1)
    d_gate, d_up, logit_grad, router_row, *in_parts, gate_sent, up_sent = local_kernel(
        backward_kernel,
        place,
        [pick, gate_pick, rows, hidden, cot, act, slope, router_rows, *down_weights],
        [shape(narrow, bf16)] * 2 + [shape(table, bf16), shape((8, model_width), f32)]
        + [shape((2, *weight_rows), bf16)] * 3 + [shape(weight_rows, bf16)] * 2,
        [vmem(table, bf16)] * 2 + [vmem(wide, bf16), vmem(narrow, bf16), vmem(wide, bf16),
         vmem(narrow, bf16), vmem(narrow, bf16), vmem(router_rows.shape, f32), whole_weight,
         pltpu.SemaphoreType.DMA((11,))],
        LONG,
    )
    (d_gate, router_row, in_parts[1], in_parts[2], gate_sent, up_sent, down_came_partner,
     mixed_near, mixed_late, down_from) = together(
        d_gate, router_row, in_parts[1], in_parts[2], gate_sent, up_sent, down_came_partner,
        mixed_near, mixed_late, down_from
    )
    mixed_late = sum_slots(mixed_own[: 2 * row_count], jnp.split(mixed_late, 2))
    small = jnp.concatenate(
        [
            mm_rows(jnp.concatenate([null_grad, share_grad], axis=1), tokens),
            mm_rows(const_rest, grad_out),
        ],
        axis=0,
    )
    experts = lax.broadcasted_iota(jnp.int32, (expert_count, 1), 0)
    routed = jnp.where(experts == expert, router_row[0:1], 0.0)
    small = jnp.concatenate([routed, small], axis=0)
    gate_came, in_from, small_came = dp_swap(gate_sent, 2), dp_swap(in_parts[1], 1), dp_swap(small, 2)
    mixed_side = ring(mixed_first[1].astype(bf16), 1)
    mixed_near = ring(add(mixed_near, mixed_late[1]).astype(bf16), -1)
    back_own, back_other = local_kernel(
        back_kernel,
        place,
        [pick, d_gate, d_up, logit_grad, router_rows, *in_weights],
        [shape(wide, bf16)] * 2,
        [vmem(table, bf16), vmem(narrow, bf16), vmem(narrow, bf16), vmem(table, bf16),
         vmem(router_rows.shape, f32), whole_weight, whole_weight,
         pltpu.SemaphoreType.DMA((13,))],
        LONG,
    )
    (back_own, back_other, gate_came, in_from, small_came, mixed_side, mixed_near, up_sent,
     in_parts[2]) = together(
        back_own, back_other, gate_came, in_from, small_came, mixed_side, mixed_near, up_sent,
        in_parts[2]
    )
    up_came, in_came_partner = dp_swap(up_sent, 2), dp_swap(in_parts[2], 3)
    small = small + small_came
    back_came, small_came = together(dp_swap(back_other, 1), dp_swap(small, 1))
    back_late = sum_slots(back_own[: 2 * row_count], jnp.split(back_came[: 2 * row_count], 2))
    back_first = sum_slots(back_own[2 * row_count :], jnp.split(back_came[2 * row_count :], 2))
    back_near, back_side = ring(back_first[0], -1), ring(back_first[1], 1)
    small = small + small_came
    small_came = lax.ppermute(small, "expert", [(i, i ^ 1) for i in range(4)])
    back_near, back_side, up_came = together(back_near, back_side, up_came)
    back_near = ring(add(back_near, back_late[1]).astype(bf16), -1)
    small = small + small_came
    small = small + lax.ppermute(small, "expert", [(i, i ^ 2) for i in range(4)])
    mixed_sum = add(mixed_side, mixed_near) + mixed_late[0].astype(f32)
    back_sum = add(back_side, back_near) + back_late[0].astype(f32)
    grad_down = pair(add(down_parts[0], down_came), add(down_from, down_came_partner))
    mixed = (
        mixed_sum + coefficient[:, None] * tokens_float + mm(const_rest, const_vec)
    ).astype(bf16)
    back_local = (
        coefficient[:, None] * grad_float
        + mm_last(null_grad, router[:, expert_count:])
        + mm_last(share_grad, const_gate)
    )
    grad_tokens = (back_sum + back_local).astype(bf16)

    up_came, in_came_partner, mixed, grad_down, grad_tokens, small = together(
        up_came, in_came_partner, mixed, grad_down, grad_tokens, small
    )
    grad_gate, grad_up = (
        pair(add(in_parts[0][i], came), add(in_from[i], in_came_partner[i]))
        for i, came in enumerate((gate_came, up_came))
    )
    grad_router = small[:id_count].T
    grad_const_gate = small[id_count : id_count + const_count].T
    grad_const_vec = small[id_count + const_count :]
    return (
        mixed,
        grad_tokens,
        grad_gate,
        grad_up,
        grad_down,
        grad_router,
        grad_const_vec,
        grad_const_gate,
    )


def solution(mesh):
    paired = mesh.shape["rep"] == 1 and mesh.shape["dp"] == 4

    def on_device(tokens, routes, gate_weight, *others):
        id_count = others[2].shape[1]
        stored_experts, stored_rows, hidden_width = gate_weight.shape
        row_count, top_count = routes.shape
        halved = row_count * top_count == (row_count // 2) * id_count
        if paired and stored_experts == 2 and halved and row_count == 128:
            return on_device_paired(tokens, routes, gate_weight, *others)
        return on_device_general(tokens, routes, gate_weight, *others)

    placed = (
        P(("groups", "expert", "dp"), None),
        P(("groups", "expert", "dp"), None),
        P("expert", ("dp", "rep"), None),
        P("expert", ("dp", "rep"), None),
        P("expert", ("dp", "rep"), None),
        P(),
        P(),
        P(),
        P(("groups", "expert", "dp"), None),
    )
    return jax.shard_map(
        on_device,
        mesh=mesh,
        in_specs=placed,
        out_specs=(
            P(("groups", "expert", "dp"), None),
            P(("groups", "expert", "dp"), None),
            P(("groups", "expert"), ("dp", "rep"), None),
            P(("groups", "expert"), ("dp", "rep"), None),
            P(("groups", "expert"), ("dp", "rep"), None),
            P("groups", None),
            P("groups", None),
            P("groups", None),
        ),
        check_vma=False,
    )
```

```python
import jax
import jax.numpy as jnp
from jax import lax
from jax.experimental import pallas as pl
from jax.experimental.pallas import tpu as pltpu
from jax.sharding import PartitionSpec as P

ROWS_CONTRACT = (((0,), (0,)), ((), ()))
LAST_CONTRACT = (((1,), (1,)), ((), ()))


def silu_slope(argument):
    logistic = jax.nn.sigmoid(argument)
    return logistic * (1.0 + argument * (1.0 - logistic))


def expert_forward(token_rows, w_gate, w_up, w_down):
    pre_gate = jnp.dot(token_rows, w_gate, preferred_element_type=jnp.float32)
    pre_up = jnp.dot(token_rows, w_up, preferred_element_type=jnp.float32)
    hidden = (jax.nn.silu(pre_gate) * pre_up).astype(jnp.bfloat16)
    output_rows = lax.dot_general(hidden, w_down, LAST_CONTRACT, preferred_element_type=jnp.float32)
    return (output_rows.astype(jnp.bfloat16), hidden, pre_gate, pre_up)


def expert_backward(pre_gate, pre_up, upstream, w_gate, w_up, w_down):
    d_hidden = jnp.dot(upstream, w_down, preferred_element_type=jnp.float32)
    d_gate = (d_hidden * pre_up * silu_slope(pre_gate)).astype(jnp.bfloat16)
    d_up = (d_hidden * jax.nn.silu(pre_gate)).astype(jnp.bfloat16)
    back_rows = lax.dot_general(d_gate, w_gate, LAST_CONTRACT, preferred_element_type=jnp.float32)
    back_rows = back_rows + lax.dot_general(
        d_up, w_up, LAST_CONTRACT, preferred_element_type=jnp.float32
    )
    return (back_rows.astype(jnp.bfloat16), d_gate, d_up)


def block_terms(token_rows, hidden, upstream, d_gate, d_up):
    term_gate = lax.dot_general(
        token_rows, d_gate, ROWS_CONTRACT, preferred_element_type=jnp.float32
    )
    term_up = lax.dot_general(token_rows, d_up, ROWS_CONTRACT, preferred_element_type=jnp.float32)
    term_down = lax.dot_general(upstream, hidden, ROWS_CONTRACT, preferred_element_type=jnp.float32)
    return (term_gate, term_up, term_down)


def token_trip(buffer):
    return lax.all_to_all(buffer, ("expert", "dp"), split_axis=0, concat_axis=0, tiled=True)


def on_device_general(
    tokens, routes, gate_weight, up_weight, down_weight, router, const_vec, const_gate, grad_out
):
    shard_rows, top_count = routes.shape
    row_count = shard_rows // lax.axis_size("rep")
    first_row = lax.axis_index("rep") * row_count
    tokens = lax.dynamic_slice_in_dim(tokens, first_row, row_count, 0)
    routes = lax.dynamic_slice_in_dim(routes, first_row, row_count, 0)
    grad_out = lax.dynamic_slice_in_dim(grad_out, first_row, row_count, 0)
    model_width = tokens.shape[1]
    id_count = router.shape[1]
    const_count = const_vec.shape[0]
    expert_count = id_count - 2 - const_count
    half_rows = row_count // 2
    capacity = (half_rows * top_count + id_count - 1) // id_count
    target_count = lax.axis_size("expert") * lax.axis_size("dp")
    slot_count = target_count * capacity
    stored_experts, stored_rows, hidden_width = gate_weight.shape
    spread = lax.axis_size("dp") * lax.axis_size("rep")
    id_range = lax.broadcasted_iota(jnp.int32, (1, 1, id_count), 2)
    picks = routes[:, :, None] == id_range
    named = jnp.sum(picks.astype(jnp.float32), axis=1)
    row_index = lax.broadcasted_iota(jnp.int32, (row_count, row_count), 0)
    column_index = lax.broadcasted_iota(jnp.int32, (row_count, row_count), 1)
    before = (
        (column_index < row_index) & (column_index // half_rows == row_index // half_rows)
    ).astype(jnp.float32)
    earlier = jnp.dot(before, named, precision=lax.Precision.HIGHEST)
    slot = jnp.sum(jnp.where(picks, earlier[:, None, :], 0.0), axis=2).astype(jnp.int32)
    member = lax.broadcasted_iota(jnp.int32, (row_count, top_count), 0) // half_rows
    routed = routes < expert_count
    target = jnp.where(routed, (2 * routes + member) * capacity + slot, slot_count)
    slot_range = lax.broadcasted_iota(jnp.int32, (slot_count, 1), 0)
    pair_range = lax.broadcasted_iota(jnp.int32, (1, row_count * top_count), 1)
    hits = slot_range == target.reshape(1, -1)
    owner = jnp.sum(jnp.where(hits, pair_range, 0), axis=1)
    filled = jnp.any(hits, axis=1)
    owner_token = owner // top_count
    target_safe = jnp.where(routed, target, 0)
    logits = jnp.dot(tokens, router, preferred_element_type=jnp.float32)
    chosen = jnp.sum(jnp.where(picks, jax.nn.sigmoid(logits)[:, None, :], 0.0), axis=2)
    gates = chosen.astype(jnp.bfloat16)
    gates_float = gates.astype(jnp.float32)
    slot_gate = jnp.where(filled, gates.reshape(-1)[owner], jnp.zeros((), jnp.bfloat16)).astype(
        jnp.float32
    )
    repeat = spread // stored_experts
    fetched = (
        lax.all_to_all(
            jnp.repeat(gate_weight, repeat, axis=0),
            ("dp", "rep"),
            split_axis=0,
            concat_axis=1,
            tiled=True,
        ),
        lax.all_to_all(
            jnp.repeat(up_weight, repeat, axis=0),
            ("dp", "rep"),
            split_axis=0,
            concat_axis=1,
            tiled=True,
        ),
        lax.all_to_all(
            jnp.repeat(down_weight, repeat, axis=0),
            ("dp", "rep"),
            split_axis=0,
            concat_axis=1,
            tiled=True,
        ),
    )
    w_gate = fetched[0].reshape(model_width, hidden_width)
    w_up = fetched[1].reshape(model_width, hidden_width)
    w_down = fetched[2].reshape(model_width, hidden_width)
    send_rows = jnp.where(filled[:, None], tokens[owner_token], jnp.zeros((), jnp.bfloat16))
    arrived = token_trip(send_rows.reshape(target_count, capacity, model_width)).reshape(
        slot_count, model_width
    )
    output_rows, hidden, pre_gate, pre_up = expert_forward(arrived, w_gate, w_up, w_down)
    returned = token_trip(output_rows.reshape(target_count, capacity, model_width)).reshape(
        slot_count, model_width
    )
    picked_out = returned[target_safe].astype(jnp.float32)
    mixed_sum = jnp.sum(
        jnp.where(routed[:, :, None], gates_float[:, :, None] * picked_out, 0.0), axis=1
    )
    cotangent_all = grad_out.astype(jnp.float32)
    routed_grad = jnp.sum(
        jnp.where(routed[:, :, None], picked_out * cotangent_all[:, None, :], 0.0), axis=2
    )
    upstream_send = (slot_gate[:, None] * grad_out[owner_token].astype(jnp.float32)).astype(
        jnp.bfloat16
    )
    upstream = token_trip(upstream_send.reshape(target_count, capacity, model_width)).reshape(
        slot_count, model_width
    )
    back_rows, d_gate, d_up = expert_backward(pre_gate, pre_up, upstream, w_gate, w_up, w_down)
    terms = block_terms(arrived, hidden, upstream, d_gate, d_up)
    sent_terms = tuple(
        (term.astype(jnp.bfloat16).reshape(spread, stored_rows, hidden_width) for term in terms)
    )
    gathered_terms = (
        lax.all_to_all(sent_terms[0], ("dp", "rep"), split_axis=0, concat_axis=0, tiled=True),
        lax.all_to_all(sent_terms[1], ("dp", "rep"), split_axis=0, concat_axis=0, tiled=True),
        lax.all_to_all(sent_terms[2], ("dp", "rep"), split_axis=0, concat_axis=0, tiled=True),
    )
    copies = spread // stored_experts
    grad_gate, grad_up, grad_down = (
        jnp.sum(
            arrived_term.reshape(stored_experts, copies, stored_rows, hidden_width),
            axis=1,
            dtype=jnp.float32,
        ).astype(jnp.bfloat16)
        for arrived_term in gathered_terms
    )
    returned_back = token_trip(back_rows.reshape(target_count, capacity, model_width)).reshape(
        slot_count, model_width
    )
    back_sum = jnp.sum(
        jnp.where(routed[:, :, None], returned_back[target_safe].astype(jnp.float32), 0.0), axis=1
    )
    is_copy = routes == expert_count + 1
    const_ids = expert_count + 2 + lax.broadcasted_iota(jnp.int32, (1, 1, const_count), 2)
    is_const = routes[:, :, None] == const_ids
    copy_weight = jnp.sum(jnp.where(is_copy, gates_float, 0.0), axis=1)
    const_weight = jnp.sum(jnp.where(is_const, gates_float[:, :, None], 0.0), axis=1)
    const_share = jax.nn.sigmoid(jnp.dot(tokens, const_gate, preferred_element_type=jnp.float32))
    const_rest = (const_weight * (1.0 - const_share)).astype(jnp.bfloat16)
    coefficient = copy_weight + jnp.sum(const_weight * const_share, axis=1)
    tokens_float = tokens.astype(jnp.float32)
    constant_term = jnp.dot(const_rest, const_vec, preferred_element_type=jnp.float32)
    mixed = (mixed_sum + coefficient[:, None] * tokens_float + constant_term).astype(jnp.bfloat16)
    along_token = jnp.sum(cotangent_all * tokens_float, axis=1)
    along_const = lax.dot_general(
        grad_out, const_vec, LAST_CONTRACT, preferred_element_type=jnp.float32
    )
    const_value = const_share * along_token[:, None] + (1.0 - const_share) * along_const
    null_grad = jnp.where(is_copy, along_token[:, None], 0.0) + jnp.sum(
        jnp.where(is_const, const_value[:, None, :], 0.0), axis=2
    )
    pick_grad = routed_grad + null_grad
    slope_grad = pick_grad * chosen * (1.0 - chosen)
    logit_grad = jnp.sum(jnp.where(picks, slope_grad[:, :, None], 0.0), axis=1).astype(jnp.bfloat16)
    share_grad = (
        const_weight * (along_token[:, None] - along_const) * const_share * (1.0 - const_share)
    ).astype(jnp.bfloat16)
    back_local = coefficient[:, None] * cotangent_all
    back_local = back_local + lax.dot_general(
        logit_grad, router, LAST_CONTRACT, preferred_element_type=jnp.float32
    )
    back_local = back_local + lax.dot_general(
        share_grad, const_gate, LAST_CONTRACT, preferred_element_type=jnp.float32
    )
    grad_tokens = (back_sum + back_local).astype(jnp.bfloat16)
    router_part = lax.dot_general(
        tokens, logit_grad, ROWS_CONTRACT, preferred_element_type=jnp.float32
    )
    vector_part = lax.dot_general(
        const_rest, grad_out, ROWS_CONTRACT, preferred_element_type=jnp.float32
    )
    mixing_part = lax.dot_general(
        tokens, share_grad, ROWS_CONTRACT, preferred_element_type=jnp.float32
    )
    grad_router, grad_const_vec, grad_const_gate = lax.psum(
        (router_part, vector_part, mixing_part), ("expert", "dp", "rep")
    )
    mixed_all, grad_tokens_all = (
        lax.all_gather(mixed, "rep", axis=0, tiled=True),
        lax.all_gather(grad_tokens, "rep", axis=0, tiled=True),
    )
    return (
        mixed_all,
        grad_tokens_all,
        grad_gate,
        grad_up,
        grad_down,
        grad_router,
        grad_const_vec,
        grad_const_gate,
    )


HALF = 64
SLOTS = 32
SCRATCH_BYTES = 22 * 1024 * 1024
LONG = 20_000_000_000


def local_kernel(body, scalars, held, operands, outputs, scratch, moved, mark=None):
    marks = [] if mark is None else [mark]

    def kernel(place, *refs):
        body(place, *refs[len(marks) :])

    return pl.pallas_call(
        kernel,
        out_shape=outputs,
        in_specs=[pl.BlockSpec(memory_space=pltpu.SMEM)]
        + [pl.BlockSpec(memory_space=pl.ANY) for _ in marks]
        + [pl.BlockSpec(memory_space=pltpu.VMEM) for _ in held]
        + [pl.BlockSpec(memory_space=pl.ANY) for _ in operands],
        out_specs=[pl.BlockSpec(memory_space=pltpu.VMEM) for _ in outputs],
        scratch_shapes=scratch,
        compiler_params=pltpu.CompilerParams(vmem_limit_bytes=SCRATCH_BYTES),
        cost_estimate=pl.CostEstimate(flops=moved, bytes_accessed=moved, transcendentals=0),
    )(scalars, *marks, *held, *operands)


def bring(pairs, sems):
    copies = [
        pltpu.make_async_copy(source, target, sems.at[i])
        for i, (source, target) in enumerate(pairs)
    ]
    for copy in copies:
        copy.start()
    return copies


def mm(a, b):
    return jnp.dot(a, b, preferred_element_type=jnp.float32)


def mm_rows(a, b):
    return lax.dot_general(a, b, ROWS_CONTRACT, preferred_element_type=jnp.float32)


def mm_last(a, b):
    return lax.dot_general(a, b, LAST_CONTRACT, preferred_element_type=jnp.float32)


def weight_pairs(core, parts, target):
    stored, *fetched = parts
    width = target.shape[0] // 4
    sources = [stored.at[core], *fetched]
    return [(s, target.at[pl.ds(j * width, width)]) for j, s in enumerate(sources)]


def payload_kernel(tokens, grads, routes, router, out, step):
    step[...] = jnp.zeros_like(step)
    count = tokens.shape[0]
    ids = lax.broadcasted_iota(jnp.int32, (router.shape[0], count), 0)
    named = routes[0:1, :] == ids
    for k in range(1, routes.shape[0]):
        named = named | (routes[k : k + 1, :] == ids)
    gates = jnp.where(named, jax.nn.sigmoid(mm_last(router[...], tokens[...])), 0.0)
    out[0:count, :] = tokens[...]
    out[count : 2 * count, :] = grads[...]
    for e in range(out.shape[1] // count):
        out[2 * count :, e * count : (e + 1) * count] = jnp.broadcast_to(
            gates[e : e + 1], (16, count)
        ).astype(jnp.bfloat16)


def step_kernel(before, after_it):
    after_it[...] = before[...]


def next_step(step):
    return pl.pallas_call(
        step_kernel,
        out_shape=jax.ShapeDtypeStruct(step.shape, step.dtype),
        cost_estimate=pl.CostEstimate(flops=LONG, bytes_accessed=LONG, transcendentals=0),
    )(step)


def forward_kernel(place, *refs):
    payloads = refs[0:8]
    gate_weight, up_weight, partner, cross, cross_partner = refs[8:13]
    (pick_out, gate_out, rows_out, cot_out, hidden_out, act_out, slope_out, upstream,
     cross_out) = refs[13:22]
    blocks, w_gate, w_up, sems = refs[22:26]
    me, expert = place[0], place[1]
    core = me & 1
    count = pick_out.shape[1]
    slots = count // HALF * SLOTS
    copies = bring(
        [(payloads[b], blocks.at[b]) for b in range(8)]
        + weight_pairs(core, (gate_weight, partner.at[0], cross.at[0], cross_partner.at[0]), w_gate)
        + weight_pairs(core, (up_weight, partner.at[1], cross.at[1], cross_partner.at[1]), w_up),
        sems,
    )
    width = w_gate.shape[0] // 4
    row = lax.broadcasted_iota(jnp.int32, (count, count), 0)
    column = lax.broadcasted_iota(jnp.int32, (count, count), 1)
    before = ((row < column) & (row // HALF == column // HALF)).astype(jnp.bfloat16)
    lane = lax.broadcasted_iota(jnp.int32, (1, count), 1)
    slot = lax.broadcasted_iota(jnp.int32, (slots, count), 0)
    mine = pl.ds(pl.multiple_of(expert * count, count), count)
    for b in range(8):
        copies[b].wait()
    gates = jnp.concatenate(
        [blocks[b, 2 * count :, mine].astype(jnp.float32)[0:1] for b in range(8)], axis=0
    )
    picked = gates != 0.0
    earlier = mm(picked.astype(jnp.bfloat16), before).astype(jnp.int32)
    target = jnp.where(picked, (lane // HALF) * SLOTS + earlier, -1)
    for b in range(8):
        chosen = slot == target[b : b + 1]
        pick = chosen.astype(jnp.bfloat16)
        gate_pick = jnp.where(chosen, gates[b : b + 1], 0.0)
        gate = jnp.sum(gate_pick, axis=1, keepdims=True)
        at = b * slots
        pick_out[at : at + slots, :] = pick
        gate_out[at : at + slots, :] = gate_pick.astype(jnp.bfloat16)
        for j in range(4):
            columns = pl.ds(pl.multiple_of((me ^ j) * width, width), width)
            here = (slice(at, at + slots), slice(j * width, (j + 1) * width))
            rows_out[here] = mm(pick, blocks[b, 0:count, columns]).astype(jnp.bfloat16)
            cot = mm(pick, blocks[b, count : 2 * count, columns])
            cot_out[here] = cot.astype(jnp.bfloat16)
            upstream[here] = (gate * cot).astype(jnp.bfloat16)
    for copy in copies[8:]:
        copy.wait()
    pre_gate = mm(rows_out[...], w_gate[...])
    pre_up = mm(rows_out[...], w_up[...])
    logistic = jax.nn.sigmoid(pre_gate)
    act = pre_gate * logistic
    hidden_out[...] = (act * pre_up).astype(jnp.bfloat16)
    act_out[...] = act.astype(jnp.bfloat16)
    slope = logistic * (1.0 + pre_gate * (1.0 - logistic))
    slope_out[...] = (pre_up * slope).astype(jnp.bfloat16)
    cross_out[...] = mm_rows(upstream[:, 2 * width : 3 * width], hidden_out[...]).astype(jnp.bfloat16)


def scatter(me, pick, own_out, other_out, column_block):
    width = own_out.shape[1] // 4
    slots = pick.shape[0] // 8
    count = pick.shape[1]
    for j in range(4):
        columns = pl.ds(pl.multiple_of((me ^ j) * width, width), width)
        block = column_block(j, columns).astype(jnp.bfloat16)
        for b in range(8):
            out = own_out if b % 2 == 0 else other_out
            at = b * slots
            out[(b // 2) * count : (b // 2 + 1) * count, columns] = mm_rows(
                pick[at : at + slots, :], block[at : at + slots]
            ).astype(jnp.bfloat16)


def output_kernel(place, *refs):
    gate_pick, hidden, upstream, down_weight, partner, cross, cross_partner = refs[0:7]
    own_out, other_out = refs[7:9]
    outs = refs[9:12]
    w_down, sems = refs[12:14]
    me = place[0]
    copies = bring(
        weight_pairs(me & 1, (down_weight, partner.at[2], cross.at[me & 1], cross_partner), w_down),
        sems,
    )
    width = w_down.shape[0] // 4
    for j, out in zip((0, 1, 3), outs):
        out[...] = mm_rows(
            upstream[:, j * width : (j + 1) * width], hidden[...]
        ).astype(jnp.bfloat16)
    for copy in copies:
        copy.wait()
    scatter(me, gate_pick, own_out, other_out, lambda j, _: (
        mm_last(hidden[...], w_down[j * width : (j + 1) * width])
    ))


def backward_kernel(place, *refs):
    (gate_pick, rows, hidden, cot, act, slope, router,
     down_weight, partner, cross, cross_partner) = refs[0:11]
    (d_gate_out, d_up_out, logit_out, router_out, keep_out, partner_out, cross_partner_out,
     gate_sent, up_sent) = refs[11:20]
    w_down, sems = refs[20:22]
    me, expert = place[0], place[1]
    copies = bring(
        weight_pairs(me & 1, (down_weight, partner.at[2], cross.at[me & 1], cross_partner), w_down),
        sems,
    )
    for copy in copies:
        copy.wait()
    width = w_down.shape[0] // 4
    along = mm(cot[...], w_down[...])
    score = jnp.sum(hidden[...].astype(jnp.float32) * along, axis=1, keepdims=True)
    gate = jnp.sum(gate_pick[...].astype(jnp.float32), axis=1, keepdims=True)
    d_hidden = gate * along
    d_gate_out[...] = (d_hidden * slope[...].astype(jnp.float32)).astype(jnp.bfloat16)
    d_up_out[...] = (d_hidden * act[...].astype(jnp.float32)).astype(jnp.bfloat16)
    gate_outs = (keep_out.at[0], partner_out.at[0], gate_sent, cross_partner_out.at[0])
    up_outs = (keep_out.at[1], partner_out.at[1], up_sent, cross_partner_out.at[1])
    for j in range(4):
        part = rows[:, j * width : (j + 1) * width]
        gate_outs[j][...] = mm_rows(part, d_gate_out[...]).astype(jnp.bfloat16)
        up_outs[j][...] = mm_rows(part, d_up_out[...]).astype(jnp.bfloat16)
    ids = router.shape[0]
    logits = jnp.zeros((gate_pick.shape[0], ids), jnp.float32)
    for j in range(4):
        columns = pl.ds(pl.multiple_of((me ^ j) * width, width), width)
        logits += mm_last(
            rows[:, j * width : (j + 1) * width], router[:, columns].astype(jnp.bfloat16)
        )
    named = lax.broadcasted_iota(jnp.int32, (1, ids), 1) == expert
    share = jax.nn.sigmoid(jnp.sum(jnp.where(named, logits, 0.0), axis=1, keepdims=True))
    slope_grad = jnp.where(gate != 0.0, score * share * (1.0 - share), 0.0)
    logit_grad = jnp.broadcast_to(slope_grad, logit_out.shape).astype(jnp.bfloat16)
    logit_out[...] = logit_grad
    for j in range(4):
        columns = pl.ds(pl.multiple_of((me ^ j) * width, width), width)
        total = mm_rows(logit_grad, rows[:, j * width : (j + 1) * width])
        router_out[:, columns] = total[0 : router_out.shape[0]]


def back_kernel(place, *refs):
    (pick, d_gate, d_up, logit_grad, router, gate_weight, up_weight, partner,
     cross, cross_partner) = refs[0:10]
    own_out, other_out = refs[10:12]
    w_gate, w_up, sems = refs[12:15]
    me, expert = place[0], place[1]
    core = me & 1
    copies = bring(
        weight_pairs(core, (gate_weight, partner.at[0], cross.at[0], cross_partner.at[0]), w_gate)
        + weight_pairs(core, (up_weight, partner.at[1], cross.at[1], cross_partner.at[1]), w_up),
        sems,
    )
    for copy in copies:
        copy.wait()
    width = w_gate.shape[0] // 4
    slope_grad = logit_grad[:, 0:1].astype(jnp.float32)

    def column_block(j, columns):
        here = slice(j * width, (j + 1) * width)
        return (
            mm_last(d_gate[...], w_gate[here])
            + mm_last(d_up[...], w_up[here])
            + slope_grad * router[pl.ds(expert, 1), columns]
        )

    scatter(me, pick, own_out, other_out, column_block)


def dp_swap(value, step):
    return lax.ppermute(value, "dp", [(i, i ^ step) for i in range(4)])


def ring(value, step):
    size = lax.axis_size("expert")
    return lax.ppermute(value, "expert", [(i, (i + step) % size) for i in range(size)])


def after(value, *earlier):
    return lax.optimization_barrier((value, *earlier))[0]


def on_device_paired(
    tokens, routes, gate_weight, up_weight, down_weight, router, const_vec, const_gate, grad_out
):
    bf16, f32 = jnp.bfloat16, jnp.float32
    row_count, model_width = tokens.shape
    id_count = router.shape[1]
    const_count = const_vec.shape[0]
    expert_count = id_count - 2 - const_count
    stored_experts, stored_rows, hidden_width = gate_weight.shape
    me = lax.axis_index("dp")
    z = lax.axis_index("expert")
    core = me % 2
    expert = stored_experts * z + core
    place = jnp.stack([me, expert]).astype(jnp.int32)

    def of_expert(weight, which):
        return lax.dynamic_index_in_dim(weight, which, 0, keepdims=False)

    shape = jax.ShapeDtypeStruct
    vmem = pltpu.VMEM
    slot_count = 4 * row_count
    wide, narrow = (slot_count, model_width), (slot_count, hidden_width)
    table = (slot_count, row_count)
    weight_rows = (stored_rows, hidden_width)
    whole_weight = vmem((model_width, hidden_width), bf16)

    def together(*values):
        return lax.optimization_barrier(values)

    payload, step = pl.pallas_call(
        payload_kernel,
        out_shape=[shape((2 * row_count + 16, model_width), bf16), shape((8, 128), jnp.int32)],
        cost_estimate=pl.CostEstimate(flops=LONG, bytes_accessed=LONG, transcendentals=0),
    )(tokens, grad_out, routes.T, router.T)
    group = lax.axis_index("groups")
    near, payload_partner = ring(payload, 1), dp_swap(payload, 1)
    payload, payload_partner = together(payload, payload_partner)
    far_side = ring(payload, -1)
    in_sent = jnp.where(group == 0, gate_weight, up_weight)
    cut = stored_rows // 8 * 3
    in_came = [dp_swap(in_sent[:, :cut], 2), dp_swap(in_sent[:, cut:], 2)]
    down_cross = dp_swap(after(down_weight, payload_partner), 2)
    in_other = [lax.ppermute(in_came[0], "groups", [(0, 1), (1, 0)])]
    near, in_came[0], step = together(near, in_came[0], step)
    far = ring(near, 1)
    partner = dp_swap(
        jnp.stack([of_expert(w, 1 - core) for w in (gate_weight, up_weight, down_weight)]), 1
    )
    step = next_step(step)
    in_came[1], partner, step = together(in_came[1], partner, step)
    in_other.append(lax.ppermute(in_came[1], "groups", [(0, 1), (1, 0)]))
    step = next_step(step)
    in_other[0], in_other[1], step = together(*in_other, step)
    far_side, far, step = together(far_side, far, step)
    down_cross, step_down = together(down_cross, step)
    near_partner, far_side_partner, far_partner = dp_swap(near, 1), dp_swap(far_side, 1), dp_swap(far, 1)

    def of_core(first, second, which):
        came = jnp.concatenate([of_expert(part, which) for part in first])
        other = jnp.concatenate([of_expert(part, which) for part in second])
        return jnp.where(group == 0, jnp.stack([came, other]), jnp.stack([other, came]))

    in_cross = of_core(in_came, in_other, core)
    in_cross_partner = dp_swap(of_core(in_came, in_other, 1 - core), 1)
    down_cross_partner = dp_swap(of_expert(down_cross, 1 - core), 1)
    payloads = [payload, payload_partner, near, near_partner, far, far_partner, far_side,
                far_side_partner]
    in_weights = [gate_weight, up_weight, partner, in_cross, in_cross_partner]
    router_rows = jnp.pad(router.T.astype(f32), ((0, 16 - id_count), (0, 0)))
    pick, gate_pick, rows, cot, hidden, act, slope, upstream, down_cross_part = local_kernel(
        forward_kernel,
        place,
        [],
        [*payloads, *in_weights],
        [shape(table, bf16)] * 2 + [shape(wide, bf16)] * 2 + [shape(narrow, bf16)] * 3
        + [shape(wide, bf16), shape(weight_rows, bf16)],
        [vmem((8, *payload.shape), bf16), whole_weight, whole_weight,
         pltpu.SemaphoreType.DMA((16,))],
        LONG,
        step,
    )
    hidden, down_cross_partner = together(hidden, down_cross_partner)
    down_weights = [down_weight, partner, down_cross, down_cross_partner]
    def add(one, two):
        return one.astype(f32) + two.astype(f32)

    def sum_slots(own, came):
        return [
            add(mine, theirs).astype(bf16) for mine, theirs in zip(jnp.split(own, 2), came)
        ]

    def pair(mine, theirs):
        of = lax.broadcasted_iota(jnp.int32, (2, 1, 1), 0)
        return jnp.where(of == core, mine[None], theirs[None]).astype(bf16)

    id_range = lax.broadcasted_iota(jnp.int32, (1, 1, id_count), 2)
    named = jnp.any(routes[:, :, None] == id_range, axis=1)[:, expert_count:]
    share = jax.nn.sigmoid(mm(tokens, router[:, expert_count:]))
    gates = jnp.where(named, share, 0.0).astype(bf16).astype(f32)
    tokens_float = tokens.astype(f32)
    grad_float = grad_out.astype(f32)
    copy_weight = gates[:, 1]
    const_weight = gates[:, 2:]
    const_share = jax.nn.sigmoid(mm(tokens, const_gate))
    const_rest = (const_weight * (1.0 - const_share)).astype(bf16)
    coefficient = copy_weight + jnp.sum(const_weight * const_share, axis=1)
    along_token = jnp.sum(grad_float * tokens_float, axis=1, keepdims=True)
    along_const = mm_last(grad_out, const_vec)
    const_value = const_share * along_token + (1.0 - const_share) * along_const
    pick_grad = jnp.concatenate(
        [jnp.zeros_like(along_token), along_token, const_value], axis=1
    )
    null_grad = jnp.where(named, pick_grad * share * (1.0 - share), 0.0).astype(bf16)
    share_grad = (
        const_weight * (along_token - along_const) * const_share * (1.0 - const_share)
    ).astype(bf16)
    mixed_own, mixed_other, *down_parts = local_kernel(
        output_kernel,
        place,
        [gate_pick, hidden, upstream],
        down_weights,
        [shape(wide, bf16)] * 2 + [shape(weight_rows, bf16)] * 3,
        [whole_weight, pltpu.SemaphoreType.DMA((4,))],
        LONG,
        step_down,
    )
    down_came, down_came_partner = dp_swap(down_cross_part, 2), dp_swap(down_parts[2], 3)
    parts = [mixed_other[k * row_count : (k + 1) * row_count] for k in range(4)]
    mixed_came = [dp_swap(parts[2], 1), dp_swap(parts[3], 1)]
    mixed_own, mixed_came[0], mixed_came[1], down_came, cot = together(
        mixed_own, *mixed_came, down_came, cot
    )
    mixed_first = sum_slots(mixed_own[2 * row_count :], mixed_came)
    mixed_near = ring(mixed_first[0], -1)
    mixed_late = dp_swap(mixed_other[: 2 * row_count], 1)
    down_from = dp_swap(down_parts[1], 1)
    d_gate, d_up, logit_grad, router_row, *in_parts, gate_sent, up_sent = local_kernel(
        backward_kernel,
        place,
        [gate_pick, rows, hidden, cot, act, slope, router_rows],
        down_weights,
        [shape(narrow, bf16)] * 2 + [shape(table, bf16), shape((8, model_width), f32)]
        + [shape((2, *weight_rows), bf16)] * 3 + [shape(weight_rows, bf16)] * 2,
        [whole_weight, pltpu.SemaphoreType.DMA((4,))],
        LONG,
    )
    (d_gate, router_row, in_parts[1], in_parts[2], gate_sent, up_sent, down_came_partner,
     mixed_near, mixed_late, down_from) = together(
        d_gate, router_row, in_parts[1], in_parts[2], gate_sent, up_sent, down_came_partner,
        mixed_near, mixed_late, down_from
    )
    mixed_late = sum_slots(mixed_own[: 2 * row_count], jnp.split(mixed_late, 2))
    small = jnp.concatenate(
        [
            mm_rows(jnp.concatenate([null_grad, share_grad], axis=1), tokens),
            mm_rows(const_rest, grad_out),
        ],
        axis=0,
    )
    experts = lax.broadcasted_iota(jnp.int32, (expert_count, 1), 0)
    routed = jnp.where(experts == expert, router_row[0:1], 0.0)
    small = jnp.concatenate([routed, small], axis=0)
    gate_came, in_from, small_came = dp_swap(gate_sent, 2), dp_swap(in_parts[1], 1), dp_swap(small, 2)
    mixed_side = ring(mixed_first[1].astype(bf16), 1)
    mixed_near = ring(add(mixed_near, mixed_late[1]).astype(bf16), -1)
    back_own, back_other = local_kernel(
        back_kernel,
        place,
        [pick, d_gate, d_up, logit_grad, router_rows],
        in_weights,
        [shape(wide, bf16)] * 2,
        [whole_weight, whole_weight, pltpu.SemaphoreType.DMA((8,))],
        LONG,
    )
    (back_own, back_other, gate_came, in_from, small_came, mixed_side, mixed_near, up_sent,
     in_parts[2]) = together(
        back_own, back_other, gate_came, in_from, small_came, mixed_side, mixed_near, up_sent,
        in_parts[2]
    )
    up_came, in_came_partner = dp_swap(up_sent, 2), dp_swap(in_parts[2], 3)
    small = small + small_came
    back_came, small_came = together(dp_swap(back_other, 1), dp_swap(small, 1))
    back_late = sum_slots(back_own[: 2 * row_count], jnp.split(back_came[: 2 * row_count], 2))
    back_first = sum_slots(back_own[2 * row_count :], jnp.split(back_came[2 * row_count :], 2))
    back_near, back_side = ring(back_first[0], -1), ring(back_first[1], 1)
    small = small + small_came
    small_came = lax.ppermute(small, "expert", [(i, i ^ 1) for i in range(4)])
    back_near, back_side, up_came, mixed_near, small_came = together(
        back_near, back_side, up_came, mixed_near, small_came
    )
    back_near = ring(add(back_near, back_late[1]).astype(bf16), -1)
    small = small + small_came
    small = small + lax.ppermute(small, "expert", [(i, i ^ 2) for i in range(4)])
    mixed_sum = add(mixed_side, mixed_near) + mixed_late[0].astype(f32)
    grad_router = small[:id_count].T
    grad_const_gate = small[id_count : id_count + const_count].T
    grad_const_vec = small[id_count + const_count :]
    back_sum = add(back_side, back_near) + back_late[0].astype(f32)
    grad_down = pair(add(down_parts[0], down_came), add(down_from, down_came_partner))
    mixed = (
        mixed_sum + coefficient[:, None] * tokens_float + mm(const_rest, const_vec)
    ).astype(bf16)
    back_local = (
        coefficient[:, None] * grad_float
        + mm_last(null_grad, router[:, expert_count:])
        + mm_last(share_grad, const_gate)
    )
    grad_tokens = (back_sum + back_local).astype(bf16)

    mine = [add(in_parts[0][i], came).astype(bf16) for i, came in enumerate((gate_came, up_came))]
    (mine[0], mine[1], in_came_partner, mixed, grad_down, grad_tokens, grad_router,
     grad_const_gate, grad_const_vec) = together(
        *mine, in_came_partner, mixed, grad_down, grad_tokens, grad_router, grad_const_gate,
        grad_const_vec
    )
    grad_gate, grad_up = (
        pair(mine[i], add(in_from[i], in_came_partner[i])) for i in range(2)
    )
    return (
        mixed,
        grad_tokens,
        grad_gate,
        grad_up,
        grad_down,
        grad_router,
        grad_const_vec,
        grad_const_gate,
    )


def solution(mesh):
    paired = mesh.shape["rep"] == 1 and mesh.shape["dp"] == 4

    def on_device(tokens, routes, gate_weight, *others):
        id_count = others[2].shape[1]
        stored_experts, stored_rows, hidden_width = gate_weight.shape
        row_count, top_count = routes.shape
        halved = row_count * top_count == (row_count // 2) * id_count
        if paired and stored_experts == 2 and halved and row_count == 128:
            return on_device_paired(tokens, routes, gate_weight, *others)
        return on_device_general(tokens, routes, gate_weight, *others)

    placed = (
        P(("groups", "expert", "dp"), None),
        P(("groups", "expert", "dp"), None),
        P("expert", ("dp", "rep"), None),
        P("expert", ("dp", "rep"), None),
        P("expert", ("dp", "rep"), None),
        P(),
        P(),
        P(),
        P(("groups", "expert", "dp"), None),
    )
    return jax.shard_map(
        on_device,
        mesh=mesh,
        in_specs=placed,
        out_specs=(
            P(("groups", "expert", "dp"), None),
            P(("groups", "expert", "dp"), None),
            P(("groups", "expert"), ("dp", "rep"), None),
            P(("groups", "expert"), ("dp", "rep"), None),
            P(("groups", "expert"), ("dp", "rep"), None),
            P("groups", None),
            P("groups", None),
            P("groups", None),
        ),
        check_vma=False,
    )
```

```python
import jax
import jax.numpy as jnp
from jax import lax
from jax.experimental import pallas as pl
from jax.experimental.pallas import tpu as pltpu
from jax.sharding import PartitionSpec as P

ROWS_CONTRACT = (((0,), (0,)), ((), ()))
LAST_CONTRACT = (((1,), (1,)), ((), ()))


def silu_slope(argument):
    logistic = jax.nn.sigmoid(argument)
    return logistic * (1.0 + argument * (1.0 - logistic))


def expert_forward(token_rows, w_gate, w_up, w_down):
    pre_gate = jnp.dot(token_rows, w_gate, preferred_element_type=jnp.float32)
    pre_up = jnp.dot(token_rows, w_up, preferred_element_type=jnp.float32)
    hidden = (jax.nn.silu(pre_gate) * pre_up).astype(jnp.bfloat16)
    output_rows = lax.dot_general(hidden, w_down, LAST_CONTRACT, preferred_element_type=jnp.float32)
    return (output_rows.astype(jnp.bfloat16), hidden, pre_gate, pre_up)


def expert_backward(pre_gate, pre_up, upstream, w_gate, w_up, w_down):
    d_hidden = jnp.dot(upstream, w_down, preferred_element_type=jnp.float32)
    d_gate = (d_hidden * pre_up * silu_slope(pre_gate)).astype(jnp.bfloat16)
    d_up = (d_hidden * jax.nn.silu(pre_gate)).astype(jnp.bfloat16)
    back_rows = lax.dot_general(d_gate, w_gate, LAST_CONTRACT, preferred_element_type=jnp.float32)
    back_rows = back_rows + lax.dot_general(
        d_up, w_up, LAST_CONTRACT, preferred_element_type=jnp.float32
    )
    return (back_rows.astype(jnp.bfloat16), d_gate, d_up)


def block_terms(token_rows, hidden, upstream, d_gate, d_up):
    term_gate = lax.dot_general(
        token_rows, d_gate, ROWS_CONTRACT, preferred_element_type=jnp.float32
    )
    term_up = lax.dot_general(token_rows, d_up, ROWS_CONTRACT, preferred_element_type=jnp.float32)
    term_down = lax.dot_general(upstream, hidden, ROWS_CONTRACT, preferred_element_type=jnp.float32)
    return (term_gate, term_up, term_down)


def token_trip(buffer):
    return lax.all_to_all(buffer, ("expert", "dp"), split_axis=0, concat_axis=0, tiled=True)


def on_device_general(
    tokens, routes, gate_weight, up_weight, down_weight, router, const_vec, const_gate, grad_out
):
    shard_rows, top_count = routes.shape
    row_count = shard_rows // lax.axis_size("rep")
    first_row = lax.axis_index("rep") * row_count
    tokens = lax.dynamic_slice_in_dim(tokens, first_row, row_count, 0)
    routes = lax.dynamic_slice_in_dim(routes, first_row, row_count, 0)
    grad_out = lax.dynamic_slice_in_dim(grad_out, first_row, row_count, 0)
    model_width = tokens.shape[1]
    id_count = router.shape[1]
    const_count = const_vec.shape[0]
    expert_count = id_count - 2 - const_count
    half_rows = row_count // 2
    capacity = (half_rows * top_count + id_count - 1) // id_count
    target_count = lax.axis_size("expert") * lax.axis_size("dp")
    slot_count = target_count * capacity
    stored_experts, stored_rows, hidden_width = gate_weight.shape
    spread = lax.axis_size("dp") * lax.axis_size("rep")
    id_range = lax.broadcasted_iota(jnp.int32, (1, 1, id_count), 2)
    picks = routes[:, :, None] == id_range
    named = jnp.sum(picks.astype(jnp.float32), axis=1)
    row_index = lax.broadcasted_iota(jnp.int32, (row_count, row_count), 0)
    column_index = lax.broadcasted_iota(jnp.int32, (row_count, row_count), 1)
    before = (
        (column_index < row_index) & (column_index // half_rows == row_index // half_rows)
    ).astype(jnp.float32)
    earlier = jnp.dot(before, named, precision=lax.Precision.HIGHEST)
    slot = jnp.sum(jnp.where(picks, earlier[:, None, :], 0.0), axis=2).astype(jnp.int32)
    member = lax.broadcasted_iota(jnp.int32, (row_count, top_count), 0) // half_rows
    routed = routes < expert_count
    target = jnp.where(routed, (2 * routes + member) * capacity + slot, slot_count)
    slot_range = lax.broadcasted_iota(jnp.int32, (slot_count, 1), 0)
    pair_range = lax.broadcasted_iota(jnp.int32, (1, row_count * top_count), 1)
    hits = slot_range == target.reshape(1, -1)
    owner = jnp.sum(jnp.where(hits, pair_range, 0), axis=1)
    filled = jnp.any(hits, axis=1)
    owner_token = owner // top_count
    target_safe = jnp.where(routed, target, 0)
    logits = jnp.dot(tokens, router, preferred_element_type=jnp.float32)
    chosen = jnp.sum(jnp.where(picks, jax.nn.sigmoid(logits)[:, None, :], 0.0), axis=2)
    gates = chosen.astype(jnp.bfloat16)
    gates_float = gates.astype(jnp.float32)
    slot_gate = jnp.where(filled, gates.reshape(-1)[owner], jnp.zeros((), jnp.bfloat16)).astype(
        jnp.float32
    )
    repeat = spread // stored_experts
    fetched = (
        lax.all_to_all(
            jnp.repeat(gate_weight, repeat, axis=0),
            ("dp", "rep"),
            split_axis=0,
            concat_axis=1,
            tiled=True,
        ),
        lax.all_to_all(
            jnp.repeat(up_weight, repeat, axis=0),
            ("dp", "rep"),
            split_axis=0,
            concat_axis=1,
            tiled=True,
        ),
        lax.all_to_all(
            jnp.repeat(down_weight, repeat, axis=0),
            ("dp", "rep"),
            split_axis=0,
            concat_axis=1,
            tiled=True,
        ),
    )
    w_gate = fetched[0].reshape(model_width, hidden_width)
    w_up = fetched[1].reshape(model_width, hidden_width)
    w_down = fetched[2].reshape(model_width, hidden_width)
    send_rows = jnp.where(filled[:, None], tokens[owner_token], jnp.zeros((), jnp.bfloat16))
    arrived = token_trip(send_rows.reshape(target_count, capacity, model_width)).reshape(
        slot_count, model_width
    )
    output_rows, hidden, pre_gate, pre_up = expert_forward(arrived, w_gate, w_up, w_down)
    returned = token_trip(output_rows.reshape(target_count, capacity, model_width)).reshape(
        slot_count, model_width
    )
    picked_out = returned[target_safe].astype(jnp.float32)
    mixed_sum = jnp.sum(
        jnp.where(routed[:, :, None], gates_float[:, :, None] * picked_out, 0.0), axis=1
    )
    cotangent_all = grad_out.astype(jnp.float32)
    routed_grad = jnp.sum(
        jnp.where(routed[:, :, None], picked_out * cotangent_all[:, None, :], 0.0), axis=2
    )
    upstream_send = (slot_gate[:, None] * grad_out[owner_token].astype(jnp.float32)).astype(
        jnp.bfloat16
    )
    upstream = token_trip(upstream_send.reshape(target_count, capacity, model_width)).reshape(
        slot_count, model_width
    )
    back_rows, d_gate, d_up = expert_backward(pre_gate, pre_up, upstream, w_gate, w_up, w_down)
    terms = block_terms(arrived, hidden, upstream, d_gate, d_up)
    sent_terms = tuple(
        (term.astype(jnp.bfloat16).reshape(spread, stored_rows, hidden_width) for term in terms)
    )
    gathered_terms = (
        lax.all_to_all(sent_terms[0], ("dp", "rep"), split_axis=0, concat_axis=0, tiled=True),
        lax.all_to_all(sent_terms[1], ("dp", "rep"), split_axis=0, concat_axis=0, tiled=True),
        lax.all_to_all(sent_terms[2], ("dp", "rep"), split_axis=0, concat_axis=0, tiled=True),
    )
    copies = spread // stored_experts
    grad_gate, grad_up, grad_down = (
        jnp.sum(
            arrived_term.reshape(stored_experts, copies, stored_rows, hidden_width),
            axis=1,
            dtype=jnp.float32,
        ).astype(jnp.bfloat16)
        for arrived_term in gathered_terms
    )
    returned_back = token_trip(back_rows.reshape(target_count, capacity, model_width)).reshape(
        slot_count, model_width
    )
    back_sum = jnp.sum(
        jnp.where(routed[:, :, None], returned_back[target_safe].astype(jnp.float32), 0.0), axis=1
    )
    is_copy = routes == expert_count + 1
    const_ids = expert_count + 2 + lax.broadcasted_iota(jnp.int32, (1, 1, const_count), 2)
    is_const = routes[:, :, None] == const_ids
    copy_weight = jnp.sum(jnp.where(is_copy, gates_float, 0.0), axis=1)
    const_weight = jnp.sum(jnp.where(is_const, gates_float[:, :, None], 0.0), axis=1)
    const_share = jax.nn.sigmoid(jnp.dot(tokens, const_gate, preferred_element_type=jnp.float32))
    const_rest = (const_weight * (1.0 - const_share)).astype(jnp.bfloat16)
    coefficient = copy_weight + jnp.sum(const_weight * const_share, axis=1)
    tokens_float = tokens.astype(jnp.float32)
    constant_term = jnp.dot(const_rest, const_vec, preferred_element_type=jnp.float32)
    mixed = (mixed_sum + coefficient[:, None] * tokens_float + constant_term).astype(jnp.bfloat16)
    along_token = jnp.sum(cotangent_all * tokens_float, axis=1)
    along_const = lax.dot_general(
        grad_out, const_vec, LAST_CONTRACT, preferred_element_type=jnp.float32
    )
    const_value = const_share * along_token[:, None] + (1.0 - const_share) * along_const
    null_grad = jnp.where(is_copy, along_token[:, None], 0.0) + jnp.sum(
        jnp.where(is_const, const_value[:, None, :], 0.0), axis=2
    )
    pick_grad = routed_grad + null_grad
    slope_grad = pick_grad * chosen * (1.0 - chosen)
    logit_grad = jnp.sum(jnp.where(picks, slope_grad[:, :, None], 0.0), axis=1).astype(jnp.bfloat16)
    share_grad = (
        const_weight * (along_token[:, None] - along_const) * const_share * (1.0 - const_share)
    ).astype(jnp.bfloat16)
    back_local = coefficient[:, None] * cotangent_all
    back_local = back_local + lax.dot_general(
        logit_grad, router, LAST_CONTRACT, preferred_element_type=jnp.float32
    )
    back_local = back_local + lax.dot_general(
        share_grad, const_gate, LAST_CONTRACT, preferred_element_type=jnp.float32
    )
    grad_tokens = (back_sum + back_local).astype(jnp.bfloat16)
    router_part = lax.dot_general(
        tokens, logit_grad, ROWS_CONTRACT, preferred_element_type=jnp.float32
    )
    vector_part = lax.dot_general(
        const_rest, grad_out, ROWS_CONTRACT, preferred_element_type=jnp.float32
    )
    mixing_part = lax.dot_general(
        tokens, share_grad, ROWS_CONTRACT, preferred_element_type=jnp.float32
    )
    grad_router, grad_const_vec, grad_const_gate = lax.psum(
        (router_part, vector_part, mixing_part), ("expert", "dp", "rep")
    )
    mixed_all, grad_tokens_all = (
        lax.all_gather(mixed, "rep", axis=0, tiled=True),
        lax.all_gather(grad_tokens, "rep", axis=0, tiled=True),
    )
    return (
        mixed_all,
        grad_tokens_all,
        grad_gate,
        grad_up,
        grad_down,
        grad_router,
        grad_const_vec,
        grad_const_gate,
    )


HALF = 64
SLOTS = 32
SCRATCH_BYTES = 22 * 1024 * 1024
LONG = 20_000_000_000


def local_kernel(body, scalars, held, operands, outputs, scratch, moved, mark=None):
    marks = [] if mark is None else [mark]

    def kernel(place, *refs):
        body(place, *refs[len(marks) :])

    return pl.pallas_call(
        kernel,
        out_shape=outputs,
        in_specs=[pl.BlockSpec(memory_space=pltpu.SMEM)]
        + [pl.BlockSpec(memory_space=pl.ANY) for _ in marks]
        + [pl.BlockSpec(memory_space=pltpu.VMEM) for _ in held]
        + [pl.BlockSpec(memory_space=pl.ANY) for _ in operands],
        out_specs=[pl.BlockSpec(memory_space=pltpu.VMEM) for _ in outputs],
        scratch_shapes=scratch,
        compiler_params=pltpu.CompilerParams(vmem_limit_bytes=SCRATCH_BYTES),
        cost_estimate=pl.CostEstimate(flops=moved, bytes_accessed=moved, transcendentals=0),
    )(scalars, *marks, *held, *operands)


def bring(pairs, sems):
    copies = [
        pltpu.make_async_copy(source, target, sems.at[i])
        for i, (source, target) in enumerate(pairs)
    ]
    for copy in copies:
        copy.start()
    return copies


def mm(a, b):
    return jnp.dot(a, b, preferred_element_type=jnp.float32)


def mm_rows(a, b):
    return lax.dot_general(a, b, ROWS_CONTRACT, preferred_element_type=jnp.float32)


def mm_last(a, b):
    return lax.dot_general(a, b, LAST_CONTRACT, preferred_element_type=jnp.float32)


def weight_pairs(core, parts, target):
    stored, *fetched = parts
    width = target.shape[0] // 4
    sources = [stored.at[core], *fetched]
    return [(s, target.at[pl.ds(j * width, width)]) for j, s in enumerate(sources)]


def payload_kernel(tokens, grads, routes, router, out, step):
    step[...] = jnp.zeros_like(step)
    count = tokens.shape[0]
    ids = lax.broadcasted_iota(jnp.int32, (router.shape[0], count), 0)
    named = routes[0:1, :] == ids
    for k in range(1, routes.shape[0]):
        named = named | (routes[k : k + 1, :] == ids)
    gates = jnp.where(named, jax.nn.sigmoid(mm_last(router[...], tokens[...])), 0.0)
    out[0:count, :] = tokens[...]
    out[count : 2 * count, :] = grads[...]
    for e in range(out.shape[1] // count):
        out[2 * count :, e * count : (e + 1) * count] = jnp.broadcast_to(
            gates[e : e + 1], (16, count)
        ).astype(jnp.bfloat16)


def step_kernel(before, after_it):
    del before, after_it


def next_step(step):
    return pl.pallas_call(
        step_kernel,
        out_shape=jax.ShapeDtypeStruct(step.shape, step.dtype),
        in_specs=[pl.BlockSpec(memory_space=pl.ANY)],
        out_specs=pl.BlockSpec(memory_space=pl.ANY),
        input_output_aliases={0: 0},
        cost_estimate=pl.CostEstimate(flops=LONG, bytes_accessed=LONG, transcendentals=0),
    )(step)


def forward_kernel(place, *refs):
    payloads = refs[0:8]
    gate_weight, up_weight, partner, cross, cross_partner = refs[8:13]
    (pick_out, gate_out, rows_out, cot_out, hidden_out, act_out, slope_out, upstream,
     cross_out) = refs[13:22]
    blocks, w_gate, w_up, sems = refs[22:26]
    me, expert = place[0], place[1]
    core = me & 1
    count = pick_out.shape[1]
    slots = count // HALF * SLOTS
    copies = bring(
        [(payloads[b], blocks.at[b]) for b in range(8)]
        + weight_pairs(core, (gate_weight, partner.at[0], cross.at[0], cross_partner.at[0]), w_gate)
        + weight_pairs(core, (up_weight, partner.at[1], cross.at[1], cross_partner.at[1]), w_up),
        sems,
    )
    width = w_gate.shape[0] // 4
    row = lax.broadcasted_iota(jnp.int32, (count, count), 0)
    column = lax.broadcasted_iota(jnp.int32, (count, count), 1)
    before = ((row < column) & (row // HALF == column // HALF)).astype(jnp.bfloat16)
    lane = lax.broadcasted_iota(jnp.int32, (1, count), 1)
    slot = lax.broadcasted_iota(jnp.int32, (slots, count), 0)
    mine = pl.ds(pl.multiple_of(expert * count, count), count)
    for b in range(8):
        copies[b].wait()
    gates = jnp.concatenate(
        [blocks[b, 2 * count :, mine].astype(jnp.float32)[0:1] for b in range(8)], axis=0
    )
    picked = gates != 0.0
    earlier = mm(picked.astype(jnp.bfloat16), before).astype(jnp.int32)
    target = jnp.where(picked, (lane // HALF) * SLOTS + earlier, -1)
    for b in range(8):
        chosen = slot == target[b : b + 1]
        pick = chosen.astype(jnp.bfloat16)
        gate_pick = jnp.where(chosen, gates[b : b + 1], 0.0)
        gate = jnp.sum(gate_pick, axis=1, keepdims=True)
        at = b * slots
        pick_out[at : at + slots, :] = pick
        gate_out[at : at + slots, :] = gate_pick.astype(jnp.bfloat16)
        for j in range(4):
            columns = pl.ds(pl.multiple_of((me ^ j) * width, width), width)
            here = (slice(at, at + slots), slice(j * width, (j + 1) * width))
            rows_out[here] = mm(pick, blocks[b, 0:count, columns]).astype(jnp.bfloat16)
            cot = mm(pick, blocks[b, count : 2 * count, columns])
            cot_out[here] = cot.astype(jnp.bfloat16)
            upstream[here] = (gate * cot).astype(jnp.bfloat16)
    for copy in copies[8:]:
        copy.wait()
    pre_gate = mm(rows_out[...], w_gate[...])
    pre_up = mm(rows_out[...], w_up[...])
    logistic = jax.nn.sigmoid(pre_gate)
    act = pre_gate * logistic
    hidden_out[...] = (act * pre_up).astype(jnp.bfloat16)
    act_out[...] = act.astype(jnp.bfloat16)
    slope = logistic * (1.0 + pre_gate * (1.0 - logistic))
    slope_out[...] = (pre_up * slope).astype(jnp.bfloat16)
    cross_out[...] = mm_rows(upstream[:, 2 * width : 3 * width], hidden_out[...]).astype(jnp.bfloat16)


def scatter(me, pick, own_out, other_out, column_block):
    width = own_out.shape[1] // 4
    slots = pick.shape[0] // 8
    count = pick.shape[1]
    for j in range(4):
        columns = pl.ds(pl.multiple_of((me ^ j) * width, width), width)
        block = column_block(j, columns).astype(jnp.bfloat16)
        for b in range(8):
            out = own_out if b % 2 == 0 else other_out
            at = b * slots
            out[(b // 2) * count : (b // 2 + 1) * count, columns] = mm_rows(
                pick[at : at + slots, :], block[at : at + slots]
            ).astype(jnp.bfloat16)


def output_kernel(place, *refs):
    gate_pick, hidden, upstream, down_weight, partner, cross, cross_partner = refs[0:7]
    own_out, other_out = refs[7:9]
    outs = refs[9:12]
    w_down, sems = refs[12:14]
    me = place[0]
    copies = bring(
        weight_pairs(me & 1, (down_weight, partner.at[2], cross.at[me & 1], cross_partner), w_down),
        sems,
    )
    width = w_down.shape[0] // 4
    for j, out in zip((0, 1, 3), outs):
        out[...] = mm_rows(
            upstream[:, j * width : (j + 1) * width], hidden[...]
        ).astype(jnp.bfloat16)
    for copy in copies:
        copy.wait()
    scatter(me, gate_pick, own_out, other_out, lambda j, _: (
        mm_last(hidden[...], w_down[j * width : (j + 1) * width])
    ))


def backward_kernel(place, *refs):
    (gate_pick, rows, hidden, cot, act, slope, router,
     down_weight, partner, cross, cross_partner) = refs[0:11]
    (d_gate_out, d_up_out, logit_out, router_out, keep_out, partner_out, cross_partner_out,
     gate_sent, up_sent) = refs[11:20]
    w_down, sems = refs[20:22]
    me, expert = place[0], place[1]
    copies = bring(
        weight_pairs(me & 1, (down_weight, partner.at[2], cross.at[me & 1], cross_partner), w_down),
        sems,
    )
    for copy in copies:
        copy.wait()
    width = w_down.shape[0] // 4
    along = mm(cot[...], w_down[...])
    score = jnp.sum(hidden[...].astype(jnp.float32) * along, axis=1, keepdims=True)
    gate = jnp.sum(gate_pick[...].astype(jnp.float32), axis=1, keepdims=True)
    d_hidden = gate * along
    d_gate_out[...] = (d_hidden * slope[...].astype(jnp.float32)).astype(jnp.bfloat16)
    d_up_out[...] = (d_hidden * act[...].astype(jnp.float32)).astype(jnp.bfloat16)
    gate_outs = (keep_out.at[0], partner_out.at[0], gate_sent, cross_partner_out.at[0])
    up_outs = (keep_out.at[1], partner_out.at[1], up_sent, cross_partner_out.at[1])
    for j in range(4):
        part = rows[:, j * width : (j + 1) * width]
        gate_outs[j][...] = mm_rows(part, d_gate_out[...]).astype(jnp.bfloat16)
        up_outs[j][...] = mm_rows(part, d_up_out[...]).astype(jnp.bfloat16)
    ids = router.shape[0]
    logits = jnp.zeros((gate_pick.shape[0], ids), jnp.float32)
    for j in range(4):
        columns = pl.ds(pl.multiple_of((me ^ j) * width, width), width)
        logits += mm_last(
            rows[:, j * width : (j + 1) * width], router[:, columns].astype(jnp.bfloat16)
        )
    named = lax.broadcasted_iota(jnp.int32, (1, ids), 1) == expert
    share = jax.nn.sigmoid(jnp.sum(jnp.where(named, logits, 0.0), axis=1, keepdims=True))
    slope_grad = jnp.where(gate != 0.0, score * share * (1.0 - share), 0.0)
    logit_grad = jnp.broadcast_to(slope_grad, logit_out.shape).astype(jnp.bfloat16)
    logit_out[...] = logit_grad
    for j in range(4):
        columns = pl.ds(pl.multiple_of((me ^ j) * width, width), width)
        total = mm_rows(logit_grad, rows[:, j * width : (j + 1) * width])
        router_out[:, columns] = total[0 : router_out.shape[0]]


def back_kernel(place, *refs):
    (pick, d_gate, d_up, logit_grad, router, gate_weight, up_weight, partner,
     cross, cross_partner) = refs[0:10]
    own_out, other_out = refs[10:12]
    w_gate, w_up, sems = refs[12:15]
    me, expert = place[0], place[1]
    core = me & 1
    copies = bring(
        weight_pairs(core, (gate_weight, partner.at[0], cross.at[0], cross_partner.at[0]), w_gate)
        + weight_pairs(core, (up_weight, partner.at[1], cross.at[1], cross_partner.at[1]), w_up),
        sems,
    )
    for copy in copies:
        copy.wait()
    width = w_gate.shape[0] // 4
    slope_grad = logit_grad[:, 0:1].astype(jnp.float32)

    def column_block(j, columns):
        here = slice(j * width, (j + 1) * width)
        return (
            mm_last(d_gate[...], w_gate[here])
            + mm_last(d_up[...], w_up[here])
            + slope_grad * router[pl.ds(expert, 1), columns]
        )

    scatter(me, pick, own_out, other_out, column_block)


def dp_swap(value, step):
    return lax.ppermute(value, "dp", [(i, i ^ step) for i in range(4)])


def ring(value, step):
    size = lax.axis_size("expert")
    return lax.ppermute(value, "expert", [(i, (i + step) % size) for i in range(size)])


def after(value, *earlier):
    return lax.optimization_barrier((value, *earlier))[0]


def on_device_paired(
    tokens, routes, gate_weight, up_weight, down_weight, router, const_vec, const_gate, grad_out
):
    bf16, f32 = jnp.bfloat16, jnp.float32
    row_count, model_width = tokens.shape
    id_count = router.shape[1]
    const_count = const_vec.shape[0]
    expert_count = id_count - 2 - const_count
    stored_experts, stored_rows, hidden_width = gate_weight.shape
    me = lax.axis_index("dp")
    z = lax.axis_index("expert")
    core = me % 2
    expert = stored_experts * z + core
    place = jnp.stack([me, expert]).astype(jnp.int32)

    def of_expert(weight, which):
        return lax.dynamic_index_in_dim(weight, which, 0, keepdims=False)

    shape = jax.ShapeDtypeStruct
    vmem = pltpu.VMEM
    slot_count = 4 * row_count
    wide, narrow = (slot_count, model_width), (slot_count, hidden_width)
    table = (slot_count, row_count)
    weight_rows = (stored_rows, hidden_width)
    whole_weight = vmem((model_width, hidden_width), bf16)

    def together(*values):
        return lax.optimization_barrier(values)

    payload, step = pl.pallas_call(
        payload_kernel,
        out_shape=[shape((2 * row_count + 16, model_width), bf16), shape((8, 128), jnp.int32)],
        cost_estimate=pl.CostEstimate(flops=LONG, bytes_accessed=LONG, transcendentals=0),
    )(tokens, grad_out, routes.T, router.T)
    group = lax.axis_index("groups")
    near, payload_partner = ring(payload, 1), dp_swap(payload, 1)
    payload, payload_partner = together(payload, payload_partner)
    far_side = ring(payload, -1)
    in_sent = jnp.where(group == 0, gate_weight, up_weight)
    cut = stored_rows // 8 * 3
    in_came = [dp_swap(in_sent[:, :cut], 2), dp_swap(in_sent[:, cut:], 2)]
    down_cross = dp_swap(after(down_weight, payload_partner), 2)
    in_other = [lax.ppermute(in_came[0], "groups", [(0, 1), (1, 0)])]
    near, in_came[0], step = together(near, in_came[0], step)
    far = ring(near, 1)
    partner = dp_swap(
        jnp.stack([of_expert(w, 1 - core) for w in (gate_weight, up_weight, down_weight)]), 1
    )
    step = next_step(step)
    in_came[1], partner, step = together(in_came[1], partner, step)
    in_other.append(lax.ppermute(in_came[1], "groups", [(0, 1), (1, 0)]))
    step = next_step(step)
    in_other[0], in_other[1], step = together(*in_other, step)
    far_side, far, step = together(far_side, far, step)
    down_cross, step_down = together(down_cross, step)
    near_partner, far_side_partner, far_partner = dp_swap(near, 1), dp_swap(far_side, 1), dp_swap(far, 1)

    def of_core(first, second, which):
        came = jnp.concatenate([of_expert(part, which) for part in first])
        other = jnp.concatenate([of_expert(part, which) for part in second])
        return jnp.where(group == 0, jnp.stack([came, other]), jnp.stack([other, came]))

    in_cross = of_core(in_came, in_other, core)
    in_cross_partner = dp_swap(of_core(in_came, in_other, 1 - core), 1)
    down_cross_partner = dp_swap(of_expert(down_cross, 1 - core), 1)
    payloads = [payload, payload_partner, near, near_partner, far, far_partner, far_side,
                far_side_partner]
    in_weights = [gate_weight, up_weight, partner, in_cross, in_cross_partner]
    router_rows = jnp.pad(router.T.astype(f32), ((0, 16 - id_count), (0, 0)))
    pick, gate_pick, rows, cot, hidden, act, slope, upstream, down_cross_part = local_kernel(
        forward_kernel,
        place,
        [],
        [*payloads, *in_weights],
        [shape(table, bf16)] * 2 + [shape(wide, bf16)] * 2 + [shape(narrow, bf16)] * 3
        + [shape(wide, bf16), shape(weight_rows, bf16)],
        [vmem((8, *payload.shape), bf16), whole_weight, whole_weight,
         pltpu.SemaphoreType.DMA((16,))],
        LONG,
        step,
    )
    hidden, down_cross_partner = together(hidden, down_cross_partner)
    down_weights = [down_weight, partner, down_cross, down_cross_partner]
    def add(one, two):
        return one.astype(f32) + two.astype(f32)

    def sum_slots(own, came):
        return [
            add(mine, theirs).astype(bf16) for mine, theirs in zip(jnp.split(own, 2), came)
        ]

    def pair(mine, theirs):
        of = lax.broadcasted_iota(jnp.int32, (2, 1, 1), 0)
        return jnp.where(of == core, mine[None], theirs[None]).astype(bf16)

    id_range = lax.broadcasted_iota(jnp.int32, (1, 1, id_count), 2)
    named = jnp.any(routes[:, :, None] == id_range, axis=1)[:, expert_count:]
    share = jax.nn.sigmoid(mm(tokens, router[:, expert_count:]))
    gates = jnp.where(named, share, 0.0).astype(bf16).astype(f32)
    tokens_float = tokens.astype(f32)
    grad_float = grad_out.astype(f32)
    copy_weight = gates[:, 1]
    const_weight = gates[:, 2:]
    const_share = jax.nn.sigmoid(mm(tokens, const_gate))
    const_rest = (const_weight * (1.0 - const_share)).astype(bf16)
    coefficient = copy_weight + jnp.sum(const_weight * const_share, axis=1)
    along_token = jnp.sum(grad_float * tokens_float, axis=1, keepdims=True)
    along_const = mm_last(grad_out, const_vec)
    const_value = const_share * along_token + (1.0 - const_share) * along_const
    pick_grad = jnp.concatenate(
        [jnp.zeros_like(along_token), along_token, const_value], axis=1
    )
    null_grad = jnp.where(named, pick_grad * share * (1.0 - share), 0.0).astype(bf16)
    share_grad = (
        const_weight * (along_token - along_const) * const_share * (1.0 - const_share)
    ).astype(bf16)
    mixed_own, mixed_other, *down_parts = local_kernel(
        output_kernel,
        place,
        [gate_pick, hidden, upstream],
        down_weights,
        [shape(wide, bf16)] * 2 + [shape(weight_rows, bf16)] * 3,
        [whole_weight, pltpu.SemaphoreType.DMA((4,))],
        LONG,
        step_down,
    )
    down_came, down_came_partner = dp_swap(down_cross_part, 2), dp_swap(down_parts[2], 3)
    parts = [mixed_other[k * row_count : (k + 1) * row_count] for k in range(4)]
    mixed_came = [dp_swap(parts[2], 1), dp_swap(parts[3], 1)]
    mixed_own, mixed_came[0], mixed_came[1], down_came, cot = together(
        mixed_own, *mixed_came, down_came, cot
    )
    mixed_first = sum_slots(mixed_own[2 * row_count :], mixed_came)
    mixed_near = ring(mixed_first[0], -1)
    mixed_late = dp_swap(mixed_other[: 2 * row_count], 1)
    down_from = dp_swap(down_parts[1], 1)
    d_gate, d_up, logit_grad, router_row, *in_parts, gate_sent, up_sent = local_kernel(
        backward_kernel,
        place,
        [gate_pick, rows, hidden, cot, act, slope, router_rows],
        down_weights,
        [shape(narrow, bf16)] * 2 + [shape(table, bf16), shape((8, model_width), f32)]
        + [shape((2, *weight_rows), bf16)] * 3 + [shape(weight_rows, bf16)] * 2,
        [whole_weight, pltpu.SemaphoreType.DMA((4,))],
        LONG,
    )
    (d_gate, router_row, in_parts[1], in_parts[2], gate_sent, up_sent, down_came_partner,
     mixed_near, mixed_late, down_from) = together(
        d_gate, router_row, in_parts[1], in_parts[2], gate_sent, up_sent, down_came_partner,
        mixed_near, mixed_late, down_from
    )
    mixed_late = sum_slots(mixed_own[: 2 * row_count], jnp.split(mixed_late, 2))
    small = jnp.concatenate(
        [
            mm_rows(jnp.concatenate([null_grad, share_grad], axis=1), tokens),
            mm_rows(const_rest, grad_out),
        ],
        axis=0,
    )
    experts = lax.broadcasted_iota(jnp.int32, (expert_count, 1), 0)
    routed = jnp.where(experts == expert, router_row[0:1], 0.0)
    small = jnp.concatenate([routed, small], axis=0)
    gate_came, in_from, small_came = dp_swap(gate_sent, 2), dp_swap(in_parts[1], 1), dp_swap(small, 2)
    mixed_side = ring(mixed_first[1].astype(bf16), 1)
    mixed_near = ring(add(mixed_near, mixed_late[1]).astype(bf16), -1)
    back_own, back_other = local_kernel(
        back_kernel,
        place,
        [pick, d_gate, d_up, logit_grad, router_rows],
        in_weights,
        [shape(wide, bf16)] * 2,
        [whole_weight, whole_weight, pltpu.SemaphoreType.DMA((8,))],
        LONG,
    )
    (back_own, back_other, gate_came, in_from, small_came, mixed_side, mixed_near, up_sent,
     in_parts[2]) = together(
        back_own, back_other, gate_came, in_from, small_came, mixed_side, mixed_near, up_sent,
        in_parts[2]
    )
    up_came, in_came_partner = dp_swap(up_sent, 2), dp_swap(in_parts[2], 3)
    small = small + small_came
    back_came, small_came = together(dp_swap(back_other, 1), dp_swap(small, 1))
    back_late = sum_slots(back_own[: 2 * row_count], jnp.split(back_came[: 2 * row_count], 2))
    back_first = sum_slots(back_own[2 * row_count :], jnp.split(back_came[2 * row_count :], 2))
    back_near, back_side = ring(back_first[0], -1), ring(back_first[1], 1)
    small = small + small_came
    small_came = lax.ppermute(small, "expert", [(i, i ^ 1) for i in range(4)])
    back_near, back_side, up_came, mixed_near, small_came = together(
        back_near, back_side, up_came, mixed_near, small_came
    )
    back_near = ring(add(back_near, back_late[1]).astype(bf16), -1)
    small = small + small_came
    small = small + lax.ppermute(small, "expert", [(i, i ^ 2) for i in range(4)])
    mixed_sum = add(mixed_side, mixed_near) + mixed_late[0].astype(f32)
    grad_router = small[:id_count].T
    grad_const_gate = small[id_count : id_count + const_count].T
    grad_const_vec = small[id_count + const_count :]
    back_sum = add(back_side, back_near) + back_late[0].astype(f32)
    grad_down = pair(add(down_parts[0], down_came), add(down_from, down_came_partner))
    mixed = (
        mixed_sum + coefficient[:, None] * tokens_float + mm(const_rest, const_vec)
    ).astype(bf16)
    back_local = (
        coefficient[:, None] * grad_float
        + mm_last(null_grad, router[:, expert_count:])
        + mm_last(share_grad, const_gate)
    )
    grad_tokens = (back_sum + back_local).astype(bf16)

    mine = [add(in_parts[0][i], came).astype(bf16) for i, came in enumerate((gate_came, up_came))]
    (mine[0], mine[1], in_came_partner, mixed, grad_down, grad_tokens, grad_router,
     grad_const_gate, grad_const_vec) = together(
        *mine, in_came_partner, mixed, grad_down, grad_tokens, grad_router, grad_const_gate,
        grad_const_vec
    )
    grad_gate, grad_up = (
        pair(mine[i], add(in_from[i], in_came_partner[i])) for i in range(2)
    )
    return (
        mixed,
        grad_tokens,
        grad_gate,
        grad_up,
        grad_down,
        grad_router,
        grad_const_vec,
        grad_const_gate,
    )


def solution(mesh):
    paired = mesh.shape["rep"] == 1 and mesh.shape["dp"] == 4

    def on_device(tokens, routes, gate_weight, *others):
        id_count = others[2].shape[1]
        stored_experts, stored_rows, hidden_width = gate_weight.shape
        row_count, top_count = routes.shape
        halved = row_count * top_count == (row_count // 2) * id_count
        if paired and stored_experts == 2 and halved and row_count == 128:
            return on_device_paired(tokens, routes, gate_weight, *others)
        return on_device_general(tokens, routes, gate_weight, *others)

    placed = (
        P(("groups", "expert", "dp"), None),
        P(("groups", "expert", "dp"), None),
        P("expert", ("dp", "rep"), None),
        P("expert", ("dp", "rep"), None),
        P("expert", ("dp", "rep"), None),
        P(),
        P(),
        P(),
        P(("groups", "expert", "dp"), None),
    )
    return jax.shard_map(
        on_device,
        mesh=mesh,
        in_specs=placed,
        out_specs=(
            P(("groups", "expert", "dp"), None),
            P(("groups", "expert", "dp"), None),
            P(("groups", "expert"), ("dp", "rep"), None),
            P(("groups", "expert"), ("dp", "rep"), None),
            P(("groups", "expert"), ("dp", "rep"), None),
            P("groups", None),
            P("groups", None),
            P("groups", None),
        ),
        check_vma=False,
    )
```

```python
import jax
import jax.numpy as jnp
from jax import lax
from jax.experimental import pallas as pl
from jax.experimental.pallas import tpu as pltpu
from jax.sharding import PartitionSpec as P

ROWS_CONTRACT = (((0,), (0,)), ((), ()))
LAST_CONTRACT = (((1,), (1,)), ((), ()))


def silu_slope(argument):
    logistic = jax.nn.sigmoid(argument)
    return logistic * (1.0 + argument * (1.0 - logistic))


def expert_forward(token_rows, w_gate, w_up, w_down):
    pre_gate = jnp.dot(token_rows, w_gate, preferred_element_type=jnp.float32)
    pre_up = jnp.dot(token_rows, w_up, preferred_element_type=jnp.float32)
    hidden = (jax.nn.silu(pre_gate) * pre_up).astype(jnp.bfloat16)
    output_rows = lax.dot_general(hidden, w_down, LAST_CONTRACT, preferred_element_type=jnp.float32)
    return (output_rows.astype(jnp.bfloat16), hidden, pre_gate, pre_up)


def expert_backward(pre_gate, pre_up, upstream, w_gate, w_up, w_down):
    d_hidden = jnp.dot(upstream, w_down, preferred_element_type=jnp.float32)
    d_gate = (d_hidden * pre_up * silu_slope(pre_gate)).astype(jnp.bfloat16)
    d_up = (d_hidden * jax.nn.silu(pre_gate)).astype(jnp.bfloat16)
    back_rows = lax.dot_general(d_gate, w_gate, LAST_CONTRACT, preferred_element_type=jnp.float32)
    back_rows = back_rows + lax.dot_general(
        d_up, w_up, LAST_CONTRACT, preferred_element_type=jnp.float32
    )
    return (back_rows.astype(jnp.bfloat16), d_gate, d_up)


def block_terms(token_rows, hidden, upstream, d_gate, d_up):
    term_gate = lax.dot_general(
        token_rows, d_gate, ROWS_CONTRACT, preferred_element_type=jnp.float32
    )
    term_up = lax.dot_general(token_rows, d_up, ROWS_CONTRACT, preferred_element_type=jnp.float32)
    term_down = lax.dot_general(upstream, hidden, ROWS_CONTRACT, preferred_element_type=jnp.float32)
    return (term_gate, term_up, term_down)


def token_trip(buffer):
    return lax.all_to_all(buffer, ("expert", "dp"), split_axis=0, concat_axis=0, tiled=True)


def on_device_general(
    tokens, routes, gate_weight, up_weight, down_weight, router, const_vec, const_gate, grad_out
):
    shard_rows, top_count = routes.shape
    row_count = shard_rows // lax.axis_size("rep")
    first_row = lax.axis_index("rep") * row_count
    tokens = lax.dynamic_slice_in_dim(tokens, first_row, row_count, 0)
    routes = lax.dynamic_slice_in_dim(routes, first_row, row_count, 0)
    grad_out = lax.dynamic_slice_in_dim(grad_out, first_row, row_count, 0)
    model_width = tokens.shape[1]
    id_count = router.shape[1]
    const_count = const_vec.shape[0]
    expert_count = id_count - 2 - const_count
    half_rows = row_count // 2
    capacity = (half_rows * top_count + id_count - 1) // id_count
    target_count = lax.axis_size("expert") * lax.axis_size("dp")
    slot_count = target_count * capacity
    stored_experts, stored_rows, hidden_width = gate_weight.shape
    spread = lax.axis_size("dp") * lax.axis_size("rep")
    id_range = lax.broadcasted_iota(jnp.int32, (1, 1, id_count), 2)
    picks = routes[:, :, None] == id_range
    named = jnp.sum(picks.astype(jnp.float32), axis=1)
    row_index = lax.broadcasted_iota(jnp.int32, (row_count, row_count), 0)
    column_index = lax.broadcasted_iota(jnp.int32, (row_count, row_count), 1)
    before = (
        (column_index < row_index) & (column_index // half_rows == row_index // half_rows)
    ).astype(jnp.float32)
    earlier = jnp.dot(before, named, precision=lax.Precision.HIGHEST)
    slot = jnp.sum(jnp.where(picks, earlier[:, None, :], 0.0), axis=2).astype(jnp.int32)
    member = lax.broadcasted_iota(jnp.int32, (row_count, top_count), 0) // half_rows
    routed = routes < expert_count
    target = jnp.where(routed, (2 * routes + member) * capacity + slot, slot_count)
    slot_range = lax.broadcasted_iota(jnp.int32, (slot_count, 1), 0)
    pair_range = lax.broadcasted_iota(jnp.int32, (1, row_count * top_count), 1)
    hits = slot_range == target.reshape(1, -1)
    owner = jnp.sum(jnp.where(hits, pair_range, 0), axis=1)
    filled = jnp.any(hits, axis=1)
    owner_token = owner // top_count
    target_safe = jnp.where(routed, target, 0)
    logits = jnp.dot(tokens, router, preferred_element_type=jnp.float32)
    chosen = jnp.sum(jnp.where(picks, jax.nn.sigmoid(logits)[:, None, :], 0.0), axis=2)
    gates = chosen.astype(jnp.bfloat16)
    gates_float = gates.astype(jnp.float32)
    slot_gate = jnp.where(filled, gates.reshape(-1)[owner], jnp.zeros((), jnp.bfloat16)).astype(
        jnp.float32
    )
    repeat = spread // stored_experts
    fetched = (
        lax.all_to_all(
            jnp.repeat(gate_weight, repeat, axis=0),
            ("dp", "rep"),
            split_axis=0,
            concat_axis=1,
            tiled=True,
        ),
        lax.all_to_all(
            jnp.repeat(up_weight, repeat, axis=0),
            ("dp", "rep"),
            split_axis=0,
            concat_axis=1,
            tiled=True,
        ),
        lax.all_to_all(
            jnp.repeat(down_weight, repeat, axis=0),
            ("dp", "rep"),
            split_axis=0,
            concat_axis=1,
            tiled=True,
        ),
    )
    w_gate = fetched[0].reshape(model_width, hidden_width)
    w_up = fetched[1].reshape(model_width, hidden_width)
    w_down = fetched[2].reshape(model_width, hidden_width)
    send_rows = jnp.where(filled[:, None], tokens[owner_token], jnp.zeros((), jnp.bfloat16))
    arrived = token_trip(send_rows.reshape(target_count, capacity, model_width)).reshape(
        slot_count, model_width
    )
    output_rows, hidden, pre_gate, pre_up = expert_forward(arrived, w_gate, w_up, w_down)
    returned = token_trip(output_rows.reshape(target_count, capacity, model_width)).reshape(
        slot_count, model_width
    )
    picked_out = returned[target_safe].astype(jnp.float32)
    mixed_sum = jnp.sum(
        jnp.where(routed[:, :, None], gates_float[:, :, None] * picked_out, 0.0), axis=1
    )
    cotangent_all = grad_out.astype(jnp.float32)
    routed_grad = jnp.sum(
        jnp.where(routed[:, :, None], picked_out * cotangent_all[:, None, :], 0.0), axis=2
    )
    upstream_send = (slot_gate[:, None] * grad_out[owner_token].astype(jnp.float32)).astype(
        jnp.bfloat16
    )
    upstream = token_trip(upstream_send.reshape(target_count, capacity, model_width)).reshape(
        slot_count, model_width
    )
    back_rows, d_gate, d_up = expert_backward(pre_gate, pre_up, upstream, w_gate, w_up, w_down)
    terms = block_terms(arrived, hidden, upstream, d_gate, d_up)
    sent_terms = tuple(
        (term.astype(jnp.bfloat16).reshape(spread, stored_rows, hidden_width) for term in terms)
    )
    gathered_terms = (
        lax.all_to_all(sent_terms[0], ("dp", "rep"), split_axis=0, concat_axis=0, tiled=True),
        lax.all_to_all(sent_terms[1], ("dp", "rep"), split_axis=0, concat_axis=0, tiled=True),
        lax.all_to_all(sent_terms[2], ("dp", "rep"), split_axis=0, concat_axis=0, tiled=True),
    )
    copies = spread // stored_experts
    grad_gate, grad_up, grad_down = (
        jnp.sum(
            arrived_term.reshape(stored_experts, copies, stored_rows, hidden_width),
            axis=1,
            dtype=jnp.float32,
        ).astype(jnp.bfloat16)
        for arrived_term in gathered_terms
    )
    returned_back = token_trip(back_rows.reshape(target_count, capacity, model_width)).reshape(
        slot_count, model_width
    )
    back_sum = jnp.sum(
        jnp.where(routed[:, :, None], returned_back[target_safe].astype(jnp.float32), 0.0), axis=1
    )
    is_copy = routes == expert_count + 1
    const_ids = expert_count + 2 + lax.broadcasted_iota(jnp.int32, (1, 1, const_count), 2)
    is_const = routes[:, :, None] == const_ids
    copy_weight = jnp.sum(jnp.where(is_copy, gates_float, 0.0), axis=1)
    const_weight = jnp.sum(jnp.where(is_const, gates_float[:, :, None], 0.0), axis=1)
    const_share = jax.nn.sigmoid(jnp.dot(tokens, const_gate, preferred_element_type=jnp.float32))
    const_rest = (const_weight * (1.0 - const_share)).astype(jnp.bfloat16)
    coefficient = copy_weight + jnp.sum(const_weight * const_share, axis=1)
    tokens_float = tokens.astype(jnp.float32)
    constant_term = jnp.dot(const_rest, const_vec, preferred_element_type=jnp.float32)
    mixed = (mixed_sum + coefficient[:, None] * tokens_float + constant_term).astype(jnp.bfloat16)
    along_token = jnp.sum(cotangent_all * tokens_float, axis=1)
    along_const = lax.dot_general(
        grad_out, const_vec, LAST_CONTRACT, preferred_element_type=jnp.float32
    )
    const_value = const_share * along_token[:, None] + (1.0 - const_share) * along_const
    null_grad = jnp.where(is_copy, along_token[:, None], 0.0) + jnp.sum(
        jnp.where(is_const, const_value[:, None, :], 0.0), axis=2
    )
    pick_grad = routed_grad + null_grad
    slope_grad = pick_grad * chosen * (1.0 - chosen)
    logit_grad = jnp.sum(jnp.where(picks, slope_grad[:, :, None], 0.0), axis=1).astype(jnp.bfloat16)
    share_grad = (
        const_weight * (along_token[:, None] - along_const) * const_share * (1.0 - const_share)
    ).astype(jnp.bfloat16)
    back_local = coefficient[:, None] * cotangent_all
    back_local = back_local + lax.dot_general(
        logit_grad, router, LAST_CONTRACT, preferred_element_type=jnp.float32
    )
    back_local = back_local + lax.dot_general(
        share_grad, const_gate, LAST_CONTRACT, preferred_element_type=jnp.float32
    )
    grad_tokens = (back_sum + back_local).astype(jnp.bfloat16)
    router_part = lax.dot_general(
        tokens, logit_grad, ROWS_CONTRACT, preferred_element_type=jnp.float32
    )
    vector_part = lax.dot_general(
        const_rest, grad_out, ROWS_CONTRACT, preferred_element_type=jnp.float32
    )
    mixing_part = lax.dot_general(
        tokens, share_grad, ROWS_CONTRACT, preferred_element_type=jnp.float32
    )
    grad_router, grad_const_vec, grad_const_gate = lax.psum(
        (router_part, vector_part, mixing_part), ("expert", "dp", "rep")
    )
    mixed_all, grad_tokens_all = (
        lax.all_gather(mixed, "rep", axis=0, tiled=True),
        lax.all_gather(grad_tokens, "rep", axis=0, tiled=True),
    )
    return (
        mixed_all,
        grad_tokens_all,
        grad_gate,
        grad_up,
        grad_down,
        grad_router,
        grad_const_vec,
        grad_const_gate,
    )


HALF = 64
SLOTS = 32
SCRATCH_BYTES = 22 * 1024 * 1024
LONG = 20_000_000_000


def local_kernel(body, scalars, held, operands, outputs, scratch, moved, mark=None):
    marks = [] if mark is None else [mark]

    def kernel(place, *refs):
        body(place, *refs[len(marks) :])

    return pl.pallas_call(
        kernel,
        out_shape=outputs,
        in_specs=[pl.BlockSpec(memory_space=pltpu.SMEM)]
        + [pl.BlockSpec(memory_space=pl.ANY) for _ in marks]
        + [pl.BlockSpec(memory_space=pltpu.VMEM) for _ in held]
        + [pl.BlockSpec(memory_space=pl.ANY) for _ in operands],
        out_specs=[pl.BlockSpec(memory_space=pltpu.VMEM) for _ in outputs],
        scratch_shapes=scratch,
        compiler_params=pltpu.CompilerParams(vmem_limit_bytes=SCRATCH_BYTES),
        cost_estimate=pl.CostEstimate(flops=moved, bytes_accessed=moved, transcendentals=0),
    )(scalars, *marks, *held, *operands)


def bring(pairs, sems):
    copies = [
        pltpu.make_async_copy(source, target, sems.at[i])
        for i, (source, target) in enumerate(pairs)
    ]
    for copy in copies:
        copy.start()
    return copies


def mm(a, b):
    return jnp.dot(a, b, preferred_element_type=jnp.float32)


def mm_rows(a, b):
    return lax.dot_general(a, b, ROWS_CONTRACT, preferred_element_type=jnp.float32)


def mm_last(a, b):
    return lax.dot_general(a, b, LAST_CONTRACT, preferred_element_type=jnp.float32)


def weight_pairs(core, parts, target):
    stored, *fetched = parts
    width = target.shape[0] // 4
    sources = [stored.at[core], *fetched]
    return [(s, target.at[pl.ds(j * width, width)]) for j, s in enumerate(sources)]


def payload_kernel(tokens, grads, routes, router, out, step):
    step[...] = jnp.zeros_like(step)
    count = tokens.shape[0]
    ids = lax.broadcasted_iota(jnp.int32, (router.shape[0], count), 0)
    named = routes[0:1, :] == ids
    for k in range(1, routes.shape[0]):
        named = named | (routes[k : k + 1, :] == ids)
    gates = jnp.where(named, jax.nn.sigmoid(mm_last(router[...], tokens[...])), 0.0)
    out[0:count, :] = tokens[...]
    out[count : 2 * count, :] = grads[...]
    for e in range(out.shape[1] // count):
        out[2 * count :, e * count : (e + 1) * count] = jnp.broadcast_to(
            gates[e : e + 1], (16, count)
        ).astype(jnp.bfloat16)


def step_kernel(before, after_it):
    del before, after_it


def next_step(step):
    return pl.pallas_call(
        step_kernel,
        out_shape=jax.ShapeDtypeStruct(step.shape, step.dtype),
        in_specs=[pl.BlockSpec(memory_space=pl.ANY)],
        out_specs=pl.BlockSpec(memory_space=pl.ANY),
        input_output_aliases={0: 0},
        cost_estimate=pl.CostEstimate(flops=LONG, bytes_accessed=LONG, transcendentals=0),
    )(step)


def forward_kernel(place, *refs):
    payloads = refs[0:8]
    gate_weight, up_weight, partner, cross, cross_partner = refs[8:13]
    (pick_out, gate_out, rows_out, cot_out, hidden_out, act_out, slope_out, upstream,
     cross_out) = refs[13:22]
    blocks, w_gate, w_up, sems = refs[22:26]
    me, expert = place[0], place[1]
    core = me & 1
    count = pick_out.shape[1]
    slots = count // HALF * SLOTS
    copies = bring(
        [(payloads[b], blocks.at[b]) for b in range(8)]
        + weight_pairs(core, (gate_weight, partner.at[0], cross.at[0], cross_partner.at[0]), w_gate)
        + weight_pairs(core, (up_weight, partner.at[1], cross.at[1], cross_partner.at[1]), w_up),
        sems,
    )
    width = w_gate.shape[0] // 4
    row = lax.broadcasted_iota(jnp.int32, (count, count), 0)
    column = lax.broadcasted_iota(jnp.int32, (count, count), 1)
    before = ((row < column) & (row // HALF == column // HALF)).astype(jnp.bfloat16)
    lane = lax.broadcasted_iota(jnp.int32, (1, count), 1)
    slot = lax.broadcasted_iota(jnp.int32, (slots, count), 0)
    mine = pl.ds(pl.multiple_of(expert * count, count), count)
    for b in range(8):
        copies[b].wait()
    gates = jnp.concatenate(
        [blocks[b, 2 * count :, mine].astype(jnp.float32)[0:1] for b in range(8)], axis=0
    )
    picked = gates != 0.0
    earlier = mm(picked.astype(jnp.bfloat16), before).astype(jnp.int32)
    target = jnp.where(picked, (lane // HALF) * SLOTS + earlier, -1)
    for b in range(8):
        chosen = slot == target[b : b + 1]
        pick = chosen.astype(jnp.bfloat16)
        gate_pick = jnp.where(chosen, gates[b : b + 1], 0.0)
        gate = jnp.sum(gate_pick, axis=1, keepdims=True)
        at = b * slots
        pick_out[at : at + slots, :] = pick
        gate_out[at : at + slots, :] = gate_pick.astype(jnp.bfloat16)
        for j in range(4):
            columns = pl.ds(pl.multiple_of((me ^ j) * width, width), width)
            here = (slice(at, at + slots), slice(j * width, (j + 1) * width))
            rows_out[here] = mm(pick, blocks[b, 0:count, columns]).astype(jnp.bfloat16)
            cot = mm(pick, blocks[b, count : 2 * count, columns])
            cot_out[here] = cot.astype(jnp.bfloat16)
            upstream[here] = (gate * cot).astype(jnp.bfloat16)
    for copy in copies[8:]:
        copy.wait()
    pre_gate = mm(rows_out[...], w_gate[...])
    pre_up = mm(rows_out[...], w_up[...])
    logistic = jax.nn.sigmoid(pre_gate)
    act = pre_gate * logistic
    hidden_out[...] = (act * pre_up).astype(jnp.bfloat16)
    act_out[...] = act.astype(jnp.bfloat16)
    slope = logistic * (1.0 + pre_gate * (1.0 - logistic))
    slope_out[...] = (pre_up * slope).astype(jnp.bfloat16)
    cross_out[...] = mm_rows(upstream[:, 2 * width : 3 * width], hidden_out[...]).astype(jnp.bfloat16)


def scatter(me, pick, own_out, other_out, column_block):
    width = own_out.shape[1] // 4
    slots = pick.shape[0] // 8
    count = pick.shape[1]
    for j in range(4):
        columns = pl.ds(pl.multiple_of((me ^ j) * width, width), width)
        block = column_block(j, columns).astype(jnp.bfloat16)
        for b in range(8):
            out = own_out if b % 2 == 0 else other_out
            at = b * slots
            out[(b // 2) * count : (b // 2 + 1) * count, columns] = mm_rows(
                pick[at : at + slots, :], block[at : at + slots]
            ).astype(jnp.bfloat16)


def output_kernel(place, *refs):
    gate_pick, hidden, upstream, down_weight, partner, cross, cross_partner = refs[0:7]
    own_out, other_out = refs[7:9]
    outs = refs[9:12]
    w_down, sems = refs[12:14]
    me = place[0]
    copies = bring(
        weight_pairs(me & 1, (down_weight, partner.at[2], cross.at[me & 1], cross_partner), w_down),
        sems,
    )
    width = w_down.shape[0] // 4
    for j, out in zip((0, 1, 3), outs):
        out[...] = mm_rows(
            upstream[:, j * width : (j + 1) * width], hidden[...]
        ).astype(jnp.bfloat16)
    for copy in copies:
        copy.wait()
    scatter(me, gate_pick, own_out, other_out, lambda j, _: (
        mm_last(hidden[...], w_down[j * width : (j + 1) * width])
    ))


def backward_kernel(place, *refs):
    (gate_pick, rows, hidden, cot, act, slope, router,
     down_weight, partner, cross, cross_partner) = refs[0:11]
    (d_gate_out, d_up_out, logit_out, router_out, keep_out, partner_out, cross_partner_out,
     gate_sent, up_sent) = refs[11:20]
    w_down, sems = refs[20:22]
    me, expert = place[0], place[1]
    copies = bring(
        weight_pairs(me & 1, (down_weight, partner.at[2], cross.at[me & 1], cross_partner), w_down),
        sems,
    )
    for copy in copies:
        copy.wait()
    width = w_down.shape[0] // 4
    along = mm(cot[...], w_down[...])
    score = jnp.sum(hidden[...].astype(jnp.float32) * along, axis=1, keepdims=True)
    gate = jnp.sum(gate_pick[...].astype(jnp.float32), axis=1, keepdims=True)
    d_hidden = gate * along
    d_gate_out[...] = (d_hidden * slope[...].astype(jnp.float32)).astype(jnp.bfloat16)
    d_up_out[...] = (d_hidden * act[...].astype(jnp.float32)).astype(jnp.bfloat16)
    gate_outs = (keep_out.at[0], partner_out.at[0], gate_sent, cross_partner_out.at[0])
    up_outs = (keep_out.at[1], partner_out.at[1], up_sent, cross_partner_out.at[1])
    for j in range(4):
        part = rows[:, j * width : (j + 1) * width]
        gate_outs[j][...] = mm_rows(part, d_gate_out[...]).astype(jnp.bfloat16)
        up_outs[j][...] = mm_rows(part, d_up_out[...]).astype(jnp.bfloat16)
    ids = router.shape[0]
    logits = jnp.zeros((gate_pick.shape[0], ids), jnp.float32)
    for j in range(4):
        columns = pl.ds(pl.multiple_of((me ^ j) * width, width), width)
        logits += mm_last(
            rows[:, j * width : (j + 1) * width], router[:, columns].astype(jnp.bfloat16)
        )
    named = lax.broadcasted_iota(jnp.int32, (1, ids), 1) == expert
    share = jax.nn.sigmoid(jnp.sum(jnp.where(named, logits, 0.0), axis=1, keepdims=True))
    slope_grad = jnp.where(gate != 0.0, score * share * (1.0 - share), 0.0)
    logit_grad = jnp.broadcast_to(slope_grad, logit_out.shape).astype(jnp.bfloat16)
    logit_out[...] = logit_grad
    for j in range(4):
        columns = pl.ds(pl.multiple_of((me ^ j) * width, width), width)
        total = mm_rows(logit_grad, rows[:, j * width : (j + 1) * width])
        router_out[:, columns] = total[0 : router_out.shape[0]]


def back_kernel(place, *refs):
    (pick, d_gate, d_up, logit_grad, router, gate_weight, up_weight, partner,
     cross, cross_partner) = refs[0:10]
    own_out, other_out = refs[10:12]
    w_gate, w_up, sems = refs[12:15]
    me, expert = place[0], place[1]
    core = me & 1
    copies = bring(
        weight_pairs(core, (gate_weight, partner.at[0], cross.at[0], cross_partner.at[0]), w_gate)
        + weight_pairs(core, (up_weight, partner.at[1], cross.at[1], cross_partner.at[1]), w_up),
        sems,
    )
    for copy in copies:
        copy.wait()
    width = w_gate.shape[0] // 4
    slope_grad = logit_grad[:, 0:1].astype(jnp.float32)

    def column_block(j, columns):
        here = slice(j * width, (j + 1) * width)
        return (
            mm_last(d_gate[...], w_gate[here])
            + mm_last(d_up[...], w_up[here])
            + slope_grad * router[pl.ds(expert, 1), columns]
        )

    scatter(me, pick, own_out, other_out, column_block)


def dp_swap(value, step):
    return lax.ppermute(value, "dp", [(i, i ^ step) for i in range(4)])


def ring(value, step):
    size = lax.axis_size("expert")
    return lax.ppermute(value, "expert", [(i, (i + step) % size) for i in range(size)])


def after(value, *earlier):
    return lax.optimization_barrier((value, *earlier))[0]


def on_device_paired(
    tokens, routes, gate_weight, up_weight, down_weight, router, const_vec, const_gate, grad_out
):
    bf16, f32 = jnp.bfloat16, jnp.float32
    row_count, model_width = tokens.shape
    id_count = router.shape[1]
    const_count = const_vec.shape[0]
    expert_count = id_count - 2 - const_count
    stored_experts, stored_rows, hidden_width = gate_weight.shape
    me = lax.axis_index("dp")
    z = lax.axis_index("expert")
    core = me % 2
    expert = stored_experts * z + core
    place = jnp.stack([me, expert]).astype(jnp.int32)

    def of_expert(weight, which):
        return lax.dynamic_index_in_dim(weight, which, 0, keepdims=False)

    shape = jax.ShapeDtypeStruct
    vmem = pltpu.VMEM
    slot_count = 4 * row_count
    wide, narrow = (slot_count, model_width), (slot_count, hidden_width)
    table = (slot_count, row_count)
    weight_rows = (stored_rows, hidden_width)
    whole_weight = vmem((model_width, hidden_width), bf16)

    def together(*values):
        return lax.optimization_barrier(values)

    payload, step = pl.pallas_call(
        payload_kernel,
        out_shape=[shape((2 * row_count + 16, model_width), bf16), shape((8, 128), jnp.int32)],
        cost_estimate=pl.CostEstimate(flops=LONG, bytes_accessed=LONG, transcendentals=0),
    )(tokens, grad_out, routes.T, router.T)
    group = lax.axis_index("groups")
    near, payload_partner = ring(payload, 1), dp_swap(payload, 1)
    payload, payload_partner = together(payload, payload_partner)
    far_side = ring(payload, -1)
    in_sent = jnp.where(group == 0, gate_weight, up_weight)
    cut = stored_rows // 8 * 3
    in_came = [dp_swap(in_sent[:, :cut], 2), dp_swap(in_sent[:, cut:], 2)]
    down_cross = dp_swap(after(down_weight, payload_partner), 2)
    in_other = [lax.ppermute(in_came[0], "groups", [(0, 1), (1, 0)])]
    near, in_came[0], step = together(near, in_came[0], step)
    far = ring(near, 1)
    partner = dp_swap(
        jnp.stack([of_expert(w, 1 - core) for w in (gate_weight, up_weight, down_weight)]), 1
    )
    step = next_step(step)
    in_came[1], partner, step = together(in_came[1], partner, step)
    in_other.append(lax.ppermute(in_came[1], "groups", [(0, 1), (1, 0)]))
    step = next_step(step)
    in_other[0], in_other[1], step = together(*in_other, step)
    far_side, far, step = together(far_side, far, step)
    down_cross, step_down = together(down_cross, step)
    near_partner, far_side_partner, far_partner = dp_swap(near, 1), dp_swap(far_side, 1), dp_swap(far, 1)

    def of_core(first, second, which):
        came = jnp.concatenate([of_expert(part, which) for part in first])
        other = jnp.concatenate([of_expert(part, which) for part in second])
        return jnp.where(group == 0, jnp.stack([came, other]), jnp.stack([other, came]))

    in_cross = of_core(in_came, in_other, core)
    in_cross_partner = dp_swap(of_core(in_came, in_other, 1 - core), 1)
    down_cross_partner = dp_swap(of_expert(down_cross, 1 - core), 1)
    payloads = [payload, payload_partner, near, near_partner, far, far_partner, far_side,
                far_side_partner]
    in_weights = [gate_weight, up_weight, partner, in_cross, in_cross_partner]
    router_rows = jnp.pad(router.T.astype(f32), ((0, 16 - id_count), (0, 0)))
    pick, gate_pick, rows, cot, hidden, act, slope, upstream, down_cross_part = local_kernel(
        forward_kernel,
        place,
        [],
        [*payloads, *in_weights],
        [shape(table, bf16)] * 2 + [shape(wide, bf16)] * 2 + [shape(narrow, bf16)] * 3
        + [shape(wide, bf16), shape(weight_rows, bf16)],
        [vmem((8, *payload.shape), bf16), whole_weight, whole_weight,
         pltpu.SemaphoreType.DMA((16,))],
        LONG,
        step,
    )
    hidden, down_cross_partner = together(hidden, down_cross_partner)
    down_weights = [down_weight, partner, down_cross, down_cross_partner]
    def add(one, two):
        return one.astype(f32) + two.astype(f32)

    def sum_slots(own, came):
        return [
            add(mine, theirs).astype(bf16) for mine, theirs in zip(jnp.split(own, 2), came)
        ]

    def pair(mine, theirs):
        of = lax.broadcasted_iota(jnp.int32, (2, 1, 1), 0)
        return jnp.where(of == core, mine[None], theirs[None]).astype(bf16)

    id_range = lax.broadcasted_iota(jnp.int32, (1, 1, id_count), 2)
    named = jnp.any(routes[:, :, None] == id_range, axis=1)[:, expert_count:]
    share = jax.nn.sigmoid(mm(tokens, router[:, expert_count:]))
    gates = jnp.where(named, share, 0.0).astype(bf16).astype(f32)
    tokens_float = tokens.astype(f32)
    grad_float = grad_out.astype(f32)
    copy_weight = gates[:, 1]
    const_weight = gates[:, 2:]
    const_share = jax.nn.sigmoid(mm(tokens, const_gate))
    const_rest = (const_weight * (1.0 - const_share)).astype(bf16)
    coefficient = copy_weight + jnp.sum(const_weight * const_share, axis=1)
    along_token = jnp.sum(grad_float * tokens_float, axis=1, keepdims=True)
    along_const = mm_last(grad_out, const_vec)
    const_value = const_share * along_token + (1.0 - const_share) * along_const
    pick_grad = jnp.concatenate(
        [jnp.zeros_like(along_token), along_token, const_value], axis=1
    )
    null_grad = jnp.where(named, pick_grad * share * (1.0 - share), 0.0).astype(bf16)
    share_grad = (
        const_weight * (along_token - along_const) * const_share * (1.0 - const_share)
    ).astype(bf16)
    mixed_own, mixed_other, *down_parts = local_kernel(
        output_kernel,
        place,
        [gate_pick, hidden, upstream],
        down_weights,
        [shape(wide, bf16)] * 2 + [shape(weight_rows, bf16)] * 3,
        [whole_weight, pltpu.SemaphoreType.DMA((4,))],
        LONG,
        step_down,
    )
    down_came, down_came_partner = dp_swap(down_cross_part, 2), dp_swap(down_parts[2], 3)
    parts = [mixed_other[k * row_count : (k + 1) * row_count] for k in range(4)]
    mixed_came = [dp_swap(parts[2], 1), dp_swap(parts[3], 1)]
    mixed_own, mixed_came[0], mixed_came[1], down_came, cot = together(
        mixed_own, *mixed_came, down_came, cot
    )
    mixed_first = sum_slots(mixed_own[2 * row_count :], mixed_came)
    mixed_near = ring(mixed_first[0], -1)
    mixed_late = dp_swap(mixed_other[: 2 * row_count], 1)
    down_from = dp_swap(down_parts[1], 1)
    d_gate, d_up, logit_grad, router_row, *in_parts, gate_sent, up_sent = local_kernel(
        backward_kernel,
        place,
        [gate_pick, rows, hidden, cot, act, slope, router_rows],
        down_weights,
        [shape(narrow, bf16)] * 2 + [shape(table, bf16), shape((8, model_width), f32)]
        + [shape((2, *weight_rows), bf16)] * 3 + [shape(weight_rows, bf16)] * 2,
        [whole_weight, pltpu.SemaphoreType.DMA((4,))],
        LONG,
    )
    (d_gate, router_row, in_parts[1], in_parts[2], gate_sent, up_sent, down_came_partner,
     mixed_near, mixed_late, down_from) = together(
        d_gate, router_row, in_parts[1], in_parts[2], gate_sent, up_sent, down_came_partner,
        mixed_near, mixed_late, down_from
    )
    mixed_late = sum_slots(mixed_own[: 2 * row_count], jnp.split(mixed_late, 2))
    small = jnp.concatenate(
        [
            mm_rows(jnp.concatenate([null_grad, share_grad], axis=1), tokens),
            mm_rows(const_rest, grad_out),
        ],
        axis=0,
    )
    experts = lax.broadcasted_iota(jnp.int32, (expert_count, 1), 0)
    routed = jnp.where(experts == expert, router_row[0:1], 0.0)
    small = jnp.concatenate([routed, small], axis=0)
    gate_came, in_from, small_came = dp_swap(gate_sent, 2), dp_swap(in_parts[1], 1), dp_swap(small, 2)
    mixed_side = ring(mixed_first[1].astype(bf16), 1)
    mixed_near = ring(add(mixed_near, mixed_late[1]).astype(bf16), -1)
    back_own, back_other = local_kernel(
        back_kernel,
        place,
        [pick, d_gate, d_up, logit_grad, router_rows],
        in_weights,
        [shape(wide, bf16)] * 2,
        [whole_weight, whole_weight, pltpu.SemaphoreType.DMA((8,))],
        LONG,
    )
    (back_own, back_other, gate_came, in_from, small_came, mixed_side, mixed_near, up_sent,
     in_parts[2]) = together(
        back_own, back_other, gate_came, in_from, small_came, mixed_side, mixed_near, up_sent,
        in_parts[2]
    )
    up_came, in_came_partner = dp_swap(up_sent, 2), dp_swap(in_parts[2], 3)
    small = small + small_came
    back_came, small_came = together(dp_swap(back_other, 1), dp_swap(small, 1))
    back_late = sum_slots(back_own[: 2 * row_count], jnp.split(back_came[: 2 * row_count], 2))
    back_first = sum_slots(back_own[2 * row_count :], jnp.split(back_came[2 * row_count :], 2))
    back_first[0], back_first[1], step = together(*back_first, step_down)
    back_near, back_side = ring(back_first[0], -1), ring(back_first[1], 1)
    step = next_step(step)
    small = small + small_came
    small, step = together(small, step)
    small_came = lax.ppermute(small, "expert", [(i, i ^ 1) for i in range(4)])
    back_near, up_came, mixed_near, small_came = together(back_near, up_came, mixed_near, small_came)
    back_near = ring(add(back_near, back_late[1]).astype(bf16), -1)
    small = small + small_came
    small = small + lax.ppermute(small, "expert", [(i, i ^ 2) for i in range(4)])
    small = small + step[0:1, 0:1].astype(f32)
    mixed_sum = add(mixed_side, mixed_near) + mixed_late[0].astype(f32)
    grad_router = small[:id_count].T
    grad_const_gate = small[id_count : id_count + const_count].T
    grad_const_vec = small[id_count + const_count :]
    back_sum = add(back_side, back_near) + back_late[0].astype(f32)
    grad_down = pair(add(down_parts[0], down_came), add(down_from, down_came_partner))
    mixed = (
        mixed_sum + coefficient[:, None] * tokens_float + mm(const_rest, const_vec)
    ).astype(bf16)
    back_local = (
        coefficient[:, None] * grad_float
        + mm_last(null_grad, router[:, expert_count:])
        + mm_last(share_grad, const_gate)
    )
    grad_tokens = (back_sum + back_local).astype(bf16)

    mine = [add(in_parts[0][i], came).astype(bf16) for i, came in enumerate((gate_came, up_came))]
    (mine[0], mine[1], in_came_partner, mixed, grad_down, grad_tokens, grad_router,
     grad_const_gate, grad_const_vec) = together(
        *mine, in_came_partner, mixed, grad_down, grad_tokens, grad_router, grad_const_gate,
        grad_const_vec
    )
    grad_gate, grad_up = (
        pair(mine[i], add(in_from[i], in_came_partner[i])) for i in range(2)
    )
    return (
        mixed,
        grad_tokens,
        grad_gate,
        grad_up,
        grad_down,
        grad_router,
        grad_const_vec,
        grad_const_gate,
    )


def solution(mesh):
    paired = mesh.shape["rep"] == 1 and mesh.shape["dp"] == 4

    def on_device(tokens, routes, gate_weight, *others):
        id_count = others[2].shape[1]
        stored_experts, stored_rows, hidden_width = gate_weight.shape
        row_count, top_count = routes.shape
        halved = row_count * top_count == (row_count // 2) * id_count
        if paired and stored_experts == 2 and halved and row_count == 128:
            return on_device_paired(tokens, routes, gate_weight, *others)
        return on_device_general(tokens, routes, gate_weight, *others)

    placed = (
        P(("groups", "expert", "dp"), None),
        P(("groups", "expert", "dp"), None),
        P("expert", ("dp", "rep"), None),
        P("expert", ("dp", "rep"), None),
        P("expert", ("dp", "rep"), None),
        P(),
        P(),
        P(),
        P(("groups", "expert", "dp"), None),
    )
    return jax.shard_map(
        on_device,
        mesh=mesh,
        in_specs=placed,
        out_specs=(
            P(("groups", "expert", "dp"), None),
            P(("groups", "expert", "dp"), None),
            P(("groups", "expert"), ("dp", "rep"), None),
            P(("groups", "expert"), ("dp", "rep"), None),
            P(("groups", "expert"), ("dp", "rep"), None),
            P("groups", None),
            P("groups", None),
            P("groups", None),
        ),
        check_vma=False,
    )
```
